32 devices in a mesh: dp: 8 (over z, x), tensor: 4 (over y, core).
Axes of the slice: x: 2, y: 2, z: 4, core: 2. Of those that a mesh axis runs over, the one named last changes fastest.
Arguments:
- codes_in: int32 [16, 1024, 4], P('dp', 'tensor'), may hold values from 0 to 2047, as said below
- codes_out: int32 [16, 1024, 4], P('dp', 'tensor'), may hold values from 0 to 2047, as said below
- pad_mask: int32 [16, 1024, 4], P('dp', 'tensor'), may hold values from 0 to 1, as said below
- text_table: bfloat16 [256, 1024], replicated, may hold values from -6 to 6
- text_index: int32 [16, 64], P('dp'), may hold values from 0 to 255
- attend_in: float32 [1024, 6, 1024], P('dp', None, 'tensor'), may hold values from -0.1875 to 0.1875
- attend_out: float32 [2, 1024, 1024], P(None, 'tensor', 'dp'), may hold values from -0.75 to 0.75
- expand_weights: float32 [1024, 4096], P('dp', 'tensor'), may hold values from -0.1875 to 0.1875
- shrink_weights: float32 [4096, 1024], P('tensor', 'dp'), may hold values from -0.09375 to 0.09375
- attend_in_momentum: float32 [1024, 6, 1024], P('dp', None, 'tensor'), may hold values from -0.0024414062 to 0.0024414062
- attend_out_momentum: float32 [2, 1024, 1024], P(None, 'tensor', 'dp'), may hold values from -0.0024414062 to 0.0024414062
- expand_momentum: float32 [1024, 4096], P('dp', 'tensor'), may hold values from -0.0024414062 to 0.0024414062
- shrink_momentum: float32 [4096, 1024], P('tensor', 'dp'), may hold values from -0.0024414062 to 0.0024414062
- embed_table: float32 [4, 2048, 1024], P(None, ('dp', 'tensor')), may hold values from -4 to 4
- head_table: float32 [4, 2048, 1024], P(None, ('dp', 'tensor')), may hold values from -0.1875 to 0.1875
- norm_params: float32 [8, 1024], replicated, may hold values from -2 to 1.4, as said below
- embed_first: float32 [4, 2048, 1024], P(None, ('dp', 'tensor')), may hold values from -4.7683716e-06 to 4.7683716e-06
- embed_second: float32 [4, 2048, 1024], P(None, ('dp', 'tensor')), may hold values from 6.3329935e-13 to 2.0489097e-12
- head_first: float32 [4, 2048, 1024], P(None, ('dp', 'tensor')), may hold values from -9.1552734e-05 to 9.1552734e-05
- head_second: float32 [4, 2048, 1024], P(None, ('dp', 'tensor')), may hold values from 1.7508864e-10 to 5.7742e-10
- norm_first: float32 [8, 1024], replicated, may hold values from -0.0029296875 to 0.0029296875
- norm_second: float32 [8, 1024], replicated, may hold values from 6.103516e-08 to 2.4414064e-07
Outputs:
- loss_sum: float32 [], replicated
- token_count: float32 [], replicated
- attend_in_new: float32 [1024, 6, 1024], P('dp', None, 'tensor')
- attend_out_new: float32 [2, 1024, 1024], P(None, 'tensor', 'dp')
- expand_new: float32 [1024, 4096], P('dp', 'tensor')
- shrink_new: float32 [4096, 1024], P('tensor', 'dp')
- attend_in_next: float32 [1024, 6, 1024], P('dp', None, 'tensor')
- attend_out_next: float32 [2, 1024, 1024], P(None, 'tensor', 'dp')
- expand_next: float32 [1024, 4096], P('dp', 'tensor')
- shrink_next: float32 [4096, 1024], P('tensor', 'dp')
- embed_new: float32 [4, 2048, 1024], P(None, ('dp', 'tensor'))
- head_new: float32 [4, 2048, 1024], P(None, ('dp', 'tensor'))
- norm_new: float32 [8, 1024], replicated
- embed_first_new: float32 [4, 2048, 1024], P(None, ('dp', 'tensor'))
- embed_second_new: float32 [4, 2048, 1024], P(None, ('dp', 'tensor'))
- head_first_new: float32 [4, 2048, 1024], P(None, ('dp', 'tensor'))
- head_second_new: float32 [4, 2048, 1024], P(None, ('dp', 'tensor'))
- norm_first_new: float32 [8, 1024], replicated
- norm_second_new: float32 [8, 1024], replicated
The draws below stay inside these ranges and needn't reach their ends.
Inputs may be any that keep to these rules, and one draw needn't show every extreme that they name: `codes_in`: each clip has a length from 128 to 1024, longer on average in later groups of 2 clips; one clip of each group, drawn, has length 1024. In codebook k, frame s holds a code where k <= s < length + k, else 2048 - 1. codes_out[c, t] is the code of frame t + 1 by the same rule, so codes_out[c, t] = codes_in[c, t + 1] below the last frame. `pad_mask`: 1 exactly where codebook k of frame t + 1 holds a live code by that rule. `norm_params`: rows 0, 2, 4, 6 are gains, rows 1, 3, 5, 7 shifts.
All inputs are finite; a program needn't handle non-finite values.
Results may differ from the reference program's by a relative error of at most 0.025.
Values may be sent and summed in bfloat16 or wider, within the bound.
No kernel may reach another device: no remote copies, remote signals or barrier semaphores. Data moves between devices by JAX's collectives and lax.ppermute only.
A program may use at most 256 MiB of HBM per device.

```python
import math
import jax
import jax.numpy as jnp
from jax import lax

D = 1024
HEADS = 16
HEAD_DIM = 64
FF = 4096
VOCAB = 2048
BOOKS = 4
FRAMES = 1024
CLIP_GRP = 2
TEXT_LEN = 64
TEXT_ROWS = 256
MUON_ROWS = 32
STEP = 10
CLIPS = 16
N_DP = 8


def clip_codes(key):
    length_key = jax.random.fold_in(key, 101)
    full_key = jax.random.fold_in(key, 102)
    code_key = jax.random.fold_in(key, 103)
    group_index = jnp.arange(CLIPS) // CLIP_GRP
    shortest = FRAMES // 8 + group_index * (3 * FRAMES // 4) // max(N_DP - 1, 1)
    spread = jax.random.randint(length_key, (CLIPS,), 0, 1 << 20)
    lengths = shortest + spread % (FRAMES + 1 - shortest)
    chosen = jax.random.randint(full_key, (N_DP,), 0, CLIP_GRP)
    is_full = jnp.arange(CLIPS) % CLIP_GRP == chosen[group_index]
    lengths = jnp.where(is_full, FRAMES, lengths)
    raw_codes = jax.random.randint(code_key, (CLIPS, FRAMES + 1, BOOKS), 0, VOCAB - 1)
    frame_index = jnp.arange(FRAMES + 1)[None, :, None]
    codebook = jnp.arange(BOOKS)[None, None, :]
    alive = (frame_index >= codebook) & (frame_index < lengths[:, None, None] + codebook)
    return (jnp.where(alive, raw_codes, VOCAB - 1).astype(jnp.int32), alive.astype(jnp.int32))


def draw_codes_in(key, part):
    codes, alive = clip_codes(key)
    return codes[:, :FRAMES]


def draw_codes_out(key, part):
    codes, alive = clip_codes(key)
    return codes[:, 1:]


def draw_pad_mask(key, part):
    codes, alive = clip_codes(key)
    return alive[:, 1:]


def draw_norm_params(key, part):
    key = jax.random.fold_in(key, 7)
    gain_key = jax.random.fold_in(key, 1)
    shift_key = jax.random.fold_in(key, 2)
    gains = jax.random.uniform(gain_key, (4, D), jnp.float32, 0.6, 1.4)
    shifts = jnp.clip(0.3 * jax.random.normal(shift_key, (4, D), jnp.float32), -2.0, 1.4)
    return jnp.stack([gains, shifts], 1).reshape(8, D)


def plant(result, rng, smallest, largest):
    longest = result.shape.index(max(result.shape))
    spots = []
    for shift in (0, 1):
        where = [jax.random.randint(jax.random.fold_in(rng, axis), (), 0, length) for axis, length in enumerate(result.shape)]
        where[longest] = (where[longest] + shift) % result.shape[longest]
        spots.append(tuple(where))
    return result.at[spots[0]].set(smallest).at[spots[1]].set(largest)


def levels(own_key, dims, pieces, low, high):
    def one(dim, shards_of):
        draws = jax.random.uniform(jax.random.fold_in(jax.random.fold_in(own_key, 6), dim), (shards_of,), jnp.float32, low / len(pieces), high / len(pieces))
        return jnp.repeat(jnp.exp(draws), dims[dim] // shards_of).reshape((-1,) + (1,) * (len(dims) - dim - 1))

    level = one(*pieces[0])
    for cut in pieces[1:]:
        level = level * one(*cut)
    return level


def scatter_about(key, extent, scale, bound, split=(), kind=jnp.bfloat16):
    level = levels(key, extent, split, -0.22, 0.18) if split else 1.0
    array = jax.random.normal(key, extent, jnp.float32) * scale * level
    return jnp.minimum(jnp.maximum(array, -bound), bound).astype(kind)


def setup_inputs(seed: int = 0) -> dict:
    keys = jax.random.split(jax.random.key(seed), 23)
    codes_in = draw_codes_in(jax.random.fold_in(keys[22], 71), 0)
    codes_out = draw_codes_out(jax.random.fold_in(keys[22], 71), 0)
    pad_mask = draw_pad_mask(jax.random.fold_in(keys[22], 71), 0)
    text_table = scatter_about(keys[3], (TEXT_ROWS, D), 1.0, 6.0)
    text_index = plant(jax.random.randint(keys[4], (CLIPS, TEXT_LEN), 0, TEXT_ROWS), jax.random.fold_in(keys[4], 1), 0, TEXT_ROWS - 1).astype(jnp.int32)
    attend_in = scatter_about(keys[5], (D, 6, D), D ** -0.5, 0.1875, ((0, 8), (2, 4)), jnp.float32)
    attend_out = scatter_about(keys[6], (2, D, D), (D // 16) ** -0.5, 0.75, ((1, 4), (2, 8)), jnp.float32)
    expand_weights = scatter_about(keys[7], (D, FF), D ** -0.5, 0.1875, ((0, 8), (1, 4)), jnp.float32)
    shrink_weights = scatter_about(keys[8], (FF, D), FF ** -0.5, 0.09375, ((0, 4), (1, 8)), jnp.float32)
    attend_in_momentum = scatter_about(keys[9], (D, 6, D), (0.02 * (CLIPS * FRAMES) ** -0.5), 0.0024414062, ((0, 8), (2, 4)), jnp.float32)
    attend_out_momentum = scatter_about(keys[10], (2, D, D), (0.02 * (CLIPS * FRAMES) ** -0.5), 0.0024414062, ((1, 4), (2, 8)), jnp.float32)
    expand_momentum = scatter_about(keys[11], (D, FF), (0.02 * (CLIPS * FRAMES) ** -0.5), 0.0024414062, ((0, 8), (1, 4)), jnp.float32)
    shrink_momentum = scatter_about(keys[12], (FF, D), (0.02 * (CLIPS * FRAMES) ** -0.5), 0.0024414062, ((0, 4), (1, 8)), jnp.float32)
    embed_table = scatter_about(keys[13], (BOOKS, VOCAB, D), 0.25, 4.0, ((1, 32),), jnp.float32)
    head_table = scatter_about(keys[14], (BOOKS, VOCAB, D), D ** -0.5, 0.1875, ((1, 32),), jnp.float32)
    norm_params = draw_norm_params(jax.random.fold_in(keys[22], 71), 0)
    embed_first = scatter_about(keys[16], (BOOKS, VOCAB, D), (0.008 * (CLIPS * FRAMES * VOCAB) ** -0.5 * BOOKS ** -1), 4.76837158203125e-06, ((1, 32),), jnp.float32)
    embed_second = jnp.clip(jnp.exp(math.log(2.0489096530518225e-12) - 1.1741198 * jax.random.uniform(keys[17], (BOOKS, VOCAB, D), jnp.float32) ** levels(keys[17], (BOOKS, VOCAB, D), ((1, 32),), -0.2, 0.2)), 6.332993482925653e-13, 2.0489096530518225e-12)
    head_first = scatter_about(keys[18], (BOOKS, VOCAB, D), (0.14 * (CLIPS * FRAMES * VOCAB) ** -0.5 * BOOKS ** -1), 9.1552734375e-05, ((1, 32),), jnp.float32)
    head_second = jnp.clip(jnp.exp(math.log(5.774200007024888e-10) - 1.1932776 * jax.random.uniform(keys[19], (BOOKS, VOCAB, D), jnp.float32) ** levels(keys[19], (BOOKS, VOCAB, D), ((1, 32),), -0.2, 0.2)), 1.7508863803250563e-10, 5.774200007024888e-10)
    norm_first = scatter_about(keys[20], (8, D), (0.025 * (CLIPS * FRAMES) ** -0.5), 0.0029296875, (), jnp.float32)
    norm_second = jnp.clip(jnp.exp(jax.random.uniform(keys[21], (8, D), jnp.float32, math.log(6.103515914901436e-08), math.log(2.4414063659605745e-07))), 6.103515914901436e-08, 2.4414063659605745e-07)
    return {"codes_in": codes_in, "codes_out": codes_out, "pad_mask": pad_mask, "text_table": text_table, "text_index": text_index, "attend_in": attend_in, "attend_out": attend_out, "expand_weights": expand_weights, "shrink_weights": shrink_weights, "attend_in_momentum": attend_in_momentum, "attend_out_momentum": attend_out_momentum, "expand_momentum": expand_momentum, "shrink_momentum": shrink_momentum, "embed_table": embed_table, "head_table": head_table, "norm_params": norm_params, "embed_first": embed_first, "embed_second": embed_second, "head_first": head_first, "head_second": head_second, "norm_first": norm_first, "norm_second": norm_second}


@jax.custom_vjp
def low(v):
    return lax.optimization_barrier(v.astype(jnp.bfloat16)).astype(jnp.float32)

@jax.custom_vjp
def low_back(v):
    return v

def low_keep(v):
    return (low(v), None)

def low_pass(kept, grad):
    return (grad,)

def back_keep(v):
    return (v, None)

def back_low(kept, grad):
    return (low(grad),)
low.defvjp(low_keep, low_pass)
low_back.defvjp(back_keep, back_low)
HIGHEST = lax.Precision.HIGHEST
NEWTON = (3.4445, -4.775, 2.0315)
BETA_ONE = 0.9
BETA_TWO = 0.95
ADAM_EPS = 1e-08
DECAY = 0.01
MOMENTUM = 0.95

def product(left, right):
    return jnp.matmul(left, right, precision=HIGHEST)

def layer_norm(values, gain, shift):
    centred = values - lax.optimization_barrier(jnp.mean(values, -1, keepdims=True))
    variance = lax.optimization_barrier(jnp.mean(centred * centred, -1, keepdims=True))
    return centred * lax.rsqrt(variance + 1e-05) * gain + shift

def sinusoid(first, length, width):
    half = width // 2
    rates = jnp.exp(jnp.arange(half, dtype=jnp.float32) * (-math.log(10000.0) / half))
    places = (first + jnp.arange(length, dtype=jnp.int32)).astype(jnp.float32)
    angles = places[:, None] * rates[None, :]
    return jnp.concatenate([jnp.sin(angles), jnp.cos(angles)], -1)

def attention(queries, key_rows, value_rows, causal):
    query_len = queries.shape[0]
    key_len = key_rows.shape[0]
    split_q = queries.reshape(query_len, HEADS, HEAD_DIM)
    split_k = key_rows.reshape(key_len, HEADS, HEAD_DIM)
    split_v = value_rows.reshape(key_len, HEADS, HEAD_DIM)
    scores = low_back(jnp.einsum('qhd,khd->hqk', split_q, split_k, precision=HIGHEST) * 0.125)
    if causal:
        allowed = jnp.arange(query_len)[:, None] >= jnp.arange(key_len)[None, :]
        scores = jnp.where(allowed[None], scores, -jnp.inf)
    probs = low(jax.nn.softmax(scores, -1))
    mixed = jnp.einsum('hqk,khd->qhd', probs, split_v, precision=HIGHEST)
    return low_back(low(mixed.reshape(query_len, D)))

def clip_loss(weights, codes_now, codes_next, counted, memory):
    table, head, attend_in, attend_out, expand, shrink, gains = weights
    embedded = table[0][codes_now[:, 0]]
    for codebook in range(1, BOOKS):
        embedded = embedded + table[codebook][codes_now[:, codebook]]
    residual = low_back(embedded) + sinusoid(0, FRAMES, D)
    normed = low(layer_norm(residual, gains[0], gains[1]))
    triple = [low_back(low(product(normed, attend_in[:, member]))) for member in range(3)]
    residual = residual + low_back(product(attention(triple[0], triple[1], triple[2], True), attend_out[0]))
    normed = low(layer_norm(residual, gains[2], gains[3]))
    cross_q = low_back(low(product(normed, attend_in[:, 3])))
    cross_k = low_back(low(product(memory, attend_in[:, 4])))
    cross_v = low_back(low(product(memory, attend_in[:, 5])))
    residual = residual + low_back(product(attention(cross_q, cross_k, cross_v, False), attend_out[1]))
    normed = low(layer_norm(residual, gains[4], gains[5]))
    upper = low_back(product(normed, expand))
    residual = residual + low_back(product(low(jax.nn.gelu(upper, approximate=False)), shrink))
    final = low(layer_norm(residual, gains[6], gains[7]))
    logits = low_back(jnp.einsum('td,kvd->tkv', final, head, precision=HIGHEST))
    log_probs = jax.nn.log_softmax(logits, -1)
    picked = jnp.take_along_axis(log_probs, codes_next[:, :, None], -1)[:, :, 0]
    return -jnp.sum(picked * counted)

def orthogonal(moment):
    rows, cols = moment.shape[-2:]
    blocks = moment.reshape(moment.shape[:-2] + (rows // MUON_ROWS, MUON_ROWS, cols))
    size = jnp.sqrt(lax.optimization_barrier(jnp.sum(blocks * blocks, (-2, -1), keepdims=True))) + 1e-07
    current = blocks / size
    for repeat in range(5):
        gram = jnp.matmul(current, jnp.swapaxes(current, -1, -2), precision=HIGHEST)
        mixing = NEWTON[1] * gram + NEWTON[2] * jnp.matmul(gram, gram, precision=HIGHEST)
        current = NEWTON[0] * current + jnp.matmul(mixing, current, precision=HIGHEST)
    return current.reshape(moment.shape)

def adam(weight, first, second, gradient, rate, decay):
    first = BETA_ONE * first + (1.0 - BETA_ONE) * gradient
    second = BETA_TWO * second + (1.0 - BETA_TWO) * gradient * gradient
    direction = first / (1.0 - BETA_ONE ** STEP) / (jnp.sqrt(second / (1.0 - BETA_TWO ** STEP)) + ADAM_EPS)
    return (weight - rate * (direction + decay * weight), first, second)

def reference(codes_in, codes_out, pad_mask, text_table, text_index, attend_in, attend_out, expand_weights, shrink_weights, attend_in_momentum, attend_out_momentum, expand_momentum, shrink_momentum, embed_table, head_table, norm_params, embed_first, embed_second, head_first, head_second, norm_first, norm_second):
    counted = pad_mask.astype(jnp.float32)
    token_count = jnp.sum(counted)
    memory = jnp.take(text_table.astype(jnp.float32), text_index, axis=0)

    def total_loss(params):
        rounded = tuple((low(item) for item in params[:6])) + (params[6],)

        def one_clip(carry, clip_index):
            term = jax.checkpoint(clip_loss)(rounded, codes_in[clip_index], codes_out[clip_index], counted[clip_index], memory[clip_index])
            return (carry + term, None)
        summed, ignored = lax.scan(one_clip, jnp.zeros((), jnp.float32), jnp.arange(CLIPS))
        return (summed / token_count, summed)
    params = (embed_table, head_table, attend_in, attend_out, expand_weights, shrink_weights, norm_params)
    loss_value, backward, loss_sum = jax.vjp(total_loss, params, has_aux=True)
    grads = backward(jnp.ones_like(loss_value))[0]
    grad_embed, grad_head, grad_in, grad_out, grad_expand, grad_shrink, grad_norm = grads
    next_in = MOMENTUM * attend_in_momentum + grad_in
    next_out = MOMENTUM * attend_out_momentum + grad_out
    next_expand = MOMENTUM * expand_momentum + grad_expand
    next_shrink = MOMENTUM * shrink_momentum + grad_shrink
    ortho_in = jnp.moveaxis(orthogonal(jnp.moveaxis(next_in, 1, 0)), 0, 1)
    attend_in_new = attend_in * (1.0 - 0.5 * DECAY) - 0.5 * ortho_in
    attend_out_new = attend_out * (1.0 - 1.0 * DECAY) - 1.0 * orthogonal(next_out)
    expand_new = expand_weights * (1.0 - 0.5 * DECAY) - 0.5 * orthogonal(next_expand)
    shrink_new = shrink_weights * (1.0 - 0.5 * DECAY) - 0.5 * orthogonal(next_shrink)
    embed_new, embed_first_new, embed_second_new = adam(embed_table, embed_first, embed_second, grad_embed, 0.1, DECAY)
    head_new, head_first_new, head_second_new = adam(head_table, head_first, head_second, grad_head, 0.03, DECAY)
    norm_new, norm_first_new, norm_second_new = adam(norm_params, norm_first, norm_second, grad_norm, 0.5, 0.0)
    return (loss_sum, token_count, attend_in_new, attend_out_new, expand_new, shrink_new, next_in, next_out, next_expand, next_shrink, embed_new, head_new, norm_new, embed_first_new, embed_second_new, head_first_new, head_second_new, norm_first_new, norm_second_new)
```

```python
import functools
import math

import jax
import jax.numpy as jnp
from jax import lax
from jax.sharding import Mesh
from jax.sharding import PartitionSpec as P

HEAD_DIM = 64
MUON_ROWS = 32
STEP = 10

HIGHEST = lax.Precision.HIGHEST
NEWTON = (3.4445, -4.775, 2.0315)
BETA_ONE = 0.9
BETA_TWO = 0.95
ADAM_EPS = 1e-08
DECAY = 0.01
MOMENTUM = 0.95
BF16 = jnp.bfloat16
F32 = jnp.float32


def layer_norm(values, gain, shift):
    centred = values - jnp.mean(values, -1, keepdims=True)
    variance = jnp.mean(centred * centred, -1, keepdims=True)
    return centred * lax.rsqrt(variance + 1e-05) * gain + shift


def norm_back(values, gain, shift, grad):
    result, backward = jax.vjp(layer_norm, values, gain, shift)
    return backward(grad)


def exact_gelu(values):
    return jax.nn.gelu(values, approximate=False)


def sinusoid(first, length, width):
    half = width // 2
    rates = jnp.exp(jnp.arange(half, dtype=jnp.float32) * (-math.log(10000.0) / half))
    places = (first + jnp.arange(length, dtype=jnp.int32)).astype(jnp.float32)
    angles = places[:, None] * rates[None, :]
    return jnp.concatenate([jnp.sin(angles), jnp.cos(angles)], -1)


def scores_of(part, key_rows, first, causal):
    scores = (
        jnp.einsum("qchd,kchd->chqk", part, key_rows, preferred_element_type=jnp.float32) * 0.125
    )
    if causal:
        allowed = (first + jnp.arange(part.shape[0]))[:, None] >= jnp.arange(key_rows.shape[0])[
            None, :
        ]
        scores = jnp.where(allowed[None, None], scores, -jnp.inf)
    return scores


def attend(queries, key_rows, value_rows, causal):
    frames, clips, heads_local, depth = queries.shape
    span = min(512, frames)
    grouped = queries.reshape(frames // span, span, clips, heads_local, depth)
    firsts = jnp.arange(frames // span) * span

    def one_block(inputs):
        part, first = inputs
        scores = scores_of(part, key_rows, first, causal)
        row_max = jnp.max(scores, -1, keepdims=True)
        expo = jnp.exp(scores - row_max)
        total = jnp.sum(expo, -1, keepdims=True)
        probs = (expo / total).astype(jnp.bfloat16)
        mixed = jnp.einsum("chqk,kchd->qchd", probs, value_rows, preferred_element_type=jnp.float32)
        return (mixed.astype(jnp.bfloat16), (row_max + jnp.log(total))[..., 0])

    mixed, log_total = lax.map(one_block, (grouped, firsts))
    return (mixed.reshape(frames, clips, heads_local * depth), log_total)


def attend_back(queries, key_rows, value_rows, log_total, grad_mixed, causal):
    frames, clips, heads_local, depth = queries.shape
    span = min(512, frames)
    grouped = queries.reshape(frames // span, span, clips, heads_local, depth)
    grad_grouped = grad_mixed.reshape(grouped.shape)
    firsts = jnp.arange(frames // span) * span

    def one_block(carry, inputs):
        grad_keys, grad_values = carry
        part, grad_part, log_part, first = inputs
        scores = scores_of(part, key_rows, first, causal)
        probs = jnp.exp(scores - log_part[..., None])
        grad_probs = jnp.einsum(
            "qchd,kchd->chqk", grad_part, value_rows, preferred_element_type=jnp.float32
        )
        grad_scores = (
            probs * (grad_probs - jnp.sum(probs * grad_probs, -1, keepdims=True))
        ).astype(jnp.bfloat16)
        grad_query = (
            jnp.einsum("chqk,kchd->qchd", grad_scores, key_rows, preferred_element_type=jnp.float32)
            * 0.125
        )
        grad_keys = (
            grad_keys
            + jnp.einsum("chqk,qchd->kchd", grad_scores, part, preferred_element_type=jnp.float32)
            * 0.125
        )
        grad_values = grad_values + jnp.einsum(
            "chqk,qchd->kchd",
            probs.astype(jnp.bfloat16),
            grad_part,
            preferred_element_type=jnp.float32,
        )
        return ((grad_keys, grad_values), grad_query)

    empty = jnp.zeros(key_rows.shape, jnp.float32)
    (grad_keys, grad_values), grad_query = lax.scan(
        one_block, (empty, empty), (grouped, grad_grouped, log_total, firsts)
    )
    return (grad_query.reshape(queries.shape), grad_keys, grad_values)


def adam(weight, first, second, gradient, rate, decay):
    first = BETA_ONE * first + (1.0 - BETA_ONE) * gradient
    second = BETA_TWO * second + (1.0 - BETA_TWO) * gradient * gradient
    direction = (
        first / (1.0 - BETA_ONE**STEP) / (jnp.sqrt(second / (1.0 - BETA_TWO**STEP)) + ADAM_EPS)
    )
    return (weight - rate * (direction + decay * weight), first, second)


class Grid:
    def __init__(self, sizes):
        self.sizes = sizes

    def index(self, axis):
        return lax.axis_index(axis)

    def rotate(self, value, axis):
        size = self.sizes[axis]
        return lax.ppermute(value, axis, [(i, (i + 1) % size) for i in range(size)])

    def swap(self, value, axis, step):
        return lax.ppermute(value, axis, [(i, i ^ step) for i in range(self.sizes[axis])])

    def total(self, value, axes):
        for axis in axes:
            step = 1
            while step < self.sizes[axis]:
                value = value + self.swap(value, axis, step)
                step *= 2
        return value

    def gather(self, shard, axes):
        held = [(shard, {})]
        for axis in axes:
            wave, found = held, list(held)
            for step in range(1, self.sizes[axis]):
                wave = [
                    (self.rotate(value, axis), {**moved, axis: step}) for value, moved in wave
                ]
                found += wave
            held = found
        return held

    def source(self, moved, axis):
        return lax.rem(lax.axis_index(axis) + self.sizes[axis] - moved.get(axis, 0), self.sizes[axis])

    def scatter(self, axis, pick):
        size = self.sizes[axis]
        place = lax.axis_index(axis)
        running = pick(lax.rem(place + size - 1, size))
        for step in range(1, size):
            arrived = self.rotate(running.astype(BF16), axis)
            running = arrived.astype(F32) + pick(lax.rem(place + 2 * size - step - 1, size)).astype(F32)
        return running


def chosen(array, index, axis):
    return lax.dynamic_index_in_dim(array, index, axis, keepdims=False)


def newton(grams):
    count, _, rows = grams.shape
    repeats = rows // MUON_ROWS
    band = jnp.arange(rows) // MUON_ROWS
    mask = band[:, None] == band[None, :]
    eye = jnp.eye(rows, dtype=F32)
    gram = jnp.where(mask, jnp.tile(grams, (1, repeats, 1)), 0.0)
    diagonal = jnp.sum(gram * eye, -1).reshape(count, repeats, MUON_ROWS)
    size = jnp.sqrt(jnp.sum(diagonal, -1, keepdims=True)) + 1e-07
    size = jnp.broadcast_to(size, diagonal.shape).reshape(count, rows, 1)
    gram = gram / (size * size)

    def times(left, right):
        return jnp.einsum("brs,bst->brt", left, right, precision=HIGHEST)

    factor = None
    for repeat in range(5):
        mixing = NEWTON[0] * eye + NEWTON[1] * gram + NEWTON[2] * times(gram, gram)
        factor = mixing if factor is None else times(mixing, factor)
        if repeat < 4:
            gram = times(mixing, times(gram, mixing))
    return factor / size


def folded_gram(part):
    count, rows, _ = part.shape
    gram = jnp.einsum("brc,bsc->brs", part, part, precision=HIGHEST)
    band = jnp.arange(rows) // MUON_ROWS
    gram = jnp.where(band[:, None] == band[None, :], gram, 0.0)
    return jnp.sum(gram.reshape(count, rows // MUON_ROWS, MUON_ROWS, rows), 1)


def orthogonal(factor, part):
    return jnp.einsum("brs,bsc->brc", factor, part, precision=HIGHEST)


def body(
    grid,
    codes_in,
    codes_out,
    pad_mask,
    text_table,
    text_index,
    attend_in,
    attend_out,
    expand_weights,
    shrink_weights,
    attend_in_momentum,
    attend_out_momentum,
    expand_momentum,
    shrink_momentum,
    embed_table,
    head_table,
    norm_params,
    embed_first,
    embed_second,
    head_first,
    head_second,
    norm_first,
    norm_second,
):
    sizes = grid.sizes
    at_z, at_x, at_y, at_c = (grid.index(axis) for axis in ("z", "x", "y", "c"))
    width = norm_params.shape[1]
    clips, frames_part, books = codes_in.shape
    inner = sizes["c"]
    group = sizes["z"] * sizes["x"]
    split = sizes["y"] * inner
    frames = frames_part * split
    own_frames = frames // inner
    rows_in, members, cols_in = attend_in.shape
    cols_out = attend_out.shape[2]
    quarters = expand_weights.shape[1] // cols_in
    table_rows = embed_table.shape[1]

    token_count = grid.total(
        jnp.sum(pad_mask.astype(F32)).reshape(1, 1), ("c", "y", "x", "z")
    )[0, 0]

    codes = jnp.stack([codes_in, codes_out, pad_mask], 0).transpose(0, 3, 1, 2)
    pieces = grid.gather(codes, ("c", "y"))
    codes = jnp.zeros((3, books, clips, sizes["y"], inner, frames_part), jnp.int32)
    for piece, moved in pieces:
        codes = lax.dynamic_update_slice(
            codes,
            piece[:, :, :, None, None],
            (0, 0, 0, grid.source(moved, "y"), grid.source(moved, "c"), 0),
        )
    codes = codes.reshape(3, books, clips, frames)
    codes_all = codes[0]
    mine = chosen(codes, at_y, 2)
    next_codes, counted = mine[1].T, mine[2].T.astype(F32)

    def dp_place(moved):
        return grid.source(moved, "z") * sizes["x"] + grid.source(moved, "x")

    table = jnp.zeros((books, group * table_rows, width), BF16)
    for piece, moved in grid.gather(embed_table.astype(BF16), ("z", "x")):
        table = lax.dynamic_update_slice(table, piece, (0, dp_place(moved) * table_rows, 0))
    at_tensor = at_y * inner + at_c
    owner = codes_all // table_rows % split
    local = codes_all // (table_rows * split) * table_rows + codes_all % table_rows
    slots = jnp.where(owner == at_tensor, local, -1)
    slots = slots.reshape(books, clips, inner, own_frames)

    def one_hot(places):
        return (places[..., None] == jnp.arange(group * table_rows)).astype(BF16)

    hot = one_hot(slots)
    partial = jnp.einsum("kyrfv,kvd->yrfd", hot, table, preferred_element_type=F32)
    both = grid.scatter("c", lambda target: chosen(partial, target, 1))
    embedded = grid.scatter("y", lambda target: chosen(both, target, 0))
    residual = embedded + sinusoid(at_c * own_frames, own_frames, width)

    def gather_rows(shard, axes):
        count, rows, cols = shard.shape
        full = jnp.zeros((count, group * rows, sizes["y"] * cols), BF16)
        for piece, moved in grid.gather(shard, axes):
            full = lax.dynamic_update_slice(
                full, piece, (0, dp_place(moved) * rows, grid.source(moved, "y") * cols)
            )
        return full

    def gather_cols(shard, axes):
        count, rows, cols = shard.shape
        full = jnp.zeros((count, sizes["y"] * rows, group * cols), BF16)
        for piece, moved in grid.gather(shard, axes):
            full = lax.dynamic_update_slice(
                full, piece, (0, grid.source(moved, "y") * rows, dp_place(moved) * cols)
            )
        return full

    turned_in = attend_in.transpose(1, 0, 2)
    weight_in = gather_rows(turned_in.astype(BF16), ("z", "x", "y"))
    cols_pack = jnp.concatenate(
        [attend_out, shrink_weights.reshape(quarters, cols_in, cols_out)], 0
    )
    weight_cols = gather_cols(cols_pack.astype(BF16), ("z", "y", "x"))
    weight_out, weight_shrink = weight_cols[:2], weight_cols[2:]
    turned_expand = expand_weights.reshape(rows_in, quarters, cols_in).transpose(1, 0, 2)
    weight_expand = gather_rows(turned_expand.astype(BF16), ("y", "z", "x"))
    head_place = []
    head = jnp.zeros((books, group * sizes["y"] * table_rows, width), BF16)
    for piece, moved in grid.gather(head_table.astype(BF16), ("x", "z", "y")):
        place = dp_place(moved) * sizes["y"] + grid.source(moved, "y")
        head = lax.dynamic_update_slice(head, piece, (0, place * table_rows, 0))
    head_index = jnp.arange(group * sizes["y"] * table_rows)
    head_ids = (head_index // table_rows * inner + at_c) * table_rows + head_index % table_rows

    def spread(rows):
        rows = rows.astype(BF16)
        full = jnp.zeros((inner,) + rows.shape, BF16)
        for piece, moved in grid.gather(rows, ("c",)):
            full = lax.dynamic_update_slice(full, piece[None], (grid.source(moved, "c"), 0, 0))
        return full.reshape(frames, width)

    def collect(partial_rows):
        parts = partial_rows.reshape(inner, own_frames, width)
        running = chosen(parts, lax.rem(at_c + inner - 1, inner), 0)
        for step in range(1, inner):
            arrived = grid.rotate(running, "c")
            running = arrived + chosen(parts, lax.rem(at_c + 2 * inner - step - 1, inner), 0)
        return running

    def heads_of(values):
        return values.reshape(values.shape[0], 1, -1, HEAD_DIM)

    def product(left, right):
        return jnp.dot(left, right, preferred_element_type=F32)

    gains = norm_params
    memory = jnp.take(text_table, chosen(text_index, at_y, 0), axis=0)

    normed_one = spread(layer_norm(residual, gains[0], gains[1]))
    triple = jnp.einsum(
        "fd,jdn->jfn", normed_one, weight_in[:3], preferred_element_type=F32
    ).astype(BF16)
    self_parts = tuple(heads_of(triple[member]) for member in range(3))
    self_mixed, self_total = attend(*self_parts, True)
    self_mixed = self_mixed[:, 0]
    residual_one = residual + collect(product(self_mixed, weight_out[0]))

    normed_two = spread(layer_norm(residual_one, gains[2], gains[3]))
    cross_q = product(normed_two, weight_in[3]).astype(BF16)
    cross_kv = jnp.einsum(
        "sd,jdn->jsn", memory, weight_in[4:6], preferred_element_type=F32
    ).astype(BF16)
    cross_parts = (heads_of(cross_q), heads_of(cross_kv[0]), heads_of(cross_kv[1]))
    cross_mixed, cross_total = attend(*cross_parts, False)
    cross_mixed = cross_mixed[:, 0]
    residual_two = residual_one + collect(product(cross_mixed, weight_out[1]))

    normed_three = spread(layer_norm(residual_two, gains[4], gains[5]))
    upper = jnp.einsum("fd,bdn->bfn", normed_three, weight_expand, preferred_element_type=F32)
    active = exact_gelu(upper).astype(BF16)
    residual_three = residual_two + collect(
        jnp.einsum("bfn,bnd->fd", active, weight_shrink, preferred_element_type=F32)
    )

    final = spread(layer_norm(residual_three, gains[6], gains[7]))
    logits = jnp.einsum("fd,kvd->kfv", final, head, preferred_element_type=F32)
    row_max = jnp.max(logits, -1)
    is_target = head_ids[None, None, :] == next_codes.T[:, :, None]
    picked = jnp.sum(jnp.where(is_target, logits, 0.0), -1)
    row_sum = jnp.sum(jnp.exp(logits - row_max[..., None]), -1)
    top = row_max
    stats = grid.gather(jnp.stack([row_max, row_sum, picked], 0), ("c",))
    for piece, _ in stats[1:]:
        top = jnp.maximum(top, piece[0])
    row_sum = sum(piece[1] * jnp.exp(piece[0] - top) for piece, _ in stats)
    picked = sum(piece[2] for piece, _ in stats)
    log_total = top + jnp.log(row_sum)
    live = counted.T
    loss_local = jnp.where(at_c == 0, jnp.sum((log_total - picked) * live), 0.0)
    grad_logits = (
        (jnp.exp(logits - log_total[..., None]) - is_target.astype(F32))
        * (live / token_count)[..., None]
    ).astype(BF16)
    grad_head = jnp.einsum("kfv,fd->kvd", grad_logits, final, preferred_element_type=F32)
    grad_final = collect(
        jnp.einsum("kfv,kvd->fd", grad_logits, head, preferred_element_type=F32)
    )

    def scatter_head(value):
        value = value.reshape(books, sizes["z"], sizes["x"], sizes["y"], table_rows, width)
        value = grid.scatter("y", lambda target: chosen(value, target, 3))
        value = grid.scatter("z", lambda target: chosen(value, target, 1))
        return grid.scatter("x", lambda target: chosen(value, target, 1))

    def scatter_rows(value, axes):
        count = value.shape[0]
        value = value.reshape(count, sizes["z"], sizes["x"], rows_in, sizes["y"], cols_in)
        dims = {"z": 1, "x": 2, "y": 4}
        for axis in axes:
            spot = dims.pop(axis)
            whole = value
            value = grid.scatter(axis, lambda target: chosen(whole, target, spot))
            dims = {name: at - (at > spot) for name, at in dims.items()}
        return value

    def scatter_cols(value, axes):
        count = value.shape[0]
        value = value.reshape(count, sizes["y"], cols_in, sizes["z"], sizes["x"], cols_out)
        dims = {"y": 1, "z": 3, "x": 4}
        for axis in axes:
            spot = dims.pop(axis)
            whole = value
            value = grid.scatter(axis, lambda target: chosen(whole, target, spot))
            dims = {name: at - (at > spot) for name, at in dims.items()}
        return value

    grad_head = scatter_head(grad_head)
    grad, gain_final, shift_final = norm_back(residual_three, gains[6], gains[7], grad_final)

    rows_grad = spread(grad)
    grad_active = jnp.einsum(
        "fd,bnd->bfn", rows_grad, weight_shrink, preferred_element_type=F32
    )
    grad_shrink = jnp.einsum("bfn,fd->bnd", active, rows_grad, preferred_element_type=F32)
    grad_upper = jax.vjp(exact_gelu, upper)[1](grad_active)[0].astype(BF16)
    grad_expand = jnp.einsum("fd,bfn->bdn", normed_three, grad_upper, preferred_element_type=F32)
    grad_normed = collect(
        jnp.einsum("bfn,bdn->fd", grad_upper, weight_expand, preferred_element_type=F32)
    )
    grad_shrink = scatter_cols(grad_shrink, ("y", "x", "z"))
    grad_expand = scatter_rows(grad_expand, ("x", "y", "z"))
    change, gain_three, shift_three = norm_back(residual_two, gains[4], gains[5], grad_normed)
    grad = grad + change

    rows_grad = spread(grad)
    grad_mixed = lax.dot_general(
        rows_grad, weight_out[1], (((1,), (1,)), ((), ())), preferred_element_type=F32
    ).astype(BF16)
    grad_cross_out = jnp.einsum("fn,fd->nd", cross_mixed, rows_grad, preferred_element_type=F32)
    grad_q, grad_k, grad_v = attend_back(*cross_parts, cross_total, heads_of(grad_mixed), False)
    grad_q = grad_q.astype(BF16).reshape(frames, -1)
    grad_kv = jnp.stack([grad_k, grad_v], 0).astype(BF16).reshape(2, memory.shape[0], -1)
    grad_cross_q = jnp.einsum("fd,fn->dn", normed_two, grad_q, preferred_element_type=F32)
    grad_cross_kv = jnp.einsum("sd,jsn->jdn", memory, grad_kv, preferred_element_type=F32)
    grad_normed = collect(
        jnp.einsum("fn,dn->fd", grad_q, weight_in[3], preferred_element_type=F32)
    )
    change, gain_two, shift_two = norm_back(residual_one, gains[2], gains[3], grad_normed)
    grad = grad + change

    rows_grad = spread(grad)
    grad_mixed = lax.dot_general(
        rows_grad, weight_out[0], (((1,), (1,)), ((), ())), preferred_element_type=F32
    ).astype(BF16)
    grad_self_out = jnp.einsum("fn,fd->nd", self_mixed, rows_grad, preferred_element_type=F32)
    grad_out = scatter_cols(jnp.stack([grad_self_out, grad_cross_out], 0), ("y", "x", "z"))
    grad_cross_in = scatter_rows(
        jnp.concatenate([grad_cross_q[None], grad_cross_kv], 0), ("x", "y", "z")
    )
    grad_q, grad_k, grad_v = attend_back(*self_parts, self_total, heads_of(grad_mixed), True)
    grad_triple = jnp.stack([grad_q, grad_k, grad_v], 0).astype(BF16).reshape(3, frames, -1)
    grad_normed = collect(
        jnp.einsum("jfn,jdn->fd", grad_triple, weight_in[:3], preferred_element_type=F32)
    )
    grad_self_in = jnp.einsum(
        "fd,jfn->jdn", normed_one, grad_triple, preferred_element_type=F32
    )
    grad_self_in = scatter_rows(grad_self_in, ("y", "x", "z"))
    change, gain_one, shift_one = norm_back(residual, gains[0], gains[1], grad_normed)
    grad = grad + change

    rows_grad = grad.astype(BF16)
    all_grad = jnp.zeros((clips, inner, own_frames, width), BF16)
    for piece, moved in grid.gather(rows_grad, ("y", "c")):
        all_grad = lax.dynamic_update_slice(
            all_grad, piece[None, None], (grid.source(moved, "y"), grid.source(moved, "c"), 0, 0)
        )
    grad_table = jnp.einsum("kyrfv,yrfd->kvd", hot, all_grad, preferred_element_type=F32)
    grad_table = grad_table.reshape(books, sizes["z"], sizes["x"], table_rows, width)
    grad_table = grid.scatter("x", lambda target, v=grad_table: chosen(v, target, 2))
    grad_table = grid.scatter("z", lambda target, v=grad_table: chosen(v, target, 1))

    norm_grads = [gain_one, shift_one, gain_two, shift_two, gain_three, shift_three]
    norm_grads = jnp.stack(norm_grads + [gain_final, shift_final], 0)
    loss_row = jnp.full((8, width), loss_local)
    summed = grid.total(jnp.concatenate([norm_grads, loss_row], 0), ("c", "y", "x", "z"))
    grad_norm, loss_sum = summed[:8], summed[8, 0]

    next_in = MOMENTUM * attend_in_momentum.transpose(1, 0, 2) + jnp.concatenate(
        [grad_self_in, grad_cross_in], 0
    )
    next_out = MOMENTUM * attend_out_momentum + grad_out
    turned_momentum = expand_momentum.reshape(rows_in, quarters, cols_in).transpose(1, 0, 2)
    next_expand = MOMENTUM * turned_momentum + grad_expand
    next_expand = next_expand.transpose(1, 0, 2).reshape(expand_weights.shape)
    next_shrink = MOMENTUM * shrink_momentum + grad_shrink.reshape(shrink_weights.shape)

    stack_rows = min(128, cols_in)
    data_blocks = jnp.concatenate(
        [next_out.reshape(-1, stack_rows, cols_out), next_shrink.reshape(-1, stack_rows, cols_out)],
        0,
    )
    tensor_grams = jnp.concatenate([folded_gram(next_in), folded_gram(next_expand[None])], 0)
    tensor_factor = newton(grid.total(tensor_grams, ("c", "y")))
    data_factor = newton(grid.total(folded_gram(data_blocks), ("x", "z")))
    ortho_in = orthogonal(tensor_factor[:members], next_in)
    ortho_expand = orthogonal(tensor_factor[members:], next_expand[None])[0]
    ortho_data = orthogonal(data_factor, data_blocks)
    count_out = next_out.size // (stack_rows * cols_out)
    ortho_out = ortho_data[:count_out].reshape(next_out.shape)
    ortho_shrink = ortho_data[count_out:].reshape(next_shrink.shape)
    attend_in_new = (turned_in * (1.0 - 0.5 * DECAY) - 0.5 * ortho_in).transpose(1, 0, 2)
    attend_out_new = attend_out * (1.0 - 1.0 * DECAY) - 1.0 * ortho_out
    expand_new = expand_weights * (1.0 - 0.5 * DECAY) - 0.5 * ortho_expand
    shrink_new = shrink_weights * (1.0 - 0.5 * DECAY) - 0.5 * ortho_shrink
    embed_new, embed_first_new, embed_second_new = adam(
        embed_table, embed_first, embed_second, grad_table, 0.1, DECAY
    )
    head_new, head_first_new, head_second_new = adam(
        head_table, head_first, head_second, grad_head, 0.03, DECAY
    )
    norm_new, norm_first_new, norm_second_new = adam(
        norm_params, norm_first, norm_second, grad_norm, 0.5, 0.0
    )
    return (
        loss_sum,
        token_count,
        attend_in_new,
        attend_out_new,
        expand_new,
        shrink_new,
        next_in.transpose(1, 0, 2),
        next_out,
        next_expand,
        next_shrink,
        embed_new,
        head_new,
        norm_new,
        embed_first_new,
        embed_second_new,
        head_first_new,
        head_second_new,
        norm_first_new,
        norm_second_new,
    )


def solution(mesh):
    n_dp, n_tensor = mesh.shape["dp"], mesh.shape["tensor"]
    sizes = {"z": n_dp // 2, "x": 2, "y": 2, "c": n_tensor // 2}
    cut = Mesh(mesh.devices.reshape(tuple(sizes.values())), tuple(sizes))
    dp, tensor = ("z", "x"), ("y", "c")
    table = P(None, dp + tensor, None)
    matrices = (P(dp, None, tensor), P(None, tensor, dp), P(dp, tensor), P(tensor, dp))
    return jax.shard_map(
        functools.partial(body, Grid(sizes)),
        mesh=cut,
        in_specs=(P(dp, tensor, None),) * 3
        + (P(), P(dp, None))
        + matrices * 2
        + (table, table, P())
        + (table,) * 4
        + (P(), P()),
        out_specs=(P(), P())
        + matrices * 2
        + (table, table, P())
        + (table,) * 4
        + (P(), P()),
        check_vma=False,
    )
```

```python
import functools
import math

import jax
import jax.numpy as jnp
from jax import lax
from jax.experimental import pallas as pl
from jax.experimental.pallas import tpu as pltpu
from jax.sharding import Mesh
from jax.sharding import PartitionSpec as P

HEAD_DIM = 64
MUON_ROWS = 32
STEP = 10

HIGHEST = lax.Precision.HIGHEST
NEWTON = (3.4445, -4.775, 2.0315)
BETA_ONE = 0.9
BETA_TWO = 0.95
ADAM_EPS = 1e-08
DECAY = 0.01
MOMENTUM = 0.95
BF16 = jnp.bfloat16
F32 = jnp.float32
LANES = 128
BUDGET = 8
BACK_BUDGET = 16
KERNEL_VMEM = 48 * 1024 * 1024


def layer_norm(values, gain, shift):
    centred = values - jnp.mean(values, -1, keepdims=True)
    variance = jnp.mean(centred * centred, -1, keepdims=True)
    return centred * lax.rsqrt(variance + 1e-05) * gain + shift


def norm_back(values, gain, shift, grad):
    result, backward = jax.vjp(layer_norm, values, gain, shift)
    return backward(grad)


def exact_gelu(values):
    return jax.nn.gelu(values, approximate=False)


def sinusoid(first, length, width):
    half = width // 2
    rates = jnp.exp(jnp.arange(half, dtype=jnp.float32) * (-math.log(10000.0) / half))
    places = (first + jnp.arange(length, dtype=jnp.int32)).astype(jnp.float32)
    angles = places[:, None] * rates[None, :]
    return jnp.concatenate([jnp.sin(angles), jnp.cos(angles)], -1)


def adam(weight, first, second, gradient, rate, decay):
    first = BETA_ONE * first + (1.0 - BETA_ONE) * gradient
    second = BETA_TWO * second + (1.0 - BETA_TWO) * gradient * gradient
    direction = (
        first / (1.0 - BETA_ONE**STEP) / (jnp.sqrt(second / (1.0 - BETA_TWO**STEP)) + ADAM_EPS)
    )
    return (weight - rate * (direction + decay * weight), first, second)


class Grid:
    def __init__(self, sizes):
        self.sizes = sizes

    def index(self, axis):
        return lax.axis_index(axis)

    def rotate(self, value, axis):
        size = self.sizes[axis]
        return lax.ppermute(value, axis, [(i, (i + 1) % size) for i in range(size)])

    def swap(self, value, axis, step=1):
        return lax.ppermute(value, axis, [(i, i ^ step) for i in range(self.sizes[axis])])

    def total(self, value, axes):
        for axis in axes:
            step = 1
            while step < self.sizes[axis]:
                value = value + lax.ppermute(
                    value, axis, [(i, i ^ step) for i in range(self.sizes[axis])]
                )
                step *= 2
        return value

    def ring(self, shard, axis):
        held = [shard]
        for _ in range(1, self.sizes[axis]):
            held.append(self.rotate(held[-1], axis))
        return [held[-r % self.sizes[axis]] for r in range(self.sizes[axis])]

    def ring_sum(self, parts, axis):
        size = self.sizes[axis]
        running = parts[size - 1]
        for step in range(1, size):
            arrived = self.rotate(running.astype(BF16), axis)
            running = arrived.astype(F32) + parts[size - 1 - step].astype(F32)
        return running

    def rounds(self, tasks, budget, early=None, pack=True):
        done, results, last, when = {}, {}, [], 0
        waiting = list(tasks)
        while waiting:
            used, picked = {}, []
            for name in waiting:
                axis, size, needs, between, first, _ = tasks[name]
                ready = when >= first and all(
                    done.get(need, when) + between < when for need in needs
                )
                load = used.get(axis, 0)
                if ready and (load == 0 or load + size <= budget):
                    used[axis] = load + size
                    picked.append(name)
            messages = {}
            for name in picked:
                value = tasks[name][-1](results)
                key = (tasks[name][0], value.shape[-1], None if pack else name)
                messages.setdefault(key, []).append((name, value))
            if messages:
                values = [
                    lists[0][1]
                    if len(lists) == 1
                    else jnp.concatenate([value.reshape(-1, key[1]) for _, value in lists], 0)
                    for key, lists in messages.items()
                ]
                held = last + (early or {}).get(when, [])
                tied = lax.optimization_barrier((values, held))[0]
                last = []
                for ((axis, _, _), lists), value in zip(messages.items(), tied):
                    arrived = self.rotate(value, axis) if axis == "z" else self.swap(value, axis)
                    last.append(arrived)
                    start = 0
                    for name, sent in lists:
                        results[name] = arrived
                        if len(lists) > 1:
                            rows = sent.size // sent.shape[-1]
                            results[name] = arrived[start : start + rows].reshape(sent.shape)
                            start += rows
                        done[name] = when
            waiting = [name for name in waiting if name not in picked]
            when += 1
        return results


def chosen(array, index, axis):
    return lax.dynamic_index_in_dim(array, index, axis, keepdims=False)


def move_blocks(array, order):
    rows, cols = array.shape
    count = order.shape[0]
    block = cols // count
    if block % LANES or rows % 16:
        return jnp.take(array.reshape(rows, count, block), order, axis=1).reshape(rows, cols)

    def kernel(order_ref, from_ref, to_ref):
        to_ref[...] = from_ref[...]

    return pl.pallas_call(
        kernel,
        grid_spec=pltpu.PrefetchScalarGridSpec(
            num_scalar_prefetch=1,
            grid=(count,),
            in_specs=[pl.BlockSpec((rows, block), lambda p, order: (0, order[p]))],
            out_specs=pl.BlockSpec((rows, block), lambda p, order: (0, p)),
        ),
        out_shape=jax.ShapeDtypeStruct(array.shape, array.dtype),
        cost_estimate=pl.CostEstimate(
            flops=0, bytes_accessed=2 * array.size * array.dtype.itemsize, transcendentals=0
        ),
    )(order, array)


def arranged(blocks, order):
    count, books, rows, cols = blocks.shape
    if rows % 16:
        return jnp.take(blocks, order, axis=0).transpose(1, 0, 2, 3)

    def kernel(order_ref, from_ref, to_ref):
        to_ref[...] = from_ref[...].reshape(to_ref.shape)

    return pl.pallas_call(
        kernel,
        grid_spec=pltpu.PrefetchScalarGridSpec(
            num_scalar_prefetch=1,
            grid=(count,),
            in_specs=[pl.BlockSpec((1, books, rows, cols), lambda p, order: (order[p], 0, 0, 0))],
            out_specs=pl.BlockSpec((books, 1, rows, cols), lambda p, order: (0, p, 0, 0)),
        ),
        out_shape=jax.ShapeDtypeStruct((books, count, rows, cols), blocks.dtype),
        cost_estimate=pl.CostEstimate(
            flops=0, bytes_accessed=2 * blocks.size * blocks.dtype.itemsize, transcendentals=0
        ),
    )(order, blocks)


def after(value, token):
    return lax.optimization_barrier((value, token))[0]


def contract(left, right, left_dim, right_dim):
    return lax.dot_general(
        left, right, (((left_dim,), (right_dim,)), ((), ())), preferred_element_type=F32
    )


def contract_rows(left, right):
    return contract(left, right, 1, 0)


def spans(frames, keys, causal):
    block = min(256 if causal else 512, frames)
    return [
        (first, block, min(keys, first + block) if causal else keys)
        for first in range(0, frames, block)
    ]


def softmax_down(query, key_rows, first, causal):
    scores = contract(key_rows, query, 1, 1) * 0.125
    if causal:
        key_at = lax.broadcasted_iota(jnp.int32, scores.shape, 0)
        query_at = first + lax.broadcasted_iota(jnp.int32, scores.shape, 1)
        scores = jnp.where(key_at <= query_at, scores, -jnp.inf)
    expo = jnp.exp(scores - jnp.max(scores, 0, keepdims=True))
    return expo * (1.0 / jnp.sum(expo, 0, keepdims=True))


def head_lanes(shape, head):
    lane = lax.broadcasted_iota(jnp.int32, shape, 1)
    return (lane // HEAD_DIM) == head


def attend_kernel(causal, query_ref, key_ref, value_ref, mixed_ref):
    frames, keys = query_ref.shape[0], key_ref.shape[0]
    turned = value_ref[...].astype(F32).T.astype(BF16)
    for first, block, last in spans(frames, keys, causal):
        query = query_ref[pl.ds(first, block), :]
        parts = []
        for head in range(LANES // HEAD_DIM):
            own = jnp.where(head_lanes(query.shape, head), query, jnp.zeros_like(query))
            probs = softmax_down(own, key_ref[pl.ds(0, last), :], first, causal).astype(BF16)
            parts.append(
                contract_rows(
                    turned[head * HEAD_DIM : (head + 1) * HEAD_DIM, :last],
                    probs,
                )
            )
        mixed_ref[pl.ds(first, block), :] = jnp.concatenate(parts, 0).T.astype(BF16)


def attend_back_kernel(
    causal,
    query_ref,
    key_ref,
    value_ref,
    grad_ref,
    grad_query_ref,
    grad_key_ref,
    grad_value_ref,
    key_sum,
    value_sum,
):
    frames, keys = query_ref.shape[0], key_ref.shape[0]
    turned = key_ref[...].astype(F32).T.astype(BF16)
    key_sum[...] = jnp.zeros_like(key_sum)
    value_sum[...] = jnp.zeros_like(value_sum)
    for first, block, last in spans(frames, keys, causal):
        query = query_ref[pl.ds(first, block), :]
        grad = grad_ref[pl.ds(first, block), :]
        parts = []
        for head in range(LANES // HEAD_DIM):
            lanes = head_lanes(query.shape, head)
            own = jnp.where(lanes, query, jnp.zeros_like(query))
            own_grad = jnp.where(lanes, grad, jnp.zeros_like(grad))
            probs = softmax_down(own, key_ref[pl.ds(0, last), :], first, causal)
            grad_probs = contract(value_ref[pl.ds(0, last), :], own_grad, 1, 1)
            product = probs * grad_probs
            grad_scores = (product - probs * jnp.sum(product, 0, keepdims=True)).astype(BF16)
            value_sum[pl.ds(0, last), :] += contract_rows(probs.astype(BF16), own_grad)
            key_sum[pl.ds(0, last), :] += contract_rows(grad_scores, own)
            parts.append(
                contract_rows(
                    turned[head * HEAD_DIM : (head + 1) * HEAD_DIM, :last],
                    grad_scores,
                )
            )
        grad_query_ref[pl.ds(first, block), :] = (jnp.concatenate(parts, 0).T * 0.125).astype(BF16)
    grad_key_ref[...] = (key_sum[...] * 0.125).astype(BF16)
    grad_value_ref[...] = value_sum[...].astype(BF16)


def attend(queries, keys, values, causal):
    frames, key_rows = queries[0].shape[0], keys[0].shape[0]
    count = queries[2]
    cost = 4 * frames * key_rows * LANES * count * 2

    def spec(rows, start):
        return pl.BlockSpec((rows, LANES), lambda p, start=start: (0, start + p))

    return pl.pallas_call(
        functools.partial(attend_kernel, causal),
        grid=(count,),
        in_specs=[
            spec(frames, queries[1]),
            spec(key_rows, keys[1]),
            spec(key_rows, values[1]),
        ],
        out_specs=spec(frames, 0),
        out_shape=jax.ShapeDtypeStruct((frames, count * LANES), BF16),
        compiler_params=pltpu.CompilerParams(vmem_limit_bytes=KERNEL_VMEM),
        cost_estimate=pl.CostEstimate(
            flops=cost, bytes_accessed=cost // 256, transcendentals=cost // 256
        ),
    )(queries[0], keys[0], values[0])


def attend_back(queries, keys, values, grad, causal):
    frames, key_rows = queries[0].shape[0], keys[0].shape[0]
    count = queries[2]
    cost = 10 * frames * key_rows * LANES * count * 2

    def spec(rows, start):
        return pl.BlockSpec((rows, LANES), lambda p, start=start: (0, start + p))

    wide = count * LANES
    return pl.pallas_call(
        functools.partial(attend_back_kernel, causal),
        grid=(count,),
        in_specs=[
            spec(frames, queries[1]),
            spec(key_rows, keys[1]),
            spec(key_rows, values[1]),
            spec(frames, 0),
        ],
        out_specs=[spec(frames, 0), spec(key_rows, 0), spec(key_rows, 0)],
        out_shape=[
            jax.ShapeDtypeStruct((frames, wide), BF16),
            jax.ShapeDtypeStruct((key_rows, wide), BF16),
            jax.ShapeDtypeStruct((key_rows, wide), BF16),
        ],
        scratch_shapes=[pltpu.VMEM((key_rows, LANES), F32), pltpu.VMEM((key_rows, LANES), F32)],
        compiler_params=pltpu.CompilerParams(vmem_limit_bytes=KERNEL_VMEM),
        cost_estimate=pl.CostEstimate(
            flops=cost, bytes_accessed=cost // 512, transcendentals=cost // 512
        ),
    )(queries[0], keys[0], values[0], grad)


def newton(grams):
    count, _, rows = grams.shape
    repeats = rows // MUON_ROWS
    band = jnp.arange(rows) // MUON_ROWS
    mask = band[:, None] == band[None, :]
    eye = jnp.eye(rows, dtype=F32)
    gram = jnp.where(mask, jnp.tile(grams, (1, repeats, 1)), 0.0)
    diagonal = jnp.sum(gram * eye, -1).reshape(count, repeats, MUON_ROWS)
    size = jnp.sqrt(jnp.sum(diagonal, -1, keepdims=True)) + 1e-07
    size = jnp.broadcast_to(size, diagonal.shape).reshape(count, rows, 1)
    gram = gram / (size * size)

    def times(left, right):
        return jnp.einsum("brs,bst->brt", left, right, precision=HIGHEST)

    factor = None
    for repeat in range(5):
        mixing = NEWTON[0] * eye + NEWTON[1] * gram + NEWTON[2] * times(gram, gram)
        factor = mixing if factor is None else times(mixing, factor)
        if repeat < 4:
            gram = times(mixing, times(gram, mixing))
    return factor / size


def folded_gram(part):
    count, rows, _ = part.shape
    gram = jnp.einsum("brc,bsc->brs", part, part, precision=HIGHEST)
    band = jnp.arange(rows) // MUON_ROWS
    gram = jnp.where(band[:, None] == band[None, :], gram, 0.0)
    return jnp.sum(gram.reshape(count, rows // MUON_ROWS, MUON_ROWS, rows), 1)


def orthogonal(factor, part):
    return jnp.einsum("brs,bsc->brc", factor, part, precision=HIGHEST)


def body(
    grid,
    codes_in,
    codes_out,
    pad_mask,
    text_table,
    text_index,
    attend_in,
    attend_out,
    expand_weights,
    shrink_weights,
    attend_in_momentum,
    attend_out_momentum,
    expand_momentum,
    shrink_momentum,
    embed_table,
    head_table,
    norm_params,
    embed_first,
    embed_second,
    head_first,
    head_second,
    norm_first,
    norm_second,
):
    sizes = grid.sizes
    at_z, at_x, at_y, at_c = (grid.index(axis) for axis in ("z", "x", "y", "c"))
    deep, inner = sizes["z"], sizes["c"]
    width = norm_params.shape[1]
    clips, frames_part, books = codes_in.shape
    frames = frames_part * 2 * inner
    own_frames = frames // inner
    rows_in, members, cols_in = attend_in.shape
    cols_out = attend_out.shape[2]
    table_rows = embed_table.shape[1]
    groups = deep * 2

    place = jnp.arange(groups)
    order_near = (place % deep + at_z) % deep * 2 + (place // deep + at_x) % 2
    order_true = (place % 2 + at_x) % 2 * deep + (place // 2 - at_z) % deep

    def near(array):
        return move_blocks(array, order_near)

    def true(array):
        return move_blocks(array, order_true)

    codes = jnp.stack([codes_in, codes_out, pad_mask], 0).transpose(0, 3, 1, 2)

    def placed(pieces, axis):
        full = jnp.zeros((len(pieces),) + pieces[0].shape, pieces[0].dtype)
        for step, piece in enumerate(pieces):
            full = lax.dynamic_update_index_in_dim(
                full, piece, (lax.axis_index(axis) + step) % len(pieces), 0
            )
        return full

    def all_along(piece, axis):
        size = sizes[axis]
        held = [piece]
        for _ in range(1, size):
            held.append(
                lax.ppermute(held[-1], axis, [(i, (i + 1) % size) for i in range(size)])
            )
        return placed([held[-step % size] for step in range(size)], axis)

    codes = all_along(all_along(codes, "c"), "y")
    codes = codes.transpose(2, 3, 4, 0, 1, 5).reshape(3, books, clips, frames)
    group_count = jnp.sum(codes[2])
    codes = chosen(codes, at_y, 2)
    next_codes, live = codes[1], codes[2].astype(F32)
    codes_own = codes[0]
    codes_other = lax.ppermute(
        jnp.concatenate([codes_own, jnp.full((books, frames), group_count)], 0),
        "x",
        [(0, 1), (1, 0)],
    )
    pair_count = (group_count + codes_other[books, 0]).astype(F32).reshape(1, 1)
    codes_other = codes_other[:books]

    turned_in = attend_in.transpose(1, 0, 2)
    turned_out = attend_out.transpose(0, 2, 1)

    def side_by_side(parts):
        return jnp.concatenate([part.astype(BF16) for part in parts], 1)

    shards = {
        "embed": embed_table.astype(BF16),
        "self": side_by_side(list(turned_in[:3]) + [turned_out[0]]),
        "cross": side_by_side(list(turned_in[3:]) + [turned_out[1]]),
        "expand": expand_weights.astype(BF16),
        "shrink": shrink_weights.T.astype(BF16),
    }
    routes = {"embed": "zy", "self": "zxy", "cross": "zxy", "expand": "zxy", "shrink": "zyx"}
    tasks = {}

    def piece(results, group, axis, step):
        return results[group + axis + str(step)] if step or axis != "z" else shards[group]

    def pair(results, group, axis, step):
        return jnp.concatenate(
            [piece(results, group, "z", step), piece(results, group, axis, step)], 0
        )

    for group, route in routes.items():
        weight = 4 if group == "embed" else 2
        for step in range(deep):
            name = group + "z" + str(step)
            needs = [name] if step else []
            if step:
                ahead = [group + "z" + str(step - 1)] if step > 1 else []
                tasks[name] = (
                    "z", weight, ahead, 0, 0, lambda r, g=group, k=step: piece(r, g, "z", k - 1)
                )
            first = group + route[1] + str(step)
            tasks[first] = (
                route[1], weight, needs, 0, 0, lambda r, g=group, k=step: piece(r, g, "z", k)
            )
            if len(route) > 2:
                tasks[group + route[2] + str(step)] = (
                    route[2],
                    2 * weight,
                    [first],
                    0,
                    0,
                    lambda r, g=group, k=step, a=route[1]: pair(r, g, a, k),
                )
        if group == "self":
            last = ["embedy" + str(step) for step in range(deep)]
            tasks["rows"] = ("x", 8, last, 0, 0, lambda r: embedded_of(codes_other, table_of(r)))

    z_place = (at_z - jnp.arange(deep)) % deep
    y_place = jnp.stack([at_y, 1 - at_y])
    table_ids = ((z_place * 2 + at_x) * 2)[:, None] + y_place[None, :]
    table_ids = ((table_ids * inner + at_c)[:, :, None] * table_rows + jnp.arange(table_rows)).reshape(
        -1
    )
    kept_table = []

    def table_of(results):
        if not kept_table:
            pieces = []
            for step in range(deep):
                pieces += [piece(results, "embed", "z", step), piece(results, "embed", "y", step)]
            kept_table.append(jnp.concatenate(pieces, 1))
        return kept_table[0]

    def hot(codes):
        return (codes[..., None] == table_ids).astype(BF16)

    def embedded_of(codes, table):
        rows = jnp.einsum("kfv,kvd->fd", hot(codes), table, preferred_element_type=F32)
        rows = rows.reshape(inner, own_frames, width)
        rows = grid.ring_sum(
            [chosen(rows, (at_c + step) % inner, 0) for step in range(inner)], "c"
        )
        return rows.astype(BF16)

    results = grid.rounds(tasks, BUDGET, {2: [codes_other]}, pack=False)
    own_part = embedded_of(codes_own, table_of(results)).astype(F32)
    embedded = own_part + results["rows"].astype(F32)
    residual = near(embedded + sinusoid(at_c * own_frames, own_frames, width))

    def both_of(group):
        halves = [[[None] * deep, [None] * deep], [[None] * deep, [None] * deep]]
        inside = routes[group][1]
        for step in range(deep):
            spot = -step % deep
            first = [piece(results, group, "z", step), piece(results, group, inside, step)]
            far = piece(results, group, routes[group][2], step)
            far = [far[:rows_in], far[rows_in:]]
            for at, block in enumerate(first):
                halves[0 if inside == "x" else at][at if inside == "x" else 0][spot] = block
            for at, block in enumerate(far):
                halves[1 if inside == "x" else at][at if inside == "x" else 1][spot] = block
        return [jnp.concatenate(half[0] + half[1], 0) for half in halves]

    weight_self, weight_cross = both_of("self"), both_of("cross")
    weight_expand, weight_shrink = both_of("expand"), both_of("shrink")
    head_shard = after(head_table.astype(BF16), results["embedy" + str(deep - 1)])
    head = lax.all_gather(head_shard, ("z", "x", "y"), axis=0)
    head_order = (order_near[:, None] * 2 + y_place[None, :]).reshape(-1)
    head = arranged(head, head_order).reshape(books, -1, width)
    head_ids = (head_order * inner + at_c)[:, None] * table_rows + jnp.arange(table_rows)
    head_ids = head_ids.reshape(-1)

    def spread(rows):
        return placed(grid.ring(rows.astype(BF16), "c"), "c").reshape(frames, width)

    def collect(partial_rows):
        parts = partial_rows.reshape(inner, own_frames, width)
        running = chosen(parts, (at_c + inner - 1) % inner, 0)
        for step in range(1, inner):
            arrived = grid.rotate(running, "c")
            running = arrived + chosen(parts, (at_c + inner - 1 - step) % inner, 0)
        return running

    def product(left, right):
        return contract(left, right, 1, 0)

    def across(left, right):
        return contract(left, right, 1, 1)

    def down(left, right):
        return contract(left, right, 0, 0)

    gains = jnp.take(norm_params.reshape(8, groups, -1), order_near, axis=1).reshape(8, width)
    memory = jnp.take(text_table, chosen(text_index, at_y, 0), axis=0)
    memory = near(memory)
    pairs = cols_in // LANES
    triple = 3 * cols_in

    normed_one = spread(layer_norm(residual, gains[0], gains[1]))
    self_parts, self_mixed, total = [], [], 0.0
    for weight in weight_self:
        heads = product(normed_one, weight[:, :triple]).astype(BF16)
        parts = [(heads, member * pairs, pairs) for member in range(3)]
        mixed = attend(*parts, True)
        total = total + across(mixed, weight[:, triple:])
        self_parts.append(parts)
        self_mixed.append(mixed)
    residual_one = residual + collect(total)

    normed_two = spread(layer_norm(residual_one, gains[2], gains[3]))
    cross_parts, cross_mixed, total = [], [], 0.0
    for weight in weight_cross:
        query = product(normed_two, weight[:, :cols_in]).astype(BF16)
        key_value = product(memory, weight[:, cols_in:triple]).astype(BF16)
        parts = [(query, 0, pairs), (key_value, 0, pairs), (key_value, pairs, pairs)]
        mixed = attend(*parts, False)
        total = total + across(mixed, weight[:, triple:])
        cross_parts.append(parts)
        cross_mixed.append(mixed)
    residual_two = after(residual_one + collect(total), head)

    normed_three = spread(layer_norm(residual_two, gains[4], gains[5]))
    uppers, actives, total = [], [], 0.0
    for up, back in zip(weight_expand, weight_shrink):
        upper = product(normed_three, up)
        active = exact_gelu(upper).astype(BF16)
        total = total + across(active, back)
        uppers.append(upper)
        actives.append(active)
    residual_three = true(residual_two + collect(total))

    token_count = grid.total(after(pair_count, residual_one), ("z",))[0, 0]
    final = spread(layer_norm(residual_three, norm_params[6], norm_params[7]))
    logits = jnp.einsum("fd,kvd->kfv", final, head, preferred_element_type=F32)
    is_target = head_ids[None, None, :] == next_codes[:, :, None]
    row_max = jnp.max(logits, -1)
    picked = jnp.sum(jnp.where(is_target, logits, 0.0), -1)
    row_sum = jnp.sum(jnp.exp(logits - row_max[..., None]), -1)
    stats = grid.ring(jnp.stack([row_max, row_sum, picked], 0), "c")
    top = stats[0][0]
    for stat in stats[1:]:
        top = jnp.maximum(top, stat[0])
    row_sum = sum(stat[1] * jnp.exp(stat[0] - top) for stat in stats)
    picked = sum(stat[2] for stat in stats)
    log_total = top + jnp.log(row_sum)
    loss_local = jnp.where(at_c == 0, jnp.sum((log_total - picked) * live), 0.0)
    grad_logits = (
        (jnp.exp(logits - log_total[..., None]) - is_target.astype(F32))
        * (live / token_count)[..., None]
    ).astype(BF16)
    grad_final = collect(
        jnp.einsum("kfv,kvd->fd", grad_logits, head, preferred_element_type=F32)
    )
    tasks, sums = {}, {}

    def add(name, axis, size, needs, value, between=0, first=0):
        tasks[name] = (axis, size, needs, between, first, lambda r: value(r).astype(BF16))

    def once(name, make):
        def get(results):
            if name not in sums:
                sums[name] = make(results)
            return sums[name]

        return get

    def add_ring(name, size, needs, parts):
        get = once(name + "0", lambda r: parts(r)[deep - 1])
        for step in range(1, deep):
            add(name + "z" + str(step), "z", size, needs, get)
            needs = [name + "z" + str(step)]
            get = once(
                name + str(step),
                lambda r, n=needs[0], k=step: r[n].astype(F32) + parts(r)[deep - 1 - k].astype(F32),
            )
        return get

    def add_rows(name, size, route, first, own, other):
        half = width // 2
        if route[0] == "y":
            add(name + "y", "y", 8 * size, [], lambda r: other, 0, first)
            whole = once(name + "sum", lambda r: own + r[name + "y"].astype(F32))
            add(name + "x", "x", 4 * size, [name + "y"], lambda r: whole(r)[half:])
            quarter = once(
                name + "part", lambda r: whole(r)[:half] + r[name + "x"].astype(F32)
            )
        else:
            far = jnp.concatenate([own[half:].astype(BF16), other[half:].astype(BF16)], 0)
            add(name + "x", "x", 8 * size, [], lambda r: far, 0, first)
            add(
                name + "y",
                "y",
                4 * size,
                [name + "x"],
                lambda r: other[:half] + r[name + "x"][half:].astype(F32),
            )
            quarter = once(
                name + "part",
                lambda r: own[:half]
                + r[name + "x"][:half].astype(F32)
                + r[name + "y"].astype(F32),
            )
        return add_ring(
            name,
            size,
            [name + route[1]],
            lambda r: [
                quarter(r)[step * rows_in : (step + 1) * rows_in] for step in range(deep)
            ],
        )

    def add_head(name, first, value):
        value = value.reshape(value.shape[0], 2, deep, 2, table_rows, width)
        add(name + "x", "x", 16, [], lambda r: value[:, 1], 0, first)
        nearer = once(name + "half", lambda r: value[:, 0] + r[name + "x"].astype(F32))
        last = add_ring(
            name, 4, [name + "x"], lambda r: [nearer(r)[:, step] for step in range(deep)]
        )
        add(name + "y", "y", 2, [name + "z" + str(deep - 1)], lambda r: last(r)[:, 1])
        return lambda r: last(r)[:, 0] + r[name + "y"].astype(F32)

    grad_head = [
        add_head(
            "head" + str(half),
            half,
            jnp.einsum(
                "kfv,fd->kvd",
                grad_logits[half * books // 2 : (half + 1) * books // 2],
                final,
                preferred_element_type=F32,
            ),
        )
        for half in range(2)
    ]

    grad, gain_final, shift_final = norm_back(
        residual_three, norm_params[6], norm_params[7], grad_final
    )
    grad = near(grad)

    rows_grad = spread(grad)
    grad_uppers, total = [], 0.0
    for up, back, upper in zip(weight_expand, weight_shrink, uppers):
        grad_active = product(rows_grad, back)
        grad_upper = jax.vjp(exact_gelu, upper)[1](grad_active)[0].astype(BF16)
        total = total + across(grad_upper, up)
        grad_uppers.append(grad_upper)
    grad_normed = collect(total)
    grad_expand = add_rows(
        "expand", 2, "yxz", 1, *(down(normed_three, part) for part in grad_uppers)
    )
    grad_shrink = add_rows("shrink", 2, "yxz", 2, *(down(rows_grad, active) for active in actives))
    change, gain_three, shift_three = norm_back(residual_two, gains[4], gains[5], grad_normed)
    grad = grad + change

    rows_grad = spread(grad)
    grads, total = [], 0.0
    for weight, parts, mixed in zip(weight_cross, cross_parts, cross_mixed):
        grad_mixed = product(rows_grad, weight[:, triple:]).astype(BF16)
        grad_q, grad_k, grad_v = attend_back(*parts, grad_mixed, False)
        total = total + across(grad_q, weight[:, :cols_in])
        grads.append(
            jnp.concatenate(
                [
                    down(normed_two, grad_q),
                    down(memory, grad_k),
                    down(memory, grad_v),
                    down(rows_grad, mixed),
                ],
                1,
            )
        )
    grad_normed = collect(total)
    grad_cross = add_rows("cross", 2, "xyz", 2, *grads)
    change, gain_two, shift_two = norm_back(residual_one, gains[2], gains[3], grad_normed)
    grad = grad + change

    rows_grad = spread(grad)
    grads, total = [], 0.0
    for weight, parts, mixed in zip(weight_self, self_parts, self_mixed):
        grad_mixed = product(rows_grad, weight[:, triple:]).astype(BF16)
        grad_heads = jnp.concatenate(attend_back(*parts, grad_mixed, True), 1)
        total = total + across(grad_heads, weight[:, :triple])
        grads.append(
            jnp.concatenate([down(normed_one, grad_heads), down(rows_grad, mixed)], 1)
        )
    grad_normed = collect(total)
    change, gain_one, shift_one = norm_back(residual, gains[0], gains[1], grad_normed)
    grad_self = add_rows("self", 2, "yxz", 4, *grads)
    grad = true(grad + change)

    rows_grad = grad.astype(BF16)

    def add_table():
        add("rows", "x", 8, [], lambda r: rows_grad, 0, 4)

        def spread_out(rows):
            return placed(grid.ring(rows, "c"), "c").reshape(frames, width)

        own_rows = spread_out(rows_grad)
        other_rows = once("rows", lambda r: spread_out(r["rows"]))
        halves = []
        for half in range(2):
            name = "table" + str(half)
            part = slice(half * books // 2, (half + 1) * books // 2)

            def value(r, part=part):
                result = 0.0
                for codes, rows in ((codes_own, own_rows), (codes_other, other_rows(r))):
                    result = result + jnp.einsum(
                        "kfv,fd->kvd", hot(codes[part]), rows, preferred_element_type=F32
                    )
                return result.reshape(-1, deep, 2, table_rows, width)

            value = once(name + "value", value)
            add(name + "y", "y", 8, ["rows"], lambda r, v=value: v(r)[:, :, 1], half)
            both = once(
                name + "both",
                lambda r, v=value, n=name: v(r)[:, :, 0] + r[n + "y"].astype(F32),
            )
            halves.append(
                add_ring(
                    name,
                    2,
                    [name + "y"],
                    lambda r, b=both: [b(r)[:, -step % deep] for step in range(deep)],
                )
            )
        return halves

    grad_table = add_table()
    ranks = ["rows", "self", "table", "cross", "expand", "shrink", "head"]
    tasks = {
        name: tasks[name]
        for rank in ranks
        for name in tasks
        if name.startswith(rank)
    }
    results = grid.rounds(tasks, BACK_BUDGET)
    grad_head = jnp.concatenate([part(results) for part in grad_head], 0)
    grad_table = jnp.concatenate([part(results) for part in grad_table], 0)
    grad_self, grad_cross = grad_self(results), grad_cross(results)
    grad_expand, grad_shrink = grad_expand(results), grad_shrink(results)

    norm_grads = [gain_one, shift_one, gain_two, shift_two, gain_three, shift_three]
    norm_grads = jnp.take(
        jnp.stack(norm_grads, 0).reshape(6, groups, -1), order_true, axis=1
    ).reshape(6, width)
    norm_grads = jnp.concatenate([norm_grads, gain_final[None], shift_final[None]], 0)
    loss_row = jnp.full((8, width), loss_local)
    norm_grads = after(jnp.concatenate([norm_grads, loss_row], 0), results["table1y"])
    summed = grid.total(norm_grads, ("c", "y", "x"))
    summed = grid.total(after(summed, grad_self), ("z",))
    grad_norm, loss_sum = summed[:8], summed[8, 0]

    def columns(array, first, count):
        return [
            array[:, (first + step) * cols_in : (first + step + 1) * cols_in]
            for step in range(count)
        ]

    grad_in = jnp.stack(columns(grad_self, 0, 3) + columns(grad_cross, 0, 3), 0)
    grad_out = jnp.stack([columns(grad_self, 3, 1)[0].T, columns(grad_cross, 3, 1)[0].T], 0)
    next_in = MOMENTUM * attend_in_momentum.transpose(1, 0, 2) + grad_in
    next_out = MOMENTUM * attend_out_momentum + grad_out
    next_expand = MOMENTUM * expand_momentum + grad_expand
    next_shrink = MOMENTUM * shrink_momentum + grad_shrink.T

    stack_rows = min(128, cols_in)
    data_blocks = jnp.concatenate(
        [next_out.reshape(-1, stack_rows, cols_out), next_shrink.reshape(-1, stack_rows, cols_out)],
        0,
    )
    tensor_grams = jnp.concatenate([folded_gram(next_in), folded_gram(next_expand[None])], 0)
    tensor_factor = newton(grid.total(tensor_grams, ("c", "y")))
    data_factor = newton(grid.total(folded_gram(data_blocks), ("x", "z")))
    ortho_in = orthogonal(tensor_factor[:members], next_in)
    ortho_expand = orthogonal(tensor_factor[members:], next_expand[None])[0]
    ortho_data = orthogonal(data_factor, data_blocks)
    count_out = next_out.size // (stack_rows * cols_out)
    ortho_out = ortho_data[:count_out].reshape(next_out.shape)
    ortho_shrink = ortho_data[count_out:].reshape(next_shrink.shape)
    attend_in_new = (turned_in * (1.0 - 0.5 * DECAY) - 0.5 * ortho_in).transpose(1, 0, 2)
    attend_out_new = attend_out * (1.0 - 1.0 * DECAY) - 1.0 * ortho_out
    expand_new = expand_weights * (1.0 - 0.5 * DECAY) - 0.5 * ortho_expand
    shrink_new = shrink_weights * (1.0 - 0.5 * DECAY) - 0.5 * ortho_shrink
    embed_new, embed_first_new, embed_second_new = adam(
        embed_table, embed_first, embed_second, grad_table, 0.1, DECAY
    )
    head_new, head_first_new, head_second_new = adam(
        head_table, head_first, head_second, grad_head, 0.03, DECAY
    )
    norm_new, norm_first_new, norm_second_new = adam(
        norm_params, norm_first, norm_second, grad_norm, 0.5, 0.0
    )
    return (
        loss_sum,
        token_count,
        attend_in_new,
        attend_out_new,
        expand_new,
        shrink_new,
        next_in.transpose(1, 0, 2),
        next_out,
        next_expand,
        next_shrink,
        embed_new,
        head_new,
        norm_new,
        embed_first_new,
        embed_second_new,
        head_first_new,
        head_second_new,
        norm_first_new,
        norm_second_new,
    )


def solution(mesh):
    n_dp, n_tensor = mesh.shape["dp"], mesh.shape["tensor"]
    sizes = {"z": n_dp // 2, "x": 2, "y": 2, "c": n_tensor // 2}
    cut = Mesh(mesh.devices.reshape(tuple(sizes.values())), tuple(sizes))
    dp, tensor = ("z", "x"), ("y", "c")
    table = P(None, dp + tensor, None)
    matrices = (P(dp, None, tensor), P(None, tensor, dp), P(dp, tensor), P(tensor, dp))
    return jax.shard_map(
        lambda *args: body(Grid(sizes), *args),
        mesh=cut,
        in_specs=(P(dp, tensor, None),) * 3
        + (P(), P(dp, None))
        + matrices * 2
        + (table, table, P())
        + (table,) * 4
        + (P(), P()),
        out_specs=(P(), P())
        + matrices * 2
        + (table, table, P())
        + (table,) * 4
        + (P(), P()),
        check_vma=False,
    )
```

```python
import functools
import math

import jax
import jax.numpy as jnp
from jax import lax
from jax.experimental import pallas as pl
from jax.experimental.pallas import tpu as pltpu
from jax.sharding import Mesh
from jax.sharding import PartitionSpec as P

HEAD_DIM = 64
MUON_ROWS = 32
STEP = 10

HIGHEST = lax.Precision.HIGHEST
NEWTON = (3.4445, -4.775, 2.0315)
BETA_ONE = 0.9
BETA_TWO = 0.95
ADAM_EPS = 1e-08
DECAY = 0.01
MOMENTUM = 0.95
BF16 = jnp.bfloat16
F32 = jnp.float32
LANES = 128
BUDGET = 8
BACK_BUDGET = 16
KERNEL_VMEM = 48 * 1024 * 1024


def layer_norm(values, gain, shift):
    centred = values - jnp.mean(values, -1, keepdims=True)
    variance = jnp.mean(centred * centred, -1, keepdims=True)
    return centred * lax.rsqrt(variance + 1e-05) * gain + shift


def norm_back(values, gain, shift, grad):
    result, backward = jax.vjp(layer_norm, values, gain, shift)
    return backward(grad)


def exact_gelu(values):
    return jax.nn.gelu(values, approximate=False)


def sinusoid(first, length, width):
    half = width // 2
    rates = jnp.exp(jnp.arange(half, dtype=jnp.float32) * (-math.log(10000.0) / half))
    places = (first + jnp.arange(length, dtype=jnp.int32)).astype(jnp.float32)
    angles = places[:, None] * rates[None, :]
    return jnp.concatenate([jnp.sin(angles), jnp.cos(angles)], -1)


def adam(weight, first, second, gradient, rate, decay):
    first = BETA_ONE * first + (1.0 - BETA_ONE) * gradient
    second = BETA_TWO * second + (1.0 - BETA_TWO) * gradient * gradient
    direction = (
        first / (1.0 - BETA_ONE**STEP) / (jnp.sqrt(second / (1.0 - BETA_TWO**STEP)) + ADAM_EPS)
    )
    return (weight - rate * (direction + decay * weight), first, second)


class Grid:
    def __init__(self, sizes):
        self.sizes = sizes

    def index(self, axis):
        return lax.axis_index(axis)

    def rotate(self, value, axis, step=1):
        size = self.sizes[axis]
        return lax.ppermute(value, axis, [(i, (i + step) % size) for i in range(size)])

    def swap(self, value, axis, step=1):
        return lax.ppermute(value, axis, [(i, i ^ step) for i in range(self.sizes[axis])])

    def total(self, value, axes):
        for axis in axes:
            step = 1
            while step < self.sizes[axis]:
                value = value + lax.ppermute(
                    value, axis, [(i, i ^ step) for i in range(self.sizes[axis])]
                )
                step *= 2
        return value

    def ring(self, shard, axis):
        held = [shard]
        for _ in range(1, self.sizes[axis]):
            held.append(self.rotate(held[-1], axis))
        return [held[-r % self.sizes[axis]] for r in range(self.sizes[axis])]

    def ring_sum(self, parts, axis):
        size = self.sizes[axis]
        running = parts[size - 1]
        for step in range(1, size):
            arrived = self.rotate(running.astype(BF16), axis)
            running = arrived.astype(F32) + parts[size - 1 - step].astype(F32)
        return running

    def rounds(self, tasks, budget, early=None, pack=True):
        done, results, last, sent, when = {}, {}, [], [], 0

        def unpack(lists, arrived):
            start = 0
            for name, value in lists:
                results[name] = arrived
                if len(lists) > 1:
                    rows = value.size // value.shape[-1]
                    results[name] = arrived[start : start + rows].reshape(value.shape)
                    start += rows

        waiting = list(tasks)
        while waiting:
            used, picked = {}, []
            for name in waiting:
                axis, size, needs, between, first, _ = tasks[name]
                ready = when >= first and all(
                    done.get(need, when) + between < when for need in needs
                )
                load = used.get(axis[0], 0)
                if ready and (load == 0 or load + size <= budget):
                    used[axis[0]] = load + size
                    picked.append(name)
            tokens = (early or {}).get(when)
            if tokens and last:
                last = lax.optimization_barrier((last, tokens))[0]
                for (_, lists), arrived in zip(sent, last):
                    unpack(lists, arrived)
            messages = {}
            for name in picked:
                value = tasks[name][-1](results)
                key = (tasks[name][0], value.shape[-1], value.dtype if pack else name)
                messages.setdefault(key, []).append((name, value))
            if messages:
                values = [
                    lists[0][1]
                    if len(lists) == 1
                    else jnp.concatenate([value.reshape(-1, key[1]) for _, value in lists], 0)
                    for key, lists in messages.items()
                ]
                tied = lax.optimization_barrier((values, last))[0]
                last, sent = [], list(messages.items())
                for ((axis, _, _), lists), value in zip(sent, tied):
                    if axis[0] == "z":
                        last.append(self.rotate(value, "z", int(axis[1:] or 1)))
                    else:
                        last.append(self.swap(value, axis))
                    unpack(lists, last[-1])
                    for name, _ in lists:
                        done[name] = when
            waiting = [name for name in waiting if name not in picked]
            when += 1
        return results


def chosen(array, index, axis):
    return lax.dynamic_index_in_dim(array, index, axis, keepdims=False)


def move_blocks(array, order):
    rows, cols = array.shape
    count = order.shape[0]
    block = cols // count
    if block % LANES or rows % 16:
        return jnp.take(array.reshape(rows, count, block), order, axis=1).reshape(rows, cols)

    def kernel(order_ref, from_ref, to_ref):
        for p in range(count):
            start = pl.multiple_of(order_ref[p] * block, LANES)
            to_ref[:, p * block : (p + 1) * block] = from_ref[:, pl.ds(start, block)]

    step = min(rows, 128)
    return pl.pallas_call(
        kernel,
        grid_spec=pltpu.PrefetchScalarGridSpec(
            num_scalar_prefetch=1,
            grid=(rows // step,),
            in_specs=[pl.BlockSpec((step, cols), lambda p, order: (p, 0))],
            out_specs=pl.BlockSpec((step, cols), lambda p, order: (p, 0)),
        ),
        out_shape=jax.ShapeDtypeStruct(array.shape, array.dtype),
        cost_estimate=pl.CostEstimate(
            flops=0, bytes_accessed=2 * array.size * array.dtype.itemsize, transcendentals=0
        ),
    )(order, array)


def arranged(blocks, order):
    count, books, rows, cols = blocks.shape
    if rows % 16:
        return jnp.take(blocks, order, axis=0).transpose(1, 0, 2, 3)

    def kernel(order_ref, from_ref, to_ref):
        to_ref[...] = from_ref[...].reshape(to_ref.shape)

    return pl.pallas_call(
        kernel,
        grid_spec=pltpu.PrefetchScalarGridSpec(
            num_scalar_prefetch=1,
            grid=(count,),
            in_specs=[pl.BlockSpec((1, books, rows, cols), lambda p, order: (order[p], 0, 0, 0))],
            out_specs=pl.BlockSpec((books, 1, rows, cols), lambda p, order: (0, p, 0, 0)),
        ),
        out_shape=jax.ShapeDtypeStruct((books, count, rows, cols), blocks.dtype),
        cost_estimate=pl.CostEstimate(
            flops=0, bytes_accessed=2 * blocks.size * blocks.dtype.itemsize, transcendentals=0
        ),
    )(order, blocks)


def after(value, token):
    return lax.optimization_barrier((value, token))[0]


def contract(left, right, left_dim, right_dim):
    return lax.dot_general(
        left, right, (((left_dim,), (right_dim,)), ((), ())), preferred_element_type=F32
    )


def contract_rows(left, right):
    return contract(left, right, 1, 0)


def spans(frames, keys, causal):
    block = min(256 if causal else 512, frames)
    return [
        (first, block, min(keys, first + block) if causal else keys)
        for first in range(0, frames, block)
    ]


def softmax_down(query, key_rows, first, causal):
    scores = contract(key_rows, query, 1, 1) * 0.125
    if causal:
        key_at = lax.broadcasted_iota(jnp.int32, scores.shape, 0)
        query_at = first + lax.broadcasted_iota(jnp.int32, scores.shape, 1)
        scores = jnp.where(key_at <= query_at, scores, -jnp.inf)
    expo = jnp.exp(scores - jnp.max(scores, 0, keepdims=True))
    return expo * (1.0 / jnp.sum(expo, 0, keepdims=True))


def head_lanes(shape, head):
    lane = lax.broadcasted_iota(jnp.int32, shape, 1)
    return (lane // HEAD_DIM) == head


def attend_kernel(causal, query_ref, key_ref, value_ref, mixed_ref):
    frames, keys = query_ref.shape[0], key_ref.shape[0]
    turned = value_ref[...].astype(F32).T.astype(BF16)
    for first, block, last in spans(frames, keys, causal):
        query = query_ref[pl.ds(first, block), :]
        parts = []
        for head in range(LANES // HEAD_DIM):
            own = jnp.where(head_lanes(query.shape, head), query, jnp.zeros_like(query))
            probs = softmax_down(own, key_ref[pl.ds(0, last), :], first, causal).astype(BF16)
            parts.append(
                contract_rows(
                    turned[head * HEAD_DIM : (head + 1) * HEAD_DIM, :last],
                    probs,
                )
            )
        mixed_ref[pl.ds(first, block), :] = jnp.concatenate(parts, 0).T.astype(BF16)


def attend_back_kernel(
    causal,
    query_ref,
    key_ref,
    value_ref,
    grad_ref,
    grad_query_ref,
    grad_key_ref,
    grad_value_ref,
    key_sum,
    value_sum,
):
    frames, keys = query_ref.shape[0], key_ref.shape[0]
    turned = key_ref[...].astype(F32).T.astype(BF16)
    key_sum[...] = jnp.zeros_like(key_sum)
    value_sum[...] = jnp.zeros_like(value_sum)
    for first, block, last in spans(frames, keys, causal):
        query = query_ref[pl.ds(first, block), :]
        grad = grad_ref[pl.ds(first, block), :]
        parts = []
        for head in range(LANES // HEAD_DIM):
            lanes = head_lanes(query.shape, head)
            own = jnp.where(lanes, query, jnp.zeros_like(query))
            own_grad = jnp.where(lanes, grad, jnp.zeros_like(grad))
            probs = softmax_down(own, key_ref[pl.ds(0, last), :], first, causal)
            grad_probs = contract(value_ref[pl.ds(0, last), :], own_grad, 1, 1)
            product = probs * grad_probs
            grad_scores = (product - probs * jnp.sum(product, 0, keepdims=True)).astype(BF16)
            value_sum[pl.ds(0, last), :] += contract_rows(probs.astype(BF16), own_grad)
            key_sum[pl.ds(0, last), :] += contract_rows(grad_scores, own)
            parts.append(
                contract_rows(
                    turned[head * HEAD_DIM : (head + 1) * HEAD_DIM, :last],
                    grad_scores,
                )
            )
        grad_query_ref[pl.ds(first, block), :] = (jnp.concatenate(parts, 0).T * 0.125).astype(BF16)
    grad_key_ref[...] = (key_sum[...] * 0.125).astype(BF16)
    grad_value_ref[...] = value_sum[...].astype(BF16)


def attend(queries, keys, values, causal):
    frames, key_rows = queries[0].shape[0], keys[0].shape[0]
    count = queries[2]
    cost = 4 * frames * key_rows * LANES * count * 2

    def spec(rows, start):
        return pl.BlockSpec((rows, LANES), lambda p, start=start: (0, start + p))

    return pl.pallas_call(
        functools.partial(attend_kernel, causal),
        grid=(count,),
        in_specs=[
            spec(frames, queries[1]),
            spec(key_rows, keys[1]),
            spec(key_rows, values[1]),
        ],
        out_specs=spec(frames, 0),
        out_shape=jax.ShapeDtypeStruct((frames, count * LANES), BF16),
        compiler_params=pltpu.CompilerParams(vmem_limit_bytes=KERNEL_VMEM),
        cost_estimate=pl.CostEstimate(
            flops=cost, bytes_accessed=cost // 256, transcendentals=cost // 256
        ),
    )(queries[0], keys[0], values[0])


def attend_back(queries, keys, values, grad, causal):
    frames, key_rows = queries[0].shape[0], keys[0].shape[0]
    count = queries[2]
    cost = 10 * frames * key_rows * LANES * count * 2

    def spec(rows, start):
        return pl.BlockSpec((rows, LANES), lambda p, start=start: (0, start + p))

    wide = count * LANES
    return pl.pallas_call(
        functools.partial(attend_back_kernel, causal),
        grid=(count,),
        in_specs=[
            spec(frames, queries[1]),
            spec(key_rows, keys[1]),
            spec(key_rows, values[1]),
            spec(frames, 0),
        ],
        out_specs=[spec(frames, 0), spec(key_rows, 0), spec(key_rows, 0)],
        out_shape=[
            jax.ShapeDtypeStruct((frames, wide), BF16),
            jax.ShapeDtypeStruct((key_rows, wide), BF16),
            jax.ShapeDtypeStruct((key_rows, wide), BF16),
        ],
        scratch_shapes=[pltpu.VMEM((key_rows, LANES), F32), pltpu.VMEM((key_rows, LANES), F32)],
        compiler_params=pltpu.CompilerParams(vmem_limit_bytes=KERNEL_VMEM),
        cost_estimate=pl.CostEstimate(
            flops=cost, bytes_accessed=cost // 512, transcendentals=cost // 512
        ),
    )(queries[0], keys[0], values[0], grad)


def newton(grams):
    count, _, rows = grams.shape
    repeats = rows // MUON_ROWS
    band = jnp.arange(rows) // MUON_ROWS
    mask = band[:, None] == band[None, :]
    eye = jnp.eye(rows, dtype=F32)
    gram = jnp.where(mask, jnp.tile(grams, (1, repeats, 1)), 0.0)
    diagonal = jnp.sum(gram * eye, -1).reshape(count, repeats, MUON_ROWS)
    size = jnp.sqrt(jnp.sum(diagonal, -1, keepdims=True)) + 1e-07
    size = jnp.broadcast_to(size, diagonal.shape).reshape(count, rows, 1)
    gram = gram / (size * size)

    def times(left, right):
        return jnp.einsum("brs,bst->brt", left, right, precision=HIGHEST)

    factor = None
    for repeat in range(5):
        mixing = NEWTON[0] * eye + NEWTON[1] * gram + NEWTON[2] * times(gram, gram)
        factor = mixing if factor is None else times(mixing, factor)
        if repeat < 4:
            gram = times(mixing, times(gram, mixing))
    return factor / size


def folded_gram(part):
    count, rows, _ = part.shape
    gram = jnp.einsum("brc,bsc->brs", part, part, precision=HIGHEST)
    band = jnp.arange(rows) // MUON_ROWS
    gram = jnp.where(band[:, None] == band[None, :], gram, 0.0)
    return jnp.sum(gram.reshape(count, rows // MUON_ROWS, MUON_ROWS, rows), 1)


def orthogonal(factor, part):
    return jnp.einsum("brs,bsc->brc", factor, part, precision=HIGHEST)


def body(
    grid,
    codes_in,
    codes_out,
    pad_mask,
    text_table,
    text_index,
    attend_in,
    attend_out,
    expand_weights,
    shrink_weights,
    attend_in_momentum,
    attend_out_momentum,
    expand_momentum,
    shrink_momentum,
    embed_table,
    head_table,
    norm_params,
    embed_first,
    embed_second,
    head_first,
    head_second,
    norm_first,
    norm_second,
):
    sizes = grid.sizes
    at_z, at_x, at_y, at_c = (grid.index(axis) for axis in ("z", "x", "y", "c"))
    deep, inner = sizes["z"], sizes["c"]
    width = norm_params.shape[1]
    clips, frames_part, books = codes_in.shape
    frames = frames_part * 2 * inner
    own_frames = frames // inner
    rows_in, members, cols_in = attend_in.shape
    cols_out = attend_out.shape[2]
    table_rows = embed_table.shape[1]
    groups = deep * 2

    place = jnp.arange(groups)
    order_near = (place % deep + at_z) % deep * 2 + (place // deep + at_x) % 2
    order_true = (place % 2 + at_x) % 2 * deep + (place // 2 - at_z) % deep

    def near(array):
        return move_blocks(array, order_near)

    def true(array):
        return move_blocks(array, order_true)

    codes = jnp.stack([codes_in, codes_out, pad_mask], 0).transpose(0, 3, 1, 2)

    def placed(pieces, axis):
        full = jnp.zeros((len(pieces),) + pieces[0].shape, pieces[0].dtype)
        for step, piece in enumerate(pieces):
            full = lax.dynamic_update_index_in_dim(
                full, piece, (lax.axis_index(axis) + step) % len(pieces), 0
            )
        return full

    def all_along(piece, axis):
        size = sizes[axis]
        held = [piece]
        for _ in range(1, size):
            held.append(
                lax.ppermute(held[-1], axis, [(i, (i + 1) % size) for i in range(size)])
            )
        return placed([held[-step % size] for step in range(size)], axis)

    codes = all_along(codes, "c")

    def once(kept, name, make):
        def get(results):
            if name not in kept:
                kept[name] = make(results)
            return kept[name]

        return get

    made = {}

    def clip_codes(results):
        both = placed([codes, results["codesy"]], "y")
        both = both.transpose(2, 3, 4, 0, 1, 5).reshape(3, books, clips, frames)
        return chosen(both, at_y, 2), jnp.sum(both[2]), chosen(both[0], 1 - at_y, 1)

    clip_codes = once(made, "codes", clip_codes)

    def codes_sent(results):
        own, count, _ = clip_codes(results)
        return jnp.concatenate([own[0], jnp.full((books, frames), count)], 0)

    turned_in = attend_in.transpose(1, 0, 2)
    turned_out = attend_out.transpose(0, 2, 1)

    def side_by_side(parts):
        return jnp.concatenate([part.astype(BF16) for part in parts], 1)

    hidden = expand_weights.shape[1]
    shard_rows = [books * table_rows, rows_in, rows_in]
    shards = {
        "first": jnp.concatenate(
            [embed_table.astype(BF16).reshape(-1, width)]
            + [
                side_by_side(parts).reshape(-1, width)
                for parts in (
                    list(turned_in[:3]) + [turned_out[0]],
                    list(turned_in[3:]) + [turned_out[1]],
                )
            ],
            0,
        ),
        "feed": jnp.concatenate(
            [part.astype(BF16).reshape(-1, width) for part in (expand_weights, shrink_weights.T)], 0
        ),
    }
    attend_rows = (shards["first"].shape[0] - books * table_rows) // 2
    starts = {"embed": 0, "self": books * table_rows, "cross": books * table_rows + attend_rows}
    tasks = {}

    def arrived(results, group, step):
        return results[group + "z" + str(step)] if step else shards[group]

    def embed_piece(results, axis, step):
        if axis == "y":
            return results["embedy" + str(step)]
        rows = arrived(results, "first", step)[: starts["self"]]
        return rows.reshape(books, table_rows, width)

    def attend_piece(results, axis, step, part=None):
        if axis == "x":
            rows = results["attendx" + str(step)]
        else:
            rows = arrived(results, "first", step)[starts["self"] :]
        if part is not None:
            rows = rows[part * attend_rows : (part + 1) * attend_rows]
        return rows

    def near_part(results, part):
        order = [-spot % deep for spot in range(deep)]
        blocks = [
            attend_piece(results, axis, step, part).reshape(rows_in, -1)
            for axis in ("z", "x")
            for step in order
        ]
        return jnp.concatenate(blocks, 0)

    def add_ring_of(group, size, first):
        for step in range(1, deep):
            ahead = [group + "z" + str(step - 1)] if step > 1 else []
            tasks[group + "z" + str(step)] = (
                "z", size, ahead, 0, first, lambda r, k=step: arrived(r, group, k - 1)
            )

    add_ring_of("first", 8, 0)
    for step in range(deep):
        needs = ["firstz" + str(step)] if step else []
        tasks["embedy" + str(step)] = (
            "y", 4, needs, 0, 0, lambda r, k=step: embed_piece(r, "z", k)
        )
        tasks["attendx" + str(step)] = (
            "x", 4, needs, 0, 0, lambda r, k=step: attend_piece(r, "z", k)
        )
        tasks["selfy" + str(step)] = (
            "y", 4, ["attendx" + str(step)], 0, 0,
            lambda r, k=step: jnp.concatenate(
                [attend_piece(r, "z", k, 0), attend_piece(r, "x", k, 0)], 0
            ),
        )
    tasks["codesy"] = ("y", 0, [], 0, 1, lambda r: codes)
    tasks["codesx"] = ("x", 0, ["codesy"], 0, 2, codes_sent)

    def pair_count(results):
        count = clip_codes(results)[1] + results["codesx"][books, 0]
        return jnp.full((8, LANES), count)

    for step in range(1, deep):
        ahead = "codesx" if step == 1 else "countz" + str(step - 1)
        tasks["countz" + str(step)] = (
            "z", 0, [ahead], 0, 0,
            lambda r, k=step: pair_count(r) if k == 1 else r["countz" + str(k - 1)],
        )

    add_ring_of("feed", 4, deep - 1)
    tasks["rows"] = (
        "x", 8, ["embedy" + str(step) for step in range(deep)] + ["codesx"], 0, deep + 1,
        lambda r: embedded_of(r["codesx"][:books], table_of(r)),
    )
    tasks["crossy"] = (
        "y", 16, ["attendx" + str(step) for step in range(deep)], 0, deep + 1,
        lambda r: near_part(r, 1),
    )

    z_place = (at_z - jnp.arange(deep)) % deep
    y_place = jnp.stack([at_y, 1 - at_y])
    table_ids = ((z_place * 2 + at_x) * 2)[:, None] + y_place[None, :]
    table_ids = ((table_ids * inner + at_c)[:, :, None] * table_rows + jnp.arange(table_rows)).reshape(
        -1
    )
    beside_ids = ((z_place * 2)[:, None] + jnp.stack([at_x, 1 - at_x])[None, :]) * 2 + at_y
    beside_ids = (beside_ids * inner + at_c)[:, :, None] * table_rows + jnp.arange(table_rows)
    beside_ids = beside_ids.reshape(-1)
    kept_table = []

    def table_of(results):
        if not kept_table:
            pieces = []
            for step in range(deep):
                pieces += [embed_piece(results, "z", step), embed_piece(results, "y", step)]
            kept_table.append(jnp.concatenate(pieces, 1))
        return kept_table[0]

    def hot(codes):
        return (codes[..., None] == table_ids).astype(BF16)

    def embedded_of(codes, table):
        rows = jnp.einsum("kfv,kvd->fd", hot(codes), table, preferred_element_type=F32)
        rows = rows.reshape(inner, own_frames, width)
        rows = grid.ring_sum(
            [chosen(rows, (at_c + step) % inner, 0) for step in range(inner)], "c"
        )
        return rows.astype(BF16)

    results = grid.rounds(tasks, BUDGET, pack=False)
    clip, _, codes_beside = clip_codes(results)
    codes_own, next_codes, live = clip[0], clip[1], clip[2].astype(F32)
    codes_other = results["codesx"][:books]
    token_count = pair_count(results)[0, 0]
    for step in range(1, deep):
        token_count = token_count + results["countz" + str(step)][0, 0]
    token_count = token_count.astype(F32)
    own_part = embedded_of(codes_own, table_of(results)).astype(F32)
    embedded = own_part + results["rows"].astype(F32)
    residual = near(embedded + sinusoid(at_c * own_frames, own_frames, width))
    residual = after(
        residual, (results["crossy"], results["feedz" + str(deep - 1)], token_count)
    )

    far_self = [results["selfy" + str(-spot % deep)] for spot in range(deep)]
    far_self = [
        part[half * attend_rows : (half + 1) * attend_rows].reshape(rows_in, -1)
        for half in range(2)
        for part in far_self
    ]
    weight_self = [near_part(results, 0), jnp.concatenate(far_self, 0)]
    weight_cross = [near_part(results, 1), results["crossy"]]

    feed_rows = shards["feed"].shape[0] // 2
    halves = [
        jnp.concatenate(
            [
                arrived(results, "feed", -spot % deep)[part * feed_rows : (part + 1) * feed_rows]
                for spot in range(deep)
            ],
            0,
        )
        for part in range(2)
    ]
    up_half, back_half = after(halves, residual)
    up_far, back_far = grid.swap(up_half, "x"), grid.swap(back_half, "y")

    def feed_second(token):
        rows = up_half.shape[0]
        near_up, far_back = after((up_far, back_far), token)
        up = jnp.concatenate([up_half, near_up], 0)
        back = jnp.concatenate([back_half, far_back], 0)
        up_other, back_other = grid.swap(up, "y"), grid.swap(back, "x")
        backs = [
            jnp.concatenate([back_half, back_other[:rows]], 0),
            jnp.concatenate([far_back, back_other[rows:]], 0),
        ]
        ups = [up, up_other]
        return [
            [matrix.reshape(width, hidden) for matrix in pair] for pair in (ups, backs)
        ]

    head_shard = after(head_table.astype(BF16), results["embedy" + str(deep - 1)])
    head = lax.all_gather(head_shard, ("z", "x", "y"), axis=0)
    head_order = (order_near[:, None] * 2 + y_place[None, :]).reshape(-1)
    head = arranged(head, head_order).reshape(books, -1, width)
    head_ids = (head_order * inner + at_c)[:, None] * table_rows + jnp.arange(table_rows)
    head_ids = head_ids.reshape(-1)

    def spread(rows):
        return placed(grid.ring(rows.astype(BF16), "c"), "c").reshape(frames, width)

    def collect(partial_rows):
        parts = partial_rows.reshape(inner, own_frames, width)
        running = chosen(parts, (at_c + inner - 1) % inner, 0)
        for step in range(1, inner):
            arrived = grid.rotate(running, "c")
            running = arrived + chosen(parts, (at_c + inner - 1 - step) % inner, 0)
        return running

    def product(left, right):
        return contract(left, right, 1, 0)

    def across(left, right):
        return contract(left, right, 1, 1)

    def down(left, right):
        return contract(left, right, 0, 0)

    gains = jnp.take(norm_params.reshape(8, groups, -1), order_near, axis=1).reshape(8, width)
    memory = jnp.take(text_table, chosen(text_index, at_y, 0), axis=0)
    memory = near(memory)
    pairs = cols_in // LANES
    triple = 3 * cols_in

    normed_one = spread(layer_norm(residual, gains[0], gains[1]))
    self_parts, self_mixed, total = [], [], 0.0
    for weight in weight_self:
        heads = product(normed_one, weight[:, :triple]).astype(BF16)
        parts = [(heads, member * pairs, pairs) for member in range(3)]
        mixed = attend(*parts, True)
        total = total + across(mixed, weight[:, triple:])
        self_parts.append(parts)
        self_mixed.append(mixed)
    weight_expand, weight_shrink = feed_second(self_mixed[1])
    residual_one = residual + collect(after(total, (up_far, back_far)))

    normed_two = spread(layer_norm(residual_one, gains[2], gains[3]))
    cross_parts, cross_mixed, total = [], [], 0.0
    for weight in weight_cross:
        query = product(normed_two, weight[:, :cols_in]).astype(BF16)
        key_value = product(memory, weight[:, cols_in:triple]).astype(BF16)
        parts = [(query, 0, pairs), (key_value, 0, pairs), (key_value, pairs, pairs)]
        mixed = attend(*parts, False)
        total = total + across(mixed, weight[:, triple:])
        cross_parts.append(parts)
        cross_mixed.append(mixed)
    residual_two = after(
        residual_one + collect(total), (head, weight_expand[1], weight_shrink[1])
    )

    normed_three = spread(layer_norm(residual_two, gains[4], gains[5]))
    uppers, actives, total = [], [], 0.0
    for up, back in zip(weight_expand, weight_shrink):
        upper = product(normed_three, up)
        active = exact_gelu(upper).astype(BF16)
        total = total + across(active, back)
        uppers.append(upper)
        actives.append(active)
    residual_three = true(residual_two + collect(total))

    final = spread(layer_norm(residual_three, norm_params[6], norm_params[7]))
    logits = jnp.einsum("fd,kvd->kfv", final, head, preferred_element_type=F32)
    is_target = head_ids[None, None, :] == next_codes[:, :, None]
    row_max = jnp.max(logits, -1)
    picked = jnp.sum(jnp.where(is_target, logits, 0.0), -1)
    row_sum = jnp.sum(jnp.exp(logits - row_max[..., None]), -1)
    stats = grid.ring(jnp.stack([row_max, row_sum, picked], 0), "c")
    top = stats[0][0]
    for stat in stats[1:]:
        top = jnp.maximum(top, stat[0])
    row_sum = sum(stat[1] * jnp.exp(stat[0] - top) for stat in stats)
    picked = sum(stat[2] for stat in stats)
    log_total = top + jnp.log(row_sum)
    loss_local = jnp.where(at_c == 0, jnp.sum((log_total - picked) * live), 0.0)
    grad_logits = (
        (jnp.exp(logits - log_total[..., None]) - is_target.astype(F32))
        * (live / token_count)[..., None]
    ).astype(BF16)
    grad_final = collect(
        jnp.einsum("kfv,kvd->fd", grad_logits, head, preferred_element_type=F32)
    )
    tasks, sums = {}, {}

    def add(name, axis, size, needs, value, between=0, first=0):
        tasks[name] = (axis, size, needs, between, first, lambda r: value(r).astype(BF16))

    def add_ring(name, size, needs, parts, direct=False):
        if direct:
            for step in range(1, deep):
                add(
                    name + "z" + str(step), "z" + str(step), size, needs,
                    lambda r, k=step: parts(r)[k],
                )
            return once(
                sums,
                name + "far",
                lambda r: sum(
                    (r[name + "z" + str(step)].astype(F32) for step in range(1, deep)),
                    parts(r)[0].astype(F32),
                ),
            )
        get = once(sums, name + "0", lambda r: parts(r)[deep - 1])
        for step in range(1, deep):
            add(name + "z" + str(step), "z", size, needs, get)
            needs = [name + "z" + str(step)]
            get = once(
                sums,
                name + str(step),
                lambda r, n=needs[0], k=step: r[n].astype(F32) + parts(r)[deep - 1 - k].astype(F32),
            )
        return get

    def add_rows(name, size, route, first, own, other):
        half = width // 2
        if route[0] == "y":
            add(name + "y", "y", 8 * size, [], lambda r: other, 0, first)
            whole = once(sums, name + "sum", lambda r: own + r[name + "y"].astype(F32))
            add(name + "x", "x", 4 * size, [name + "y"], lambda r: whole(r)[half:])
            quarter = once(
                sums,
                name + "part", lambda r: whole(r)[:half] + r[name + "x"].astype(F32)
            )
        else:
            far = jnp.concatenate([own[half:].astype(BF16), other[half:].astype(BF16)], 0)
            add(name + "x", "x", 8 * size, [], lambda r: far, 0, first)
            add(
                name + "y",
                "y",
                4 * size,
                [name + "x"],
                lambda r: other[:half] + r[name + "x"][half:].astype(F32),
            )
            quarter = once(
                sums,
                name + "part",
                lambda r: own[:half]
                + r[name + "x"][:half].astype(F32)
                + r[name + "y"].astype(F32),
            )
        return quarter, [name + route[1]]

    def add_rest(name, size, parts, direct=False):
        whole = once(
            sums,
            name + "whole",
            lambda r: jnp.concatenate([quarter(r) for quarter, _ in parts], 1)
            if len(parts) > 1
            else parts[0][0](r),
        )
        return add_ring(
            name,
            size,
            [need for _, needs in parts for need in needs],
            lambda r: [
                whole(r)[step * rows_in : (step + 1) * rows_in] for step in range(deep)
            ],
            direct,
        )

    def add_head(name, route, value):
        value = value.reshape(value.shape[0], 2, deep, 2, table_rows, width)
        own, far = (value[:, 0], value[:, 1]) if route == "x" else (
            value[:, :, :, 0], value[:, :, :, 1]
        )
        add(name + route, route, 16, [], lambda r: far)
        nearer = once(sums, name + "half", lambda r: own + r[name + route].astype(F32))
        depth = 1 if route == "x" else 2
        last = add_ring(
            name,
            4,
            [name + route],
            lambda r: [
                lax.index_in_dim(nearer(r), step, depth, keepdims=False) for step in range(deep)
            ],
        )
        final_axis = "y" if route == "x" else "x"
        add(name + final_axis, final_axis, 2, [name + "z" + str(deep - 1)], lambda r: last(r)[:, 1])
        return lambda r: last(r)[:, 0] + r[name + final_axis].astype(F32)

    grad_head = [
        add_head(
            "head" + str(half),
            "xy"[half],
            jnp.einsum(
                "kfv,fd->kvd",
                grad_logits[half * books // 2 : (half + 1) * books // 2],
                final,
                preferred_element_type=F32,
            ),
        )
        for half in range(2)
    ]

    grad, gain_final, shift_final = norm_back(
        residual_three, norm_params[6], norm_params[7], grad_final
    )
    grad = near(grad)

    rows_grad = spread(grad)
    grad_uppers, total = [], 0.0
    for up, back, upper in zip(weight_expand, weight_shrink, uppers):
        grad_active = product(rows_grad, back)
        grad_upper = jax.vjp(exact_gelu, upper)[1](grad_active)[0].astype(BF16)
        total = total + across(grad_upper, up)
        grad_uppers.append(grad_upper)
    grad_normed = collect(total)
    grad_expand = add_rest(
        "expand",
        2,
        [add_rows("expand", 2, "yxz", 1, *(down(normed_three, part) for part in grad_uppers))],
    )
    grads_shrink = [down(rows_grad, active) for active in actives]
    grad_shrink = add_rest("shrink", 2, [add_rows("shrink", 2, "xyz", 1, *grads_shrink)])
    change, gain_three, shift_three = norm_back(residual_two, gains[4], gains[5], grad_normed)
    grad = grad + change

    rows_grad = spread(grad)
    grads, total = [], 0.0
    for weight, parts, mixed in zip(weight_cross, cross_parts, cross_mixed):
        grad_mixed = product(rows_grad, weight[:, triple:]).astype(BF16)
        grad_q, grad_k, grad_v = attend_back(*parts, grad_mixed, False)
        total = total + across(grad_q, weight[:, :cols_in])
        grads.append(
            jnp.concatenate(
                [
                    down(normed_two, grad_q),
                    down(memory, grad_k),
                    down(memory, grad_v),
                    down(rows_grad, mixed),
                ],
                1,
            )
        )
    grad_normed = collect(total)
    cut = grads[0].shape[1] // 2
    grad_cross = add_rest(
        "cross",
        2,
        [
            add_rows("cross0", 1, "yxz", 2, grads[0][:, :cut], grads[1][:, :cut]),
            add_rows("cross1", 1, "xyz", 2, grads[0][:, cut:], grads[1][:, cut:]),
        ],
    )
    early = {1: [rows_grad]}
    change, gain_two, shift_two = norm_back(residual_one, gains[2], gains[3], grad_normed)
    grad = grad + change

    rows_grad = spread(grad)
    grads, total = [], 0.0
    for weight, parts, mixed in zip(weight_self, self_parts, self_mixed):
        grad_mixed = product(rows_grad, weight[:, triple:]).astype(BF16)
        grad_heads = jnp.concatenate(attend_back(*parts, grad_mixed, True), 1)
        early[2] = [grad_heads]
        total = total + across(grad_heads, weight[:, :triple])
        grads.append(
            jnp.concatenate([down(normed_one, grad_heads), down(rows_grad, mixed)], 1)
        )
    grad_normed = collect(total)
    change, gain_one, shift_one = norm_back(residual, gains[0], gains[1], grad_normed)
    cut = grads[0].shape[1] // 2
    grad_self = add_rest(
        "self",
        2,
        [
            add_rows("self0", 1, "yxz", 3, grads[0][:, :cut], grads[1][:, :cut]),
            add_rows("self1", 1, "xyz", 3, grads[0][:, cut:], grads[1][:, cut:]),
        ],
        True,
    )
    grad = true(grad + change)

    rows_grad = grad.astype(BF16)
    early[3] = [rows_grad]

    def add_table():
        def spread_out(rows):
            return placed(grid.ring(rows, "c"), "c").reshape(frames, width)

        own_rows = spread_out(rows_grad)
        beside = [("x", "y", codes_other, table_ids), ("y", "x", codes_beside, beside_ids)]
        halves = []
        for half, (across_axis, sum_axis, codes_far, ids) in enumerate(beside):
            name = "table" + str(half)
            part = slice(half * books // 2, (half + 1) * books // 2)
            add("rows" + str(half), across_axis, 8, [], lambda r: rows_grad, 0, 4)
            far_rows = once(
                sums, "rows" + str(half), lambda r, k=half: spread_out(r["rows" + str(k)])
            )

            def value(r, part=part, far_rows=far_rows, codes_far=codes_far, ids=ids):
                result = 0.0
                for codes, rows in ((codes_own, own_rows), (codes_far, far_rows(r))):
                    places = (codes[part][..., None] == ids).astype(BF16)
                    result = result + jnp.einsum(
                        "kfv,fd->kvd", places, rows, preferred_element_type=F32
                    )
                return result.reshape(-1, deep, 2, table_rows, width)

            value = once(sums, name + "value", value)
            add(
                name + sum_axis, sum_axis, 8, ["rows" + str(half)],
                lambda r, v=value: v(r)[:, :, 1],
            )
            both = once(
                sums,
                name + "both",
                lambda r, v=value, n=name + sum_axis: v(r)[:, :, 0] + r[n].astype(F32),
            )
            halves.append(
                add_ring(
                    name,
                    2,
                    [name + sum_axis],
                    lambda r, b=both: [b(r)[:, -step % deep] for step in range(deep)],
                    True,
                )
            )
        return halves

    grad_table = add_table()
    norm_grads = [gain_one, shift_one, gain_two, shift_two, gain_three, shift_three]
    norm_grads = jnp.take(
        jnp.stack(norm_grads, 0).reshape(6, groups, -1), order_true, axis=1
    ).reshape(6, width)
    norm_grads = jnp.concatenate([norm_grads, gain_final[None], shift_final[None]], 0)
    loss_row = jnp.full((8, width), loss_local)
    norm_own = grid.total(jnp.concatenate([norm_grads, loss_row], 0), ("c",))
    tasks["normy"] = ("y", 0, [], 0, 3, lambda r: norm_own)
    tasks["normx"] = ("x", 0, ["normy"], 0, 4, lambda r: norm_own + r["normy"])
    norm_plane = once(sums, "norm", lambda r: norm_own + r["normy"] + r["normx"])
    for step in range(1, deep):
        tasks["normz" + str(step)] = ("z" + str(step), 0, ["normx"], 0, 0, norm_plane)
    ranks = ["self", "rows", "table", "cross", "expand", "shrink", "head", "norm"]
    tasks = {
        name: tasks[name]
        for rank in ranks
        for name in tasks
        if name.startswith(rank)
    }
    results = grid.rounds(tasks, BACK_BUDGET, early)
    grad_head = jnp.concatenate([part(results) for part in grad_head], 0)
    grad_table = jnp.concatenate([part(results) for part in grad_table], 0)
    grad_self, grad_cross = grad_self(results), grad_cross(results)
    grad_expand, grad_shrink = grad_expand(results), grad_shrink(results)
    summed = norm_plane(results)
    for step in range(1, deep):
        summed = summed + results["normz" + str(step)]
    grad_norm, loss_sum = summed[:8], summed[8, 0]

    def columns(array, first, count):
        return [
            array[:, (first + step) * cols_in : (first + step + 1) * cols_in]
            for step in range(count)
        ]

    stack_rows = min(128, cols_in)
    momentum_in = attend_in_momentum.transpose(1, 0, 2)

    def muon(tensor_parts, data_parts):
        tensor_factor = newton(
            grid.total(jnp.concatenate([folded_gram(part) for part in tensor_parts], 0), ("c", "y"))
        )
        blocks = [part.reshape(-1, stack_rows, cols_out) for part in data_parts]
        blocks = jnp.concatenate(blocks, 0)
        grams = grid.total(folded_gram(blocks), ("x", "z"))
        ortho = orthogonal(newton(grams), blocks)
        tensor_out, data_out, start = [], [], 0
        for part in tensor_parts:
            count = part.shape[0]
            tensor_out.append(orthogonal(tensor_factor[start : start + count], part))
            start += count
        start = 0
        for part in data_parts:
            count = part.size // (stack_rows * cols_out)
            data_out.append(ortho[start : start + count].reshape(part.shape))
            start += count
        return tensor_out, data_out

    next_cross = MOMENTUM * momentum_in[3:] + jnp.stack(columns(grad_cross, 0, 3), 0)
    next_expand = MOMENTUM * expand_momentum + grad_expand
    next_shrink = MOMENTUM * shrink_momentum + grad_shrink.T
    next_out_cross = MOMENTUM * attend_out_momentum[1] + columns(grad_cross, 3, 1)[0].T
    next_self = MOMENTUM * momentum_in[:3] + jnp.stack(columns(grad_self, 0, 3), 0)
    next_out_self = MOMENTUM * attend_out_momentum[0] + columns(grad_self, 3, 1)[0].T
    next_in = jnp.concatenate([next_self, next_cross], 0)
    next_out = jnp.stack([next_out_self, next_out_cross], 0)
    (ortho_in, ortho_expand), (ortho_out, ortho_shrink) = muon(
        [next_in, next_expand[None]], [next_out, next_shrink]
    )
    ortho_expand = ortho_expand[0]
    attend_in_new = (turned_in * (1.0 - 0.5 * DECAY) - 0.5 * ortho_in).transpose(1, 0, 2)
    attend_out_new = attend_out * (1.0 - 1.0 * DECAY) - 1.0 * ortho_out
    expand_new = expand_weights * (1.0 - 0.5 * DECAY) - 0.5 * ortho_expand
    shrink_new = shrink_weights * (1.0 - 0.5 * DECAY) - 0.5 * ortho_shrink
    embed_new, embed_first_new, embed_second_new = adam(
        embed_table, embed_first, embed_second, grad_table, 0.1, DECAY
    )
    head_new, head_first_new, head_second_new = adam(
        head_table, head_first, head_second, grad_head, 0.03, DECAY
    )
    norm_new, norm_first_new, norm_second_new = adam(
        norm_params, norm_first, norm_second, grad_norm, 0.5, 0.0
    )
    return (
        loss_sum,
        token_count,
        attend_in_new,
        attend_out_new,
        expand_new,
        shrink_new,
        next_in.transpose(1, 0, 2),
        next_out,
        next_expand,
        next_shrink,
        embed_new,
        head_new,
        norm_new,
        embed_first_new,
        embed_second_new,
        head_first_new,
        head_second_new,
        norm_first_new,
        norm_second_new,
    )


def solution(mesh):
    n_dp, n_tensor = mesh.shape["dp"], mesh.shape["tensor"]
    sizes = {"z": n_dp // 2, "x": 2, "y": 2, "c": n_tensor // 2}
    cut = Mesh(mesh.devices.reshape(tuple(sizes.values())), tuple(sizes))
    dp, tensor = ("z", "x"), ("y", "c")
    table = P(None, dp + tensor, None)
    matrices = (P(dp, None, tensor), P(None, tensor, dp), P(dp, tensor), P(tensor, dp))
    return jax.shard_map(
        lambda *args: body(Grid(sizes), *args),
        mesh=cut,
        in_specs=(P(dp, tensor, None),) * 3
        + (P(), P(dp, None))
        + matrices * 2
        + (table, table, P())
        + (table,) * 4
        + (P(), P()),
        out_specs=(P(), P())
        + matrices * 2
        + (table, table, P())
        + (table,) * 4
        + (P(), P()),
        check_vma=False,
    )
```

```python
import functools
import math

import jax
import jax.numpy as jnp
from jax import lax
from jax.experimental import pallas as pl
from jax.experimental.pallas import tpu as pltpu
from jax.sharding import Mesh
from jax.sharding import PartitionSpec as P

HEAD_DIM = 64
MUON_ROWS = 32
STEP = 10

HIGHEST = lax.Precision.HIGHEST
NEWTON = (3.4445, -4.775, 2.0315)
BETA_ONE = 0.9
BETA_TWO = 0.95
ADAM_EPS = 1e-08
DECAY = 0.01
MOMENTUM = 0.95
BF16 = jnp.bfloat16
F32 = jnp.float32
LANES = 128
BUDGET = 8
BACK_BUDGET = 16
KERNEL_VMEM = 48 * 1024 * 1024
LIGHT = pl.CostEstimate(flops=1024, bytes_accessed=1024, transcendentals=0)


def layer_norm(values, gain, shift):
    centred = values - jnp.mean(values, -1, keepdims=True)
    variance = jnp.mean(centred * centred, -1, keepdims=True)
    return centred * lax.rsqrt(variance + 1e-05) * gain + shift


def norm_back(values, gain, shift, grad):
    result, backward = jax.vjp(layer_norm, values, gain, shift)
    return backward(grad)


def gelu_and_slope(values):
    falling = jnp.exp(-0.5 * values * values)
    near = 1.0 / (1.0 + (0.3275911 * math.sqrt(0.5)) * jnp.abs(values))
    series = 1.061405429
    for weight in (-1.453152027, 1.421413741, -0.284496736, 0.254829592):
        series = series * near + weight
    tail = 0.5 * series * near * falling
    below = jnp.where(values >= 0.0, 1.0 - tail, tail)
    return values * below, below + values * falling * (1.0 / math.sqrt(2.0 * math.pi))


def sinusoid(first, length, width):
    half = width // 2
    rates = jnp.exp(jnp.arange(half, dtype=jnp.float32) * (-math.log(10000.0) / half))
    places = (first + jnp.arange(length, dtype=jnp.int32)).astype(jnp.float32)
    angles = places[:, None] * rates[None, :]
    return jnp.concatenate([jnp.sin(angles), jnp.cos(angles)], -1)


def adam(weight, first, second, gradient, rate, decay):
    first = BETA_ONE * first + (1.0 - BETA_ONE) * gradient
    second = BETA_TWO * second + (1.0 - BETA_TWO) * gradient * gradient
    direction = (
        first / (1.0 - BETA_ONE**STEP) / (jnp.sqrt(second / (1.0 - BETA_TWO**STEP)) + ADAM_EPS)
    )
    return (weight - rate * (direction + decay * weight), first, second)


class Grid:
    def __init__(self, sizes):
        self.sizes = sizes

    def index(self, axis):
        return lax.axis_index(axis)

    def rotate(self, value, axis, step=1):
        size = self.sizes[axis]
        return lax.ppermute(value, axis, [(i, (i + step) % size) for i in range(size)])

    def swap(self, value, axis, step=1):
        return lax.ppermute(value, axis, [(i, i ^ step) for i in range(self.sizes[axis])])

    def total(self, value, axes):
        for axis in axes:
            step = 1
            while step < self.sizes[axis]:
                value = value + lax.ppermute(
                    value, axis, [(i, i ^ step) for i in range(self.sizes[axis])]
                )
                step *= 2
        return value

    def ring(self, shard, axis):
        held = [shard]
        for _ in range(1, self.sizes[axis]):
            held.append(self.rotate(held[-1], axis))
        return [held[-r % self.sizes[axis]] for r in range(self.sizes[axis])]

    def ring_sum(self, parts, axis):
        size = self.sizes[axis]
        running = parts[size - 1]
        for step in range(1, size):
            arrived = self.rotate(running.astype(BF16), axis)
            running = arrived.astype(F32) + parts[size - 1 - step].astype(F32)
        return running

    def rounds(self, tasks, budget, early=None, pack=True):
        done, results, last, sent, when = {}, {}, [], [], 0

        def unpack(lists, arrived):
            start = 0
            for name, value in lists:
                results[name] = arrived
                if len(lists) > 1:
                    rows = value.size // value.shape[-1]
                    results[name] = arrived[start : start + rows].reshape(value.shape)
                    start += rows

        waiting = list(tasks)
        while waiting:
            used, picked = {}, []
            for name in waiting:
                axis, size, needs, between, first, _ = tasks[name]
                ready = when >= first and all(
                    done.get(need, when) + between < when for need in needs
                )
                load = used.get(axis[0], 0)
                if ready and (load == 0 or load + size <= budget):
                    used[axis[0]] = load + size
                    picked.append(name)
            tokens = (early or {}).get(when)
            if tokens and last:
                last = lax.optimization_barrier((last, tokens))[0]
                for (_, lists), arrived in zip(sent, last):
                    unpack(lists, arrived)
            messages = {}
            for name in picked:
                value = tasks[name][-1](results)
                key = (tasks[name][0], value.shape[-1], value.dtype if pack else name)
                messages.setdefault(key, []).append((name, value))
            if messages:
                values = [
                    lists[0][1]
                    if len(lists) == 1
                    else jnp.concatenate([value.reshape(-1, key[1]) for _, value in lists], 0)
                    for key, lists in messages.items()
                ]
                tied = lax.optimization_barrier((values, last))[0]
                last, sent = [], list(messages.items())
                for ((axis, _, _), lists), value in zip(sent, tied):
                    if axis[0] == "z":
                        last.append(self.rotate(value, "z", int(axis[1:] or 1)))
                    else:
                        last.append(self.swap(value, axis))
                    unpack(lists, last[-1])
                    for name, _ in lists:
                        done[name] = when
            waiting = [name for name in waiting if name not in picked]
            when += 1
        return results


def chosen(array, index, axis):
    return lax.dynamic_index_in_dim(array, index, axis, keepdims=False)


def move_blocks(array, order):
    rows, cols = array.shape
    count = order.shape[0]
    block = cols // count
    if block % LANES or rows % 16:
        return jnp.take(array.reshape(rows, count, block), order, axis=1).reshape(rows, cols)

    def kernel(order_ref, from_ref, to_ref):
        for p in range(count):
            start = pl.multiple_of(order_ref[p] * block, LANES)
            to_ref[:, p * block : (p + 1) * block] = from_ref[:, pl.ds(start, block)]

    step = min(rows, 128)
    return pl.pallas_call(
        kernel,
        grid_spec=pltpu.PrefetchScalarGridSpec(
            num_scalar_prefetch=1,
            grid=(rows // step,),
            in_specs=[pl.BlockSpec((step, cols), lambda p, order: (p, 0))],
            out_specs=pl.BlockSpec((step, cols), lambda p, order: (p, 0)),
        ),
        out_shape=jax.ShapeDtypeStruct(array.shape, array.dtype),
        cost_estimate=LIGHT,
    )(order, array)


def arranged(blocks, order):
    count, books, rows, cols = blocks.shape
    half = books // 2
    if rows % 16:
        whole = jnp.take(blocks, order, axis=0).transpose(1, 0, 2, 3)
        return whole[:half], whole[half:]

    def kernel(order_ref, from_ref, first_ref, second_ref):
        first_ref[...] = from_ref[:, :half].reshape(first_ref.shape)
        second_ref[...] = from_ref[:, half:].reshape(second_ref.shape)

    result = jax.ShapeDtypeStruct((half, count, rows, cols), blocks.dtype)
    spec = pl.BlockSpec((half, 1, rows, cols), lambda p, order: (0, p, 0, 0))
    return pl.pallas_call(
        kernel,
        grid_spec=pltpu.PrefetchScalarGridSpec(
            num_scalar_prefetch=1,
            grid=(count,),
            in_specs=[pl.BlockSpec((1, books, rows, cols), lambda p, order: (order[p], 0, 0, 0))],
            out_specs=[spec, spec],
        ),
        out_shape=[result, result],
        cost_estimate=LIGHT,
    )(order, blocks)


def after(value, token):
    return lax.optimization_barrier((value, token))[0]


def contract(left, right, left_dim, right_dim):
    return lax.dot_general(
        left, right, (((left_dim,), (right_dim,)), ((), ())), preferred_element_type=F32
    )


def contract_rows(left, right):
    return contract(left, right, 1, 0)


def spans(frames, keys, causal):
    block = min(256 if causal else 512, frames)
    return [
        (first, block, min(keys, first + block) if causal else keys)
        for first in range(0, frames, block)
    ]


def softmax_down(query, key_rows, first, causal):
    scores = contract(key_rows, query, 1, 1) * 0.125
    if causal:
        key_at = lax.broadcasted_iota(jnp.int32, scores.shape, 0)
        query_at = first + lax.broadcasted_iota(jnp.int32, scores.shape, 1)
        scores = jnp.where(key_at <= query_at, scores, -jnp.inf)
    expo = jnp.exp(scores - jnp.max(scores, 0, keepdims=True))
    return expo * (1.0 / jnp.sum(expo, 0, keepdims=True))


def head_lanes(shape, head):
    lane = lax.broadcasted_iota(jnp.int32, shape, 1)
    return (lane // HEAD_DIM) == head


def attend_kernel(causal, query_ref, key_ref, value_ref, mixed_ref):
    frames, keys = query_ref.shape[0], key_ref.shape[0]
    turned = value_ref[...].astype(F32).T.astype(BF16)
    for first, block, last in spans(frames, keys, causal):
        query = query_ref[pl.ds(first, block), :]
        parts = []
        for head in range(LANES // HEAD_DIM):
            own = jnp.where(head_lanes(query.shape, head), query, jnp.zeros_like(query))
            probs = softmax_down(own, key_ref[pl.ds(0, last), :], first, causal).astype(BF16)
            parts.append(
                contract_rows(
                    turned[head * HEAD_DIM : (head + 1) * HEAD_DIM, :last],
                    probs,
                )
            )
        mixed_ref[pl.ds(first, block), :] = jnp.concatenate(parts, 0).T.astype(BF16)


def attend_back_kernel(
    causal,
    query_ref,
    key_ref,
    value_ref,
    grad_ref,
    grad_query_ref,
    grad_key_ref,
    grad_value_ref,
    key_sum,
    value_sum,
):
    frames, keys = query_ref.shape[0], key_ref.shape[0]
    turned = key_ref[...].astype(F32).T.astype(BF16)
    key_sum[...] = jnp.zeros_like(key_sum)
    value_sum[...] = jnp.zeros_like(value_sum)
    for first, block, last in spans(frames, keys, causal):
        query = query_ref[pl.ds(first, block), :]
        grad = grad_ref[pl.ds(first, block), :]
        parts = []
        for head in range(LANES // HEAD_DIM):
            lanes = head_lanes(query.shape, head)
            own = jnp.where(lanes, query, jnp.zeros_like(query))
            own_grad = jnp.where(lanes, grad, jnp.zeros_like(grad))
            probs = softmax_down(own, key_ref[pl.ds(0, last), :], first, causal)
            grad_probs = contract(value_ref[pl.ds(0, last), :], own_grad, 1, 1)
            product = probs * grad_probs
            grad_scores = (product - probs * jnp.sum(product, 0, keepdims=True)).astype(BF16)
            value_sum[pl.ds(0, last), :] += contract_rows(probs.astype(BF16), own_grad)
            key_sum[pl.ds(0, last), :] += contract_rows(grad_scores, own)
            parts.append(
                contract_rows(
                    turned[head * HEAD_DIM : (head + 1) * HEAD_DIM, :last],
                    grad_scores,
                )
            )
        grad_query_ref[pl.ds(first, block), :] = (jnp.concatenate(parts, 0).T * 0.125).astype(BF16)
    grad_key_ref[...] = (key_sum[...] * 0.125).astype(BF16)
    grad_value_ref[...] = value_sum[...].astype(BF16)


def attend(queries, keys, values, causal):
    frames, key_rows = queries[0].shape[0], keys[0].shape[0]
    count = queries[2]

    def spec(rows, start):
        return pl.BlockSpec((rows, LANES), lambda p, start=start: (0, start + p))

    return pl.pallas_call(
        functools.partial(attend_kernel, causal),
        grid=(count,),
        in_specs=[
            spec(frames, queries[1]),
            spec(key_rows, keys[1]),
            spec(key_rows, values[1]),
        ],
        out_specs=spec(frames, 0),
        out_shape=jax.ShapeDtypeStruct((frames, count * LANES), BF16),
        compiler_params=pltpu.CompilerParams(vmem_limit_bytes=KERNEL_VMEM),
        cost_estimate=LIGHT,
    )(queries[0], keys[0], values[0])


def attend_back(queries, keys, values, grad, causal):
    frames, key_rows = queries[0].shape[0], keys[0].shape[0]
    count = queries[2]

    def spec(rows, start):
        return pl.BlockSpec((rows, LANES), lambda p, start=start: (0, start + p))

    wide = count * LANES
    return pl.pallas_call(
        functools.partial(attend_back_kernel, causal),
        grid=(count,),
        in_specs=[
            spec(frames, queries[1]),
            spec(key_rows, keys[1]),
            spec(key_rows, values[1]),
            spec(frames, 0),
        ],
        out_specs=[spec(frames, 0), spec(key_rows, 0), spec(key_rows, 0)],
        out_shape=[
            jax.ShapeDtypeStruct((frames, wide), BF16),
            jax.ShapeDtypeStruct((key_rows, wide), BF16),
            jax.ShapeDtypeStruct((key_rows, wide), BF16),
        ],
        scratch_shapes=[pltpu.VMEM((key_rows, LANES), F32), pltpu.VMEM((key_rows, LANES), F32)],
        compiler_params=pltpu.CompilerParams(vmem_limit_bytes=KERNEL_VMEM),
        cost_estimate=LIGHT,
    )(queries[0], keys[0], values[0], grad)


def newton(grams):
    count, _, rows = grams.shape
    repeats = rows // MUON_ROWS
    band = jnp.arange(rows) // MUON_ROWS
    mask = band[:, None] == band[None, :]
    eye = jnp.eye(rows, dtype=F32)
    gram = jnp.where(mask, jnp.tile(grams, (1, repeats, 1)), 0.0)
    diagonal = jnp.sum(gram * eye, -1).reshape(count, repeats, MUON_ROWS)
    size = jnp.sqrt(jnp.sum(diagonal, -1, keepdims=True)) + 1e-07
    size = jnp.broadcast_to(size, diagonal.shape).reshape(count, rows, 1)
    gram = gram / (size * size)

    def times(left, right):
        return jnp.einsum("brs,bst->brt", left, right, precision=HIGHEST)

    factor = None
    for repeat in range(5):
        mixing = NEWTON[0] * eye + NEWTON[1] * gram + NEWTON[2] * times(gram, gram)
        factor = mixing if factor is None else times(mixing, factor)
        if repeat < 4:
            gram = times(mixing, times(gram, mixing))
    return factor / size


def folded_gram(part):
    count, rows, _ = part.shape
    gram = jnp.einsum("brc,bsc->brs", part, part, precision=HIGHEST)
    band = jnp.arange(rows) // MUON_ROWS
    gram = jnp.where(band[:, None] == band[None, :], gram, 0.0)
    return jnp.sum(gram.reshape(count, rows // MUON_ROWS, MUON_ROWS, rows), 1)


def orthogonal(factor, part):
    return jnp.einsum("brs,bsc->brc", factor, part, precision=HIGHEST)


def body(
    grid,
    codes_in,
    codes_out,
    pad_mask,
    text_table,
    text_index,
    attend_in,
    attend_out,
    expand_weights,
    shrink_weights,
    attend_in_momentum,
    attend_out_momentum,
    expand_momentum,
    shrink_momentum,
    embed_table,
    head_table,
    norm_params,
    embed_first,
    embed_second,
    head_first,
    head_second,
    norm_first,
    norm_second,
):
    sizes = grid.sizes
    at_z, at_x, at_y, at_c = (grid.index(axis) for axis in ("z", "x", "y", "c"))
    deep, inner = sizes["z"], sizes["c"]
    width = norm_params.shape[1]
    clips, frames_part, books = codes_in.shape
    frames = frames_part * 2 * inner
    own_frames = frames // inner
    rows_in, members, cols_in = attend_in.shape
    cols_out = attend_out.shape[2]
    table_rows = embed_table.shape[1]
    groups = deep * 2

    place = jnp.arange(groups)
    order_near = (place % deep + at_z) % deep * 2 + (place // deep + at_x) % 2
    order_true = (place % 2 + at_x) % 2 * deep + (place // 2 - at_z) % deep

    def near(array):
        return move_blocks(array, order_near)

    def true(array):
        return move_blocks(array, order_true)

    codes = jnp.stack([codes_in, codes_out, pad_mask], 0).transpose(0, 3, 1, 2)

    def placed(pieces, axis):
        full = jnp.zeros((len(pieces),) + pieces[0].shape, pieces[0].dtype)
        for step, piece in enumerate(pieces):
            full = lax.dynamic_update_index_in_dim(
                full, piece, (lax.axis_index(axis) + step) % len(pieces), 0
            )
        return full

    def all_along(piece, axis):
        size = sizes[axis]
        held = [piece]
        for _ in range(1, size):
            held.append(
                lax.ppermute(held[-1], axis, [(i, (i + 1) % size) for i in range(size)])
            )
        return placed([held[-step % size] for step in range(size)], axis)

    codes = all_along(codes, "c")

    def once(kept, name, make):
        def get(results):
            if name not in kept:
                kept[name] = make(results)
            return kept[name]

        return get

    made = {}

    def clip_codes(results):
        both = placed([codes, results["codesy"]], "y")
        both = both.transpose(2, 3, 4, 0, 1, 5).reshape(3, books, clips, frames)
        return chosen(both, at_y, 2), jnp.sum(both[2]), chosen(both[0], 1 - at_y, 1)

    clip_codes = once(made, "codes", clip_codes)

    def codes_sent(results):
        own, count, _ = clip_codes(results)
        return jnp.concatenate([own[0], jnp.full((books, frames), count)], 0)

    turned_in = attend_in.transpose(1, 0, 2)
    turned_out = attend_out.transpose(0, 2, 1)

    def side_by_side(parts):
        return jnp.concatenate([part.astype(BF16) for part in parts], 1)

    hidden = expand_weights.shape[1]
    shard_rows = [books * table_rows, rows_in, rows_in]
    shards = {
        "first": jnp.concatenate(
            [embed_table.astype(BF16).reshape(-1, width)]
            + [
                side_by_side(parts).reshape(-1, width)
                for parts in (
                    list(turned_in[:3]) + [turned_out[0]],
                    list(turned_in[3:]) + [turned_out[1]],
                )
            ],
            0,
        ),
        "feed": jnp.concatenate(
            [part.astype(BF16).reshape(-1, width) for part in (expand_weights, shrink_weights.T)], 0
        ),
    }
    attend_rows = (shards["first"].shape[0] - books * table_rows) // 2
    starts = {"embed": 0, "self": books * table_rows, "cross": books * table_rows + attend_rows}
    tasks = {}

    def arrived(results, group, step):
        return results[group + "z" + str(step)] if step else shards[group]

    def embed_piece(results, axis, step):
        if axis == "y":
            return results["embedy" + str(step)]
        rows = arrived(results, "first", step)[: starts["self"]]
        return rows.reshape(books, table_rows, width)

    def attend_piece(results, axis, step, part=None):
        if axis == "x":
            rows = results["attendx" + str(step)]
        else:
            rows = arrived(results, "first", step)[starts["self"] :]
        if part is not None:
            rows = rows[part * attend_rows : (part + 1) * attend_rows]
        return rows

    def near_part(results, part):
        order = [-spot % deep for spot in range(deep)]
        blocks = [
            attend_piece(results, axis, step, part).reshape(rows_in, -1)
            for axis in ("z", "x")
            for step in order
        ]
        return jnp.concatenate(blocks, 0)

    def add_ring_of(group, size, first):
        for step in range(1, deep):
            ahead = [group + "z" + str(step - 1)] if step > 1 else []
            tasks[group + "z" + str(step)] = (
                "z", size, ahead, 0, first, lambda r, k=step: arrived(r, group, k - 1)
            )

    add_ring_of("first", 8, 0)
    for step in range(deep):
        needs = ["firstz" + str(step)] if step else []
        tasks["embedy" + str(step)] = (
            "y", 4, needs, 0, 0, lambda r, k=step: embed_piece(r, "z", k)
        )
        tasks["attendx" + str(step)] = (
            "x", 4, needs, 0, 0, lambda r, k=step: attend_piece(r, "z", k)
        )
        tasks["selfy" + str(step)] = (
            "y", 4, ["attendx" + str(step)], 0, 0,
            lambda r, k=step: jnp.concatenate(
                [attend_piece(r, "z", k, 0), attend_piece(r, "x", k, 0)], 0
            ),
        )
    tasks["codesy"] = ("y", 0, [], 0, 1, lambda r: codes)
    tasks["codesx"] = ("x", 0, ["codesy"], 0, 2, codes_sent)

    def pair_count(results):
        count = clip_codes(results)[1] + results["codesx"][books, 0]
        return jnp.full((8, LANES), count)

    steps = [1 << power for power in range((deep - 1).bit_length())]

    def counted(results, known):
        count = pair_count(results)
        for step in steps[:known]:
            count = count + results["count" + str(step)]
        return count

    for at, step in enumerate(steps):
        ahead = "count" + str(steps[at - 1]) if at else "codesx"
        tasks["count" + str(step)] = (
            "z" + str(step), 0, [ahead], 0, 0, lambda r, k=at: counted(r, k)
        )
    add_ring_of("feed", 4, deep - 1)
    tasks["rows"] = (
        "x", 8, ["embedy" + str(step) for step in range(deep)] + ["codesx"], 0, deep + 1,
        lambda r: embedded_of(r["codesx"][:books], table_of(r)),
    )
    tasks["crossy"] = (
        "y", 16, ["attendx" + str(step) for step in range(deep)], 0, deep + 1,
        lambda r: near_part(r, 1),
    )

    z_place = (at_z - jnp.arange(deep)) % deep
    y_place = jnp.stack([at_y, 1 - at_y])
    table_ids = ((z_place * 2 + at_x) * 2)[:, None] + y_place[None, :]
    table_ids = ((table_ids * inner + at_c)[:, :, None] * table_rows + jnp.arange(table_rows)).reshape(
        -1
    )
    beside_ids = ((z_place * 2)[:, None] + jnp.stack([at_x, 1 - at_x])[None, :]) * 2 + at_y
    beside_ids = (beside_ids * inner + at_c)[:, :, None] * table_rows + jnp.arange(table_rows)
    beside_ids = beside_ids.reshape(-1)
    kept_table = []

    def table_of(results):
        if not kept_table:
            pieces = []
            for step in range(deep):
                pieces += [embed_piece(results, "z", step), embed_piece(results, "y", step)]
            kept_table.append(jnp.concatenate(pieces, 1))
        return kept_table[0]

    def hot(codes):
        return (codes[..., None] == table_ids).astype(BF16)

    def embedded_of(codes, table):
        rows = jnp.einsum("kfv,kvd->fd", hot(codes), table, preferred_element_type=F32)
        rows = rows.reshape(inner, own_frames, width)
        rows = grid.ring_sum(
            [chosen(rows, (at_c + step) % inner, 0) for step in range(inner)], "c"
        )
        return rows.astype(BF16)

    results = grid.rounds(tasks, BUDGET, pack=False)
    clip, _, codes_beside = clip_codes(results)
    codes_own, next_codes, live = clip[0], clip[1], clip[2].astype(F32)
    codes_other = results["codesx"][:books]
    token_count = counted(results, len(steps))[0, 0].astype(F32)
    own_part = embedded_of(codes_own, table_of(results)).astype(F32)
    embedded = own_part + results["rows"].astype(F32)
    residual = near(embedded + sinusoid(at_c * own_frames, own_frames, width))
    residual = after(residual, token_count)

    far_self = [results["selfy" + str(-spot % deep)] for spot in range(deep)]
    far_self = [
        part[half * attend_rows : (half + 1) * attend_rows].reshape(rows_in, -1)
        for half in range(2)
        for part in far_self
    ]
    weight_self = [near_part(results, 0), jnp.concatenate(far_self, 0)]
    weight_cross = [near_part(results, 1), results["crossy"]]

    feed_rows = shards["feed"].shape[0] // 2
    halves = [
        jnp.concatenate(
            [
                arrived(results, "feed", -spot % deep)[part * feed_rows : (part + 1) * feed_rows]
                for spot in range(deep)
            ],
            0,
        )
        for part in range(2)
    ]
    up_half, back_half = after(halves, residual)
    up_far, back_far = grid.swap(up_half, "x"), grid.swap(back_half, "y")

    def feed_second(token):
        rows = up_half.shape[0]
        near_up, far_back = after((up_far, back_far), token)
        up = jnp.concatenate([up_half, near_up], 0)
        back = jnp.concatenate([back_half, far_back], 0)
        up_other, back_other = grid.swap(up, "y"), grid.swap(back, "x")
        backs = [
            jnp.concatenate([back_half, back_other[:rows]], 0),
            jnp.concatenate([far_back, back_other[rows:]], 0),
        ]
        ups = [up, up_other]
        return [
            [matrix.reshape(width, hidden) for matrix in pair] for pair in (ups, backs)
        ]

    head_shard = after(head_table.astype(BF16), results["rows"])
    head = lax.all_gather(head_shard, ("z", "x", "y"), axis=0)
    head_order = (order_near[:, None] * 2 + y_place[None, :]).reshape(-1)
    head = [part.reshape(books // 2, -1, width) for part in arranged(head, head_order)]
    head_ids = (head_order * inner + at_c)[:, None] * table_rows + jnp.arange(table_rows)
    head_ids = head_ids.reshape(-1)

    def spread(rows):
        return placed(grid.ring(rows.astype(BF16), "c"), "c").reshape(frames, width)

    def collect(partial_rows):
        parts = partial_rows.reshape(inner, own_frames, width)
        running = chosen(parts, (at_c + inner - 1) % inner, 0)
        for step in range(1, inner):
            arrived = grid.rotate(running, "c")
            running = arrived + chosen(parts, (at_c + inner - 1 - step) % inner, 0)
        return running

    def product(left, right):
        return contract(left, right, 1, 0)

    def across(left, right):
        return contract(left, right, 1, 1)

    def down(left, right):
        return contract(left, right, 0, 0)

    gains = jnp.take(norm_params.reshape(8, groups, -1), order_near, axis=1).reshape(8, width)
    memory = jnp.take(text_table, chosen(text_index, at_y, 0), axis=0)
    memory = near(memory)
    pairs = cols_in // LANES
    triple = 3 * cols_in

    normed_one = spread(layer_norm(residual, gains[0], gains[1]))
    self_parts, self_mixed, total = [], [], 0.0
    for weight in weight_self:
        heads = product(normed_one, weight[:, :triple]).astype(BF16)
        parts = [(heads, member * pairs, pairs) for member in range(3)]
        mixed = attend(*parts, True)
        total = total + across(mixed, weight[:, triple:])
        self_parts.append(parts)
        self_mixed.append(mixed)
    total = after(total, (results["crossy"], results["feedz" + str(deep - 1)]))
    residual_one = residual + collect(total)

    normed_two = spread(layer_norm(residual_one, gains[2], gains[3]))
    cross_parts, cross_mixed, total = [], [], 0.0
    for weight in weight_cross:
        query = product(normed_two, weight[:, :cols_in]).astype(BF16)
        key_value = product(memory, weight[:, cols_in:triple]).astype(BF16)
        parts = [(query, 0, pairs), (key_value, 0, pairs), (key_value, pairs, pairs)]
        mixed = attend(*parts, False)
        total = total + across(mixed, weight[:, triple:])
        cross_parts.append(parts)
        cross_mixed.append(mixed)
    weight_expand, weight_shrink = feed_second(cross_mixed[0])
    total = after(total, (up_far, back_far))
    residual_two = after(
        residual_one + collect(total), (head, weight_expand[1], weight_shrink[1])
    )

    normed_three = spread(layer_norm(residual_two, gains[4], gains[5]))
    slopes, actives, total = [], [], 0.0
    for up, back in zip(weight_expand, weight_shrink):
        active, slope = gelu_and_slope(product(normed_three, up))
        active, slope = lax.optimization_barrier((active.astype(BF16), slope))
        total = total + across(active, back)
        slopes.append(slope)
        actives.append(active)
    residual_three = true(residual_two + collect(total))

    final = spread(layer_norm(residual_three, norm_params[6], norm_params[7]))
    logits, targets, stats = [], [], []
    for half, part in enumerate(head):
        wanted = next_codes[half * books // 2 : (half + 1) * books // 2]
        values = jnp.einsum("fd,kvd->kfv", final, part, preferred_element_type=F32)
        is_target = head_ids[None, None, :] == wanted[:, :, None]
        row_max = jnp.max(values, -1)
        picked = jnp.sum(jnp.where(is_target, values, 0.0), -1)
        row_sum = jnp.sum(jnp.exp(values - row_max[..., None]), -1)
        logits.append(values)
        targets.append(is_target)
        stats.append(jnp.stack([row_max, row_sum, picked], 0))
    stats = grid.ring(jnp.concatenate(stats, 1), "c")
    top = stats[0][0]
    for stat in stats[1:]:
        top = jnp.maximum(top, stat[0])
    row_sum = sum(stat[1] * jnp.exp(stat[0] - top) for stat in stats)
    picked = sum(stat[2] for stat in stats)
    log_total = top + jnp.log(row_sum)
    loss_local = jnp.where(at_c == 0, jnp.sum((log_total - picked) * live), 0.0)
    share = live / token_count
    grad_logits = []
    for half in range(2):
        part = slice(half * books // 2, (half + 1) * books // 2)
        grad_part = jnp.exp(logits[half] - log_total[part][..., None]) - targets[half].astype(F32)
        grad_logits.append((grad_part * share[part][..., None]).astype(BF16))
    grad_logits = lax.optimization_barrier(grad_logits)
    grad_final = collect(
        sum(
            jnp.einsum("kfv,kvd->fd", values, part, preferred_element_type=F32)
            for values, part in zip(grad_logits, head)
        )
    )
    tasks, sums = {}, {}

    def add(name, axis, size, needs, value, between=0, first=0):
        tasks[name] = (axis, size, needs, between, first, lambda r: value(r).astype(BF16))

    def add_ring(name, size, needs, parts, direct=False):
        if direct:
            for step in range(1, deep):
                add(
                    name + "z" + str(step), "z" + str(step), size, needs,
                    lambda r, k=step: parts(r)[k],
                )
            return once(
                sums,
                name + "far",
                lambda r: sum(
                    (r[name + "z" + str(step)].astype(F32) for step in range(1, deep)),
                    parts(r)[0].astype(F32),
                ),
            )
        get = once(sums, name + "0", lambda r: parts(r)[deep - 1])
        for step in range(1, deep):
            add(name + "z" + str(step), "z", size, needs, get)
            needs = [name + "z" + str(step)]
            get = once(
                sums,
                name + str(step),
                lambda r, n=needs[0], k=step: r[n].astype(F32) + parts(r)[deep - 1 - k].astype(F32),
            )
        return get

    def add_rows(name, size, route, first, own, other):
        half = width // 2
        if route[0] == "y":
            add(name + "y", "y", 8 * size, [], lambda r: other, 0, first)
            whole = once(sums, name + "sum", lambda r: own + r[name + "y"].astype(F32))
            add(name + "x", "x", 4 * size, [name + "y"], lambda r: whole(r)[half:])
            quarter = once(
                sums,
                name + "part", lambda r: whole(r)[:half] + r[name + "x"].astype(F32)
            )
        else:
            far = jnp.concatenate([own[half:].astype(BF16), other[half:].astype(BF16)], 0)
            add(name + "x", "x", 8 * size, [], lambda r: far, 0, first)
            add(
                name + "y",
                "y",
                4 * size,
                [name + "x"],
                lambda r: other[:half] + r[name + "x"][half:].astype(F32),
            )
            quarter = once(
                sums,
                name + "part",
                lambda r: own[:half]
                + r[name + "x"][:half].astype(F32)
                + r[name + "y"].astype(F32),
            )
        return quarter, [name + route[1]]

    def add_rest(name, size, parts, direct=False):
        whole = once(
            sums,
            name + "whole",
            lambda r: jnp.concatenate([quarter(r) for quarter, _ in parts], 1)
            if len(parts) > 1
            else parts[0][0](r),
        )
        return add_ring(
            name,
            size,
            [need for _, needs in parts for need in needs],
            lambda r: [
                whole(r)[step * rows_in : (step + 1) * rows_in] for step in range(deep)
            ],
            direct,
        )

    def add_head(name, route, value):
        value = value.reshape(value.shape[0], 2, deep, 2, table_rows, width)
        own, far = (value[:, 0], value[:, 1]) if route == "x" else (
            value[:, :, :, 0], value[:, :, :, 1]
        )
        add(name + route, route, 16, [], lambda r: far)
        nearer = once(sums, name + "half", lambda r: own + r[name + route].astype(F32))
        depth = 1 if route == "x" else 2
        last = add_ring(
            name,
            4,
            [name + route],
            lambda r: [
                lax.index_in_dim(nearer(r), step, depth, keepdims=False) for step in range(deep)
            ],
        )
        final_axis = "y" if route == "x" else "x"
        add(name + final_axis, final_axis, 2, [name + "z" + str(deep - 1)], lambda r: last(r)[:, 1])
        return lambda r: last(r)[:, 0] + r[name + final_axis].astype(F32)

    grad_head = [
        add_head(
            "head" + str(half),
            "xy"[half],
            jnp.einsum(
                "kfv,fd->kvd",
                grad_logits[half],
                final,
                preferred_element_type=F32,
            ),
        )
        for half in range(2)
    ]

    grad, gain_final, shift_final = norm_back(
        residual_three, norm_params[6], norm_params[7], grad_final
    )
    grad = near(grad)

    rows_grad = spread(grad)
    grad_uppers, total = [], 0.0
    for up, back, slope in zip(weight_expand, weight_shrink, slopes):
        grad_active = product(rows_grad, back)
        grad_upper = (slope * grad_active).astype(BF16)
        total = total + across(grad_upper, up)
        grad_uppers.append(grad_upper)
    grad_normed = collect(total)
    grad_expand = add_rest(
        "expand",
        2,
        [add_rows("expand", 2, "yxz", 1, *(down(normed_three, part) for part in grad_uppers))],
    )
    grads_shrink = [down(rows_grad, active) for active in actives]
    grad_shrink = add_rest("shrink", 2, [add_rows("shrink", 2, "xyz", 1, *grads_shrink)])
    change, gain_three, shift_three = norm_back(residual_two, gains[4], gains[5], grad_normed)
    grad = grad + change

    rows_grad = spread(grad)
    grads, total = [], 0.0
    for weight, parts, mixed in zip(weight_cross, cross_parts, cross_mixed):
        grad_mixed = product(rows_grad, weight[:, triple:]).astype(BF16)
        grad_q, grad_k, grad_v = attend_back(*parts, grad_mixed, False)
        total = total + across(grad_q, weight[:, :cols_in])
        grads.append(
            jnp.concatenate(
                [
                    down(normed_two, grad_q),
                    down(memory, grad_k),
                    down(memory, grad_v),
                    down(rows_grad, mixed),
                ],
                1,
            )
        )
    grad_normed = collect(total)
    cut = grads[0].shape[1] // 2
    grad_cross = add_rest(
        "cross",
        2,
        [
            add_rows("cross0", 1, "yxz", 2, grads[0][:, :cut], grads[1][:, :cut]),
            add_rows("cross1", 1, "xyz", 2, grads[0][:, cut:], grads[1][:, cut:]),
        ],
    )
    early = {1: [rows_grad]}
    change, gain_two, shift_two = norm_back(residual_one, gains[2], gains[3], grad_normed)
    grad = grad + change

    rows_grad = spread(grad)
    grads, total = [], 0.0
    for weight, parts, mixed in zip(weight_self, self_parts, self_mixed):
        grad_mixed = product(rows_grad, weight[:, triple:]).astype(BF16)
        grad_heads = jnp.concatenate(attend_back(*parts, grad_mixed, True), 1)
        early[2] = [grad_heads]
        total = total + across(grad_heads, weight[:, :triple])
        grads.append(
            jnp.concatenate([down(normed_one, grad_heads), down(rows_grad, mixed)], 1)
        )
    grad_normed = collect(total)
    change, gain_one, shift_one = norm_back(residual, gains[0], gains[1], grad_normed)
    cut = grads[0].shape[1] // 2
    grad_self = add_rest(
        "self",
        2,
        [
            add_rows("self0", 1, "yxz", 3, grads[0][:, :cut], grads[1][:, :cut]),
            add_rows("self1", 1, "xyz", 3, grads[0][:, cut:], grads[1][:, cut:]),
        ],
        True,
    )
    grad = true(grad + change)

    rows_grad = grad.astype(BF16)
    early[3] = [rows_grad]

    def add_table():
        def spread_out(rows):
            return placed(grid.ring(rows, "c"), "c").reshape(frames, width)

        own_rows = spread_out(rows_grad)
        beside = [("x", "y", codes_other, table_ids), ("y", "x", codes_beside, beside_ids)]
        halves = []
        for half, (across_axis, sum_axis, codes_far, ids) in enumerate(beside):
            name = "table" + str(half)
            part = slice(half * books // 2, (half + 1) * books // 2)
            add("rows" + str(half), across_axis, 8, [], lambda r: rows_grad, 0, 4)
            far_rows = once(
                sums, "rows" + str(half), lambda r, k=half: spread_out(r["rows" + str(k)])
            )

            def value(r, part=part, far_rows=far_rows, codes_far=codes_far, ids=ids):
                result = 0.0
                for codes, rows in ((codes_own, own_rows), (codes_far, far_rows(r))):
                    places = (codes[part][..., None] == ids).astype(BF16)
                    result = result + jnp.einsum(
                        "kfv,fd->kvd", places, rows, preferred_element_type=F32
                    )
                return result.reshape(-1, deep, 2, table_rows, width)

            value = once(sums, name + "value", value)
            add(
                name + sum_axis, sum_axis, 8, ["rows" + str(half)],
                lambda r, v=value: v(r)[:, :, 1],
            )
            both = once(
                sums,
                name + "both",
                lambda r, v=value, n=name + sum_axis: v(r)[:, :, 0] + r[n].astype(F32),
            )
            halves.append(
                add_ring(
                    name,
                    2,
                    [name + sum_axis],
                    lambda r, b=both: [b(r)[:, -step % deep] for step in range(deep)],
                    True,
                )
            )
        return halves

    grad_table = add_table()
    norm_grads = [gain_one, shift_one, gain_two, shift_two, gain_three, shift_three]
    norm_grads = jnp.take(
        jnp.stack(norm_grads, 0).reshape(6, groups, -1), order_true, axis=1
    ).reshape(6, width)
    norm_grads = jnp.concatenate([norm_grads, gain_final[None], shift_final[None]], 0)
    loss_row = jnp.full((8, width), loss_local)
    norm_own = grid.total(jnp.concatenate([norm_grads, loss_row], 0), ("c",))
    tasks["normy"] = ("y", 0, [], 0, 3, lambda r: norm_own)
    tasks["normx"] = ("x", 0, ["normy"], 0, 4, lambda r: norm_own + r["normy"])
    norm_plane = once(sums, "norm", lambda r: norm_own + r["normy"] + r["normx"])
    for step in range(1, deep):
        tasks["normz" + str(step)] = ("z" + str(step), 0, ["normx"], 0, 0, norm_plane)
    ranks = ["self", "rows", "table", "cross", "expand", "shrink", "head", "norm"]
    tasks = {
        name: tasks[name]
        for rank in ranks
        for name in tasks
        if name.startswith(rank)
    }
    results = grid.rounds(tasks, BACK_BUDGET, early)
    grad_head = jnp.concatenate([part(results) for part in grad_head], 0)
    grad_table = jnp.concatenate([part(results) for part in grad_table], 0)
    grad_self, grad_cross = grad_self(results), grad_cross(results)
    grad_expand, grad_shrink = grad_expand(results), grad_shrink(results)
    summed = norm_plane(results)
    for step in range(1, deep):
        summed = summed + results["normz" + str(step)]
    grad_norm, loss_sum = summed[:8], summed[8, 0]

    def columns(array, first, count):
        return [
            array[:, (first + step) * cols_in : (first + step + 1) * cols_in]
            for step in range(count)
        ]

    stack_rows = min(128, cols_in)
    momentum_in = attend_in_momentum.transpose(1, 0, 2)

    def muon(tensor_parts, data_parts):
        tensor_factor = newton(
            grid.total(jnp.concatenate([folded_gram(part) for part in tensor_parts], 0), ("c", "y"))
        )
        blocks = [part.reshape(-1, stack_rows, cols_out) for part in data_parts]
        blocks = jnp.concatenate(blocks, 0)
        grams = grid.total(folded_gram(blocks), ("x", "z"))
        ortho = orthogonal(newton(grams), blocks)
        tensor_out, data_out, start = [], [], 0
        for part in tensor_parts:
            count = part.shape[0]
            tensor_out.append(orthogonal(tensor_factor[start : start + count], part))
            start += count
        start = 0
        for part in data_parts:
            count = part.size // (stack_rows * cols_out)
            data_out.append(ortho[start : start + count].reshape(part.shape))
            start += count
        return tensor_out, data_out

    next_cross = MOMENTUM * momentum_in[3:] + jnp.stack(columns(grad_cross, 0, 3), 0)
    next_expand = MOMENTUM * expand_momentum + grad_expand
    next_shrink = MOMENTUM * shrink_momentum + grad_shrink.T
    next_out_cross = MOMENTUM * attend_out_momentum[1] + columns(grad_cross, 3, 1)[0].T
    next_self = MOMENTUM * momentum_in[:3] + jnp.stack(columns(grad_self, 0, 3), 0)
    next_out_self = MOMENTUM * attend_out_momentum[0] + columns(grad_self, 3, 1)[0].T
    next_in = jnp.concatenate([next_self, next_cross], 0)
    next_out = jnp.stack([next_out_self, next_out_cross], 0)
    (ortho_in, ortho_expand), (ortho_out, ortho_shrink) = muon(
        [next_in, next_expand[None]], [next_out, next_shrink]
    )
    ortho_expand = ortho_expand[0]
    attend_in_new = (turned_in * (1.0 - 0.5 * DECAY) - 0.5 * ortho_in).transpose(1, 0, 2)
    attend_out_new = attend_out * (1.0 - 1.0 * DECAY) - 1.0 * ortho_out
    expand_new = expand_weights * (1.0 - 0.5 * DECAY) - 0.5 * ortho_expand
    shrink_new = shrink_weights * (1.0 - 0.5 * DECAY) - 0.5 * ortho_shrink
    embed_new, embed_first_new, embed_second_new = adam(
        embed_table, embed_first, embed_second, grad_table, 0.1, DECAY
    )
    head_new, head_first_new, head_second_new = adam(
        head_table, head_first, head_second, grad_head, 0.03, DECAY
    )
    norm_new, norm_first_new, norm_second_new = adam(
        norm_params, norm_first, norm_second, grad_norm, 0.5, 0.0
    )
    return (
        loss_sum,
        token_count,
        attend_in_new,
        attend_out_new,
        expand_new,
        shrink_new,
        next_in.transpose(1, 0, 2),
        next_out,
        next_expand,
        next_shrink,
        embed_new,
        head_new,
        norm_new,
        embed_first_new,
        embed_second_new,
        head_first_new,
        head_second_new,
        norm_first_new,
        norm_second_new,
    )


def solution(mesh):
    n_dp, n_tensor = mesh.shape["dp"], mesh.shape["tensor"]
    sizes = {"z": n_dp // 2, "x": 2, "y": 2, "c": n_tensor // 2}
    cut = Mesh(mesh.devices.reshape(tuple(sizes.values())), tuple(sizes))
    dp, tensor = ("z", "x"), ("y", "c")
    table = P(None, dp + tensor, None)
    matrices = (P(dp, None, tensor), P(None, tensor, dp), P(dp, tensor), P(tensor, dp))
    return jax.shard_map(
        lambda *args: body(Grid(sizes), *args),
        mesh=cut,
        in_specs=(P(dp, tensor, None),) * 3
        + (P(), P(dp, None))
        + matrices * 2
        + (table, table, P())
        + (table,) * 4
        + (P(), P()),
        out_specs=(P(), P())
        + matrices * 2
        + (table, table, P())
        + (table,) * 4
        + (P(), P()),
        check_vma=False,
    )
```

```python
import functools
import math

import jax
import jax.numpy as jnp
from jax import lax
from jax.experimental import pallas as pl
from jax.experimental.pallas import tpu as pltpu
from jax.sharding import Mesh
from jax.sharding import PartitionSpec as P

HEAD_DIM = 64
MUON_ROWS = 32
STEP = 10

HIGHEST = lax.Precision.HIGHEST
NEWTON = (3.4445, -4.775, 2.0315)
BETA_ONE = 0.9
BETA_TWO = 0.95
ADAM_EPS = 1e-08
DECAY = 0.01
MOMENTUM = 0.95
BF16 = jnp.bfloat16
F32 = jnp.float32
LANES = 128
BUDGET = 8
BACK_BUDGET = 16
KERNEL_VMEM = 48 * 1024 * 1024
LIGHT = pl.CostEstimate(flops=1024, bytes_accessed=1024, transcendentals=0)


def layer_norm(values, gain, shift):
    centred = values - jnp.mean(values, -1, keepdims=True)
    variance = jnp.mean(centred * centred, -1, keepdims=True)
    return centred * lax.rsqrt(variance + 1e-05) * gain + shift


def norm_back(values, gain, shift, grad):
    result, backward = jax.vjp(layer_norm, values, gain, shift)
    return backward(grad)


def gelu_and_slope(values):
    falling = jnp.exp(-0.5 * values * values)
    near = 1.0 / (1.0 + (0.3275911 * math.sqrt(0.5)) * jnp.abs(values))
    series = 1.061405429
    for weight in (-1.453152027, 1.421413741, -0.284496736, 0.254829592):
        series = series * near + weight
    tail = 0.5 * series * near * falling
    below = jnp.where(values >= 0.0, 1.0 - tail, tail)
    return values * below, below + values * falling * (1.0 / math.sqrt(2.0 * math.pi))


def sinusoid(first, length, width):
    half = width // 2
    rates = jnp.exp(jnp.arange(half, dtype=jnp.float32) * (-math.log(10000.0) / half))
    places = (first + jnp.arange(length, dtype=jnp.int32)).astype(jnp.float32)
    angles = places[:, None] * rates[None, :]
    return jnp.concatenate([jnp.sin(angles), jnp.cos(angles)], -1)


def adam(weight, first, second, gradient, rate, decay):
    first = BETA_ONE * first + (1.0 - BETA_ONE) * gradient
    second = BETA_TWO * second + (1.0 - BETA_TWO) * gradient * gradient
    direction = (
        first / (1.0 - BETA_ONE**STEP) / (jnp.sqrt(second / (1.0 - BETA_TWO**STEP)) + ADAM_EPS)
    )
    return (weight - rate * (direction + decay * weight), first, second)


class Grid:
    def __init__(self, sizes):
        self.sizes = sizes

    def index(self, axis):
        return lax.axis_index(axis)

    def rotate(self, value, axis, step=1):
        size = self.sizes[axis]
        return lax.ppermute(value, axis, [(i, (i + step) % size) for i in range(size)])

    def swap(self, value, axis, step=1):
        return lax.ppermute(value, axis, [(i, i ^ step) for i in range(self.sizes[axis])])

    def total(self, value, axes):
        for axis in axes:
            step = 1
            while step < self.sizes[axis]:
                value = value + lax.ppermute(
                    value, axis, [(i, i ^ step) for i in range(self.sizes[axis])]
                )
                step *= 2
        return value

    def ring(self, shard, axis):
        held = [shard]
        for _ in range(1, self.sizes[axis]):
            held.append(self.rotate(held[-1], axis))
        return [held[-r % self.sizes[axis]] for r in range(self.sizes[axis])]

    def ring_sum(self, parts, axis):
        size = self.sizes[axis]
        running = parts[size - 1]
        for step in range(1, size):
            arrived = self.rotate(running.astype(BF16), axis)
            running = arrived.astype(F32) + parts[size - 1 - step].astype(F32)
        return running

    def rounds(self, tasks, budget, early=None, pack=True):
        done, results, last, sent, when = {}, {}, [], [], 0

        def unpack(lists, arrived):
            start = 0
            for name, value in lists:
                results[name] = arrived
                if len(lists) > 1:
                    rows = value.size // value.shape[-1]
                    results[name] = arrived[start : start + rows].reshape(value.shape)
                    start += rows

        waiting = list(tasks)
        while waiting:
            used, picked = {}, []
            for name in waiting:
                axis, size, needs, between, first, _ = tasks[name]
                ready = when >= first and all(
                    done.get(need, when) + between < when for need in needs
                )
                load = used.get(axis[0], 0)
                if ready and (load == 0 or load + size <= budget):
                    used[axis[0]] = load + size
                    picked.append(name)
            tokens = (early or {}).get(when)
            if tokens and last:
                last = lax.optimization_barrier((last, tokens))[0]
                for (_, lists), arrived in zip(sent, last):
                    unpack(lists, arrived)
            messages = {}
            for name in picked:
                value = tasks[name][-1](results)
                key = (tasks[name][0], value.shape[-1], value.dtype if pack else name)
                messages.setdefault(key, []).append((name, value))
            if messages:
                values = [
                    lists[0][1]
                    if len(lists) == 1
                    else jnp.concatenate([value.reshape(-1, key[1]) for _, value in lists], 0)
                    for key, lists in messages.items()
                ]
                tied = lax.optimization_barrier((values, last))[0]
                last, sent = [], list(messages.items())
                for ((axis, _, _), lists), value in zip(sent, tied):
                    if axis[0] == "z":
                        last.append(self.rotate(value, "z", int(axis[1:] or 1)))
                    else:
                        last.append(self.swap(value, axis))
                    unpack(lists, last[-1])
                    for name, _ in lists:
                        done[name] = when
            waiting = [name for name in waiting if name not in picked]
            when += 1
        return results


def chosen(array, index, axis):
    return lax.dynamic_index_in_dim(array, index, axis, keepdims=False)


def move_blocks(array, order):
    rows, cols = array.shape
    count = order.shape[0]
    block = cols // count
    if block % LANES or rows % 16:
        return jnp.take(array.reshape(rows, count, block), order, axis=1).reshape(rows, cols)

    def kernel(order_ref, from_ref, to_ref):
        for p in range(count):
            start = pl.multiple_of(order_ref[p] * block, LANES)
            to_ref[:, p * block : (p + 1) * block] = from_ref[:, pl.ds(start, block)]

    step = min(rows, 128)
    return pl.pallas_call(
        kernel,
        grid_spec=pltpu.PrefetchScalarGridSpec(
            num_scalar_prefetch=1,
            grid=(rows // step,),
            in_specs=[pl.BlockSpec((step, cols), lambda p, order: (p, 0))],
            out_specs=pl.BlockSpec((step, cols), lambda p, order: (p, 0)),
        ),
        out_shape=jax.ShapeDtypeStruct(array.shape, array.dtype),
        cost_estimate=LIGHT,
    )(order, array)


def arranged(blocks, order):
    count, books, rows, cols = blocks.shape
    half = books // 2
    if rows % 16:
        whole = jnp.take(blocks, order, axis=0).transpose(1, 0, 2, 3)
        return whole[:half], whole[half:]

    def kernel(order_ref, from_ref, first_ref, second_ref):
        first_ref[...] = from_ref[:, :half].reshape(first_ref.shape)
        second_ref[...] = from_ref[:, half:].reshape(second_ref.shape)

    result = jax.ShapeDtypeStruct((half, count, rows, cols), blocks.dtype)
    spec = pl.BlockSpec((half, 1, rows, cols), lambda p, order: (0, p, 0, 0))
    return pl.pallas_call(
        kernel,
        grid_spec=pltpu.PrefetchScalarGridSpec(
            num_scalar_prefetch=1,
            grid=(count,),
            in_specs=[pl.BlockSpec((1, books, rows, cols), lambda p, order: (order[p], 0, 0, 0))],
            out_specs=[spec, spec],
        ),
        out_shape=[result, result],
        cost_estimate=LIGHT,
    )(order, blocks)


def after(value, token):
    return lax.optimization_barrier((value, token))[0]


def contract(left, right, left_dim, right_dim):
    return lax.dot_general(
        left, right, (((left_dim,), (right_dim,)), ((), ())), preferred_element_type=F32
    )


def contract_rows(left, right):
    return contract(left, right, 1, 0)


def spans(frames, keys, causal):
    block = min(256 if causal else 512, frames)
    return [
        (first, block, min(keys, first + block) if causal else keys)
        for first in range(0, frames, block)
    ]


def scores_down(query, key_ref, first, last, causal):
    if not causal:
        return contract(key_ref[pl.ds(0, last), :], query, 1, 1)
    edge = contract(key_ref[pl.ds(first, last - first), :], query, 1, 1)
    key_at = lax.broadcasted_iota(jnp.int32, edge.shape, 0)
    query_at = lax.broadcasted_iota(jnp.int32, edge.shape, 1)
    edge = jnp.where(key_at <= query_at, edge, -jnp.inf)
    if first == 0:
        return edge
    return jnp.concatenate([contract(key_ref[pl.ds(0, first), :], query, 1, 1), edge], 0)


def head_lanes(shape, head):
    lane = lax.broadcasted_iota(jnp.int32, shape, 1)
    return (lane // HEAD_DIM) == head


def attend_kernel(causal, query_ref, key_ref, value_ref, mixed_ref, total_ref):
    frames, keys = query_ref.shape[0], key_ref.shape[0]
    turned = value_ref[...].astype(F32).T.astype(BF16)
    for first, block, last in spans(frames, keys, causal):
        query = query_ref[pl.ds(first, block), :] * jnp.asarray(0.125, BF16)
        parts = []
        for head in range(LANES // HEAD_DIM):
            own = jnp.where(head_lanes(query.shape, head), query, jnp.zeros_like(query))
            scores = scores_down(own, key_ref, first, last, causal)
            top = jnp.max(scores, 0, keepdims=True)
            expo = jnp.exp(scores - top)
            total = jnp.sum(expo, 0, keepdims=True)
            total_ref[0, head : head + 1, pl.ds(first, block)] = top + jnp.log(total)
            parts.append(
                contract_rows(
                    turned[head * HEAD_DIM : (head + 1) * HEAD_DIM, :last],
                    (expo * (1.0 / total)).astype(BF16),
                )
            )
        mixed_ref[pl.ds(first, block), :] = jnp.concatenate(parts, 0).T.astype(BF16)


def attend_back_kernel(
    causal,
    query_ref,
    key_ref,
    value_ref,
    mixed_ref,
    total_ref,
    grad_ref,
    grad_query_ref,
    grad_key_ref,
    grad_value_ref,
    key_sum,
    value_sum,
):
    frames, keys = query_ref.shape[0], key_ref.shape[0]
    turned = key_ref[...].astype(F32).T.astype(BF16)
    key_sum[...] = jnp.zeros_like(key_sum)
    value_sum[...] = jnp.zeros_like(value_sum)
    for first, block, last in spans(frames, keys, causal):
        query = query_ref[pl.ds(first, block), :] * jnp.asarray(0.125, BF16)
        grad = grad_ref[pl.ds(first, block), :]
        shared = (grad.astype(F32) * mixed_ref[pl.ds(first, block), :].astype(F32)).T
        parts = []
        for head in range(LANES // HEAD_DIM):
            lanes = head_lanes(query.shape, head)
            own = jnp.where(lanes, query, jnp.zeros_like(query))
            own_grad = jnp.where(lanes, grad, jnp.zeros_like(grad))
            scores = scores_down(own, key_ref, first, last, causal)
            probs = jnp.exp(scores - total_ref[0, head : head + 1, pl.ds(first, block)])
            grad_probs = contract(value_ref[pl.ds(0, last), :], own_grad, 1, 1)
            mean = jnp.sum(shared[head * HEAD_DIM : (head + 1) * HEAD_DIM], 0, keepdims=True)
            grad_scores = (probs * (grad_probs - mean)).astype(BF16)
            value_sum[pl.ds(0, last), :] += contract_rows(probs.astype(BF16), own_grad)
            key_sum[pl.ds(0, last), :] += contract_rows(grad_scores, own)
            parts.append(
                contract_rows(
                    turned[head * HEAD_DIM : (head + 1) * HEAD_DIM, :last],
                    grad_scores,
                )
            )
        grad_query_ref[pl.ds(first, block), :] = (jnp.concatenate(parts, 0).T * 0.125).astype(BF16)
    grad_key_ref[...] = key_sum[...].astype(BF16)
    grad_value_ref[...] = value_sum[...].astype(BF16)


def attend(queries, keys, values, causal):
    frames, key_rows = queries[0].shape[0], keys[0].shape[0]
    count = queries[2]

    def spec(rows, start):
        return pl.BlockSpec((rows, LANES), lambda p, start=start: (0, start + p))

    return pl.pallas_call(
        functools.partial(attend_kernel, causal),
        grid=(count,),
        in_specs=[
            spec(frames, queries[1]),
            spec(key_rows, keys[1]),
            spec(key_rows, values[1]),
        ],
        out_specs=[spec(frames, 0), pl.BlockSpec((1, 2, frames), lambda p: (p, 0, 0))],
        out_shape=[
            jax.ShapeDtypeStruct((frames, count * LANES), BF16),
            jax.ShapeDtypeStruct((count, 2, frames), F32),
        ],
        compiler_params=pltpu.CompilerParams(vmem_limit_bytes=KERNEL_VMEM),
        cost_estimate=LIGHT,
    )(queries[0], keys[0], values[0])


def attend_back(queries, keys, values, mixed, total, grad, causal):
    frames, key_rows = queries[0].shape[0], keys[0].shape[0]
    count = queries[2]

    def spec(rows, start):
        return pl.BlockSpec((rows, LANES), lambda p, start=start: (0, start + p))

    wide = count * LANES
    return pl.pallas_call(
        functools.partial(attend_back_kernel, causal),
        grid=(count,),
        in_specs=[
            spec(frames, queries[1]),
            spec(key_rows, keys[1]),
            spec(key_rows, values[1]),
            spec(frames, 0),
            pl.BlockSpec((1, 2, frames), lambda p: (p, 0, 0)),
            spec(frames, 0),
        ],
        out_specs=[spec(frames, 0), spec(key_rows, 0), spec(key_rows, 0)],
        out_shape=[
            jax.ShapeDtypeStruct((frames, wide), BF16),
            jax.ShapeDtypeStruct((key_rows, wide), BF16),
            jax.ShapeDtypeStruct((key_rows, wide), BF16),
        ],
        scratch_shapes=[pltpu.VMEM((key_rows, LANES), F32), pltpu.VMEM((key_rows, LANES), F32)],
        compiler_params=pltpu.CompilerParams(vmem_limit_bytes=KERNEL_VMEM),
        cost_estimate=LIGHT,
    )(queries[0], keys[0], values[0], mixed, total, grad)


def newton(grams):
    count, _, rows = grams.shape
    repeats = rows // MUON_ROWS
    band = jnp.arange(rows) // MUON_ROWS
    mask = band[:, None] == band[None, :]
    eye = jnp.eye(rows, dtype=F32)
    gram = jnp.where(mask, jnp.tile(grams, (1, repeats, 1)), 0.0)
    diagonal = jnp.sum(gram * eye, -1).reshape(count, repeats, MUON_ROWS)
    size = jnp.sqrt(jnp.sum(diagonal, -1, keepdims=True)) + 1e-07
    size = jnp.broadcast_to(size, diagonal.shape).reshape(count, rows, 1)
    gram = gram / (size * size)

    def times(left, right):
        return jnp.einsum("brs,bst->brt", left, right, precision=HIGHEST)

    factor = None
    for repeat in range(5):
        mixing = NEWTON[0] * eye + NEWTON[1] * gram + NEWTON[2] * times(gram, gram)
        factor = mixing if factor is None else times(mixing, factor)
        if repeat < 4:
            gram = times(mixing, times(gram, mixing))
    return factor / size


def folded_gram(part):
    count, rows, _ = part.shape
    gram = jnp.einsum("brc,bsc->brs", part, part, precision=HIGHEST)
    band = jnp.arange(rows) // MUON_ROWS
    gram = jnp.where(band[:, None] == band[None, :], gram, 0.0)
    return jnp.sum(gram.reshape(count, rows // MUON_ROWS, MUON_ROWS, rows), 1)


def orthogonal(factor, part):
    return jnp.einsum("brs,bsc->brc", factor, part, precision=HIGHEST)


def body(
    grid,
    codes_in,
    codes_out,
    pad_mask,
    text_table,
    text_index,
    attend_in,
    attend_out,
    expand_weights,
    shrink_weights,
    attend_in_momentum,
    attend_out_momentum,
    expand_momentum,
    shrink_momentum,
    embed_table,
    head_table,
    norm_params,
    embed_first,
    embed_second,
    head_first,
    head_second,
    norm_first,
    norm_second,
):
    sizes = grid.sizes
    at_z, at_x, at_y, at_c = (grid.index(axis) for axis in ("z", "x", "y", "c"))
    deep, inner = sizes["z"], sizes["c"]
    width = norm_params.shape[1]
    clips, frames_part, books = codes_in.shape
    frames = frames_part * 2 * inner
    own_frames = frames // inner
    rows_in, members, cols_in = attend_in.shape
    cols_out = attend_out.shape[2]
    table_rows = embed_table.shape[1]
    groups = deep * 2

    place = jnp.arange(groups)
    order_near = (place % deep + at_z) % deep * 2 + (place // deep + at_x) % 2
    order_true = (place % 2 + at_x) % 2 * deep + (place // 2 - at_z) % deep

    def near(array):
        return move_blocks(array, order_near)

    def true(array):
        return move_blocks(array, order_true)

    codes = jnp.stack([codes_in, codes_out, pad_mask], 0).transpose(0, 3, 1, 2)

    def placed(pieces, axis):
        full = jnp.zeros((len(pieces),) + pieces[0].shape, pieces[0].dtype)
        for step, piece in enumerate(pieces):
            full = lax.dynamic_update_index_in_dim(
                full, piece, (lax.axis_index(axis) + step) % len(pieces), 0
            )
        return full

    def all_along(piece, axis):
        size = sizes[axis]
        held = [piece]
        for _ in range(1, size):
            held.append(
                lax.ppermute(held[-1], axis, [(i, (i + 1) % size) for i in range(size)])
            )
        return placed([held[-step % size] for step in range(size)], axis)

    codes = all_along(codes, "c")

    def once(kept, name, make):
        def get(results):
            if name not in kept:
                kept[name] = make(results)
            return kept[name]

        return get

    made = {}

    def clip_codes(results):
        both = placed([codes, results["codesy"]], "y")
        both = both.transpose(2, 3, 4, 0, 1, 5).reshape(3, books, clips, frames)
        return chosen(both, at_y, 2), jnp.sum(both[2]), chosen(both[0], 1 - at_y, 1)

    clip_codes = once(made, "codes", clip_codes)

    def codes_sent(results):
        own, count, _ = clip_codes(results)
        return jnp.concatenate([own[0], jnp.full((books, frames), count)], 0)

    turned_in = attend_in.transpose(1, 0, 2)
    turned_out = attend_out.transpose(0, 2, 1)

    def side_by_side(parts):
        return jnp.concatenate([part.astype(BF16) for part in parts], 1)

    hidden = expand_weights.shape[1]
    shard_rows = [books * table_rows, rows_in, rows_in]
    shards = {
        "first": jnp.concatenate(
            [embed_table.astype(BF16).reshape(-1, width)]
            + [
                side_by_side(parts).reshape(-1, width)
                for parts in (
                    list(turned_in[:3]) + [turned_out[0]],
                    list(turned_in[3:]) + [turned_out[1]],
                )
            ],
            0,
        ),
        "feed": jnp.concatenate(
            [part.astype(BF16).reshape(-1, width) for part in (expand_weights, shrink_weights.T)], 0
        ),
    }
    attend_rows = (shards["first"].shape[0] - books * table_rows) // 2
    starts = {"embed": 0, "self": books * table_rows, "cross": books * table_rows + attend_rows}
    tasks = {}

    def arrived(results, group, step):
        return results[group + "z" + str(step)] if step else shards[group]

    def embed_piece(results, axis, step):
        if axis == "y":
            return results["embedy" + str(step)]
        rows = arrived(results, "first", step)[: starts["self"]]
        return rows.reshape(books, table_rows, width)

    def attend_piece(results, axis, step, part=None):
        if axis == "x":
            rows = results["attendx" + str(step)]
        else:
            rows = arrived(results, "first", step)[starts["self"] :]
        if part is not None:
            rows = rows[part * attend_rows : (part + 1) * attend_rows]
        return rows

    def near_part(results, part):
        order = [-spot % deep for spot in range(deep)]
        blocks = [
            attend_piece(results, axis, step, part).reshape(rows_in, -1)
            for axis in ("z", "x")
            for step in order
        ]
        return jnp.concatenate(blocks, 0)

    def add_ring_of(group, size, first):
        for step in range(1, deep):
            ahead = [group + "z" + str(step - 1)] if step > 1 else []
            tasks[group + "z" + str(step)] = (
                "z", size, ahead, 0, first, lambda r, k=step: arrived(r, group, k - 1)
            )

    add_ring_of("first", 8, 0)
    for step in range(deep):
        needs = ["firstz" + str(step)] if step else []
        tasks["embedy" + str(step)] = (
            "y", 4, needs, 0, 0, lambda r, k=step: embed_piece(r, "z", k)
        )
        tasks["attendx" + str(step)] = (
            "x", 4, needs, 0, 0, lambda r, k=step: attend_piece(r, "z", k)
        )
        tasks["selfy" + str(step)] = (
            "y", 4, ["attendx" + str(step)], 0, 0,
            lambda r, k=step: jnp.concatenate(
                [attend_piece(r, "z", k, 0), attend_piece(r, "x", k, 0)], 0
            ),
        )
    tasks["codesy"] = ("y", 0, [], 0, 1, lambda r: codes)
    tasks["codesx"] = ("x", 0, ["codesy"], 0, 2, codes_sent)

    def pair_count(results):
        count = clip_codes(results)[1] + results["codesx"][books, 0]
        return jnp.full((8, LANES), count)

    steps = [1 << power for power in range((deep - 1).bit_length())]

    def counted(results, known):
        count = pair_count(results)
        for step in steps[:known]:
            count = count + results["count" + str(step)]
        return count

    for at, step in enumerate(steps):
        ahead = "count" + str(steps[at - 1]) if at else "codesx"
        tasks["count" + str(step)] = (
            "z" + str(step), 0, [ahead], 0, 0, lambda r, k=at: counted(r, k)
        )
    add_ring_of("feed", 4, deep - 1)
    tasks["rows"] = (
        "x", 8, ["embedy" + str(step) for step in range(deep)] + ["codesx"], 0, deep + 1,
        lambda r: embedded_of(r["codesx"][:books], table_of(r)),
    )
    tasks["crossy"] = (
        "y", 16, ["attendx" + str(step) for step in range(deep)], 0, deep + 1,
        lambda r: near_part(r, 1),
    )

    z_place = (at_z - jnp.arange(deep)) % deep
    y_place = jnp.stack([at_y, 1 - at_y])
    table_ids = ((z_place * 2 + at_x) * 2)[:, None] + y_place[None, :]
    table_ids = ((table_ids * inner + at_c)[:, :, None] * table_rows + jnp.arange(table_rows)).reshape(
        -1
    )
    beside_ids = ((z_place * 2)[:, None] + jnp.stack([at_x, 1 - at_x])[None, :]) * 2 + at_y
    beside_ids = (beside_ids * inner + at_c)[:, :, None] * table_rows + jnp.arange(table_rows)
    beside_ids = beside_ids.reshape(-1)
    kept_table = []

    def table_of(results):
        if not kept_table:
            pieces = []
            for step in range(deep):
                pieces += [embed_piece(results, "z", step), embed_piece(results, "y", step)]
            kept_table.append(jnp.concatenate(pieces, 1))
        return kept_table[0]

    def hot(codes):
        return (codes[..., None] == table_ids).astype(BF16)

    def embedded_of(codes, table):
        rows = jnp.einsum("kfv,kvd->fd", hot(codes), table, preferred_element_type=F32)
        rows = rows.reshape(inner, own_frames, width)
        rows = grid.ring_sum(
            [chosen(rows, (at_c + step) % inner, 0) for step in range(inner)], "c"
        )
        return rows.astype(BF16)

    results = grid.rounds(tasks, BUDGET, pack=False)
    clip, _, codes_beside = clip_codes(results)
    codes_own, next_codes, live = clip[0], clip[1], clip[2].astype(F32)
    codes_other = results["codesx"][:books]
    token_count = counted(results, len(steps))[0, 0].astype(F32)
    own_part = embedded_of(codes_own, table_of(results)).astype(F32)
    embedded = own_part + results["rows"].astype(F32)
    residual = near(embedded + sinusoid(at_c * own_frames, own_frames, width))
    residual = after(residual, token_count)

    far_self = [results["selfy" + str(-spot % deep)] for spot in range(deep)]
    far_self = [
        part[half * attend_rows : (half + 1) * attend_rows].reshape(rows_in, -1)
        for half in range(2)
        for part in far_self
    ]
    weight_self = [near_part(results, 0), jnp.concatenate(far_self, 0)]
    weight_cross = [near_part(results, 1), results["crossy"]]

    feed_rows = shards["feed"].shape[0] // 2
    halves = [
        jnp.concatenate(
            [
                arrived(results, "feed", -spot % deep)[part * feed_rows : (part + 1) * feed_rows]
                for spot in range(deep)
            ],
            0,
        )
        for part in range(2)
    ]
    up_half, back_half = after(halves, residual)
    up_far, back_far = grid.swap(up_half, "x"), grid.swap(back_half, "y")

    def feed_second(token):
        rows = up_half.shape[0]
        near_up, far_back = after((up_far, back_far), token)
        up = jnp.concatenate([up_half, near_up], 0)
        back = jnp.concatenate([back_half, far_back], 0)
        up_other, back_other = grid.swap(up, "y"), grid.swap(back, "x")
        backs = [
            jnp.concatenate([back_half, back_other[:rows]], 0),
            jnp.concatenate([far_back, back_other[rows:]], 0),
        ]
        ups = [up, up_other]
        return [
            [matrix.reshape(width, hidden) for matrix in pair] for pair in (ups, backs)
        ]

    head_shard = after(head_table.astype(BF16), results["rows"])
    head = lax.all_gather(head_shard, ("z", "x", "y"), axis=0)
    head_order = (order_near[:, None] * 2 + y_place[None, :]).reshape(-1)
    head = [part.reshape(books // 2, -1, width) for part in arranged(head, head_order)]
    head_ids = (head_order * inner + at_c)[:, None] * table_rows + jnp.arange(table_rows)
    head_ids = head_ids.reshape(-1)

    def spread(rows):
        return placed(grid.ring(rows.astype(BF16), "c"), "c").reshape(frames, width)

    def collect(partial_rows):
        parts = partial_rows.reshape(inner, own_frames, width)
        running = chosen(parts, (at_c + inner - 1) % inner, 0)
        for step in range(1, inner):
            arrived = grid.rotate(running, "c")
            running = arrived + chosen(parts, (at_c + inner - 1 - step) % inner, 0)
        return running

    def product(left, right):
        return contract(left, right, 1, 0)

    def across(left, right):
        return contract(left, right, 1, 1)

    def down(left, right):
        return contract(left, right, 0, 0)

    gains = jnp.take(norm_params.reshape(8, groups, -1), order_near, axis=1).reshape(8, width)
    memory = jnp.take(text_table, chosen(text_index, at_y, 0), axis=0)
    memory = near(memory)
    pairs = cols_in // LANES
    triple = 3 * cols_in

    normed_one = spread(layer_norm(residual, gains[0], gains[1]))
    self_parts, self_mixed, total = [], [], 0.0
    for weight in weight_self:
        heads = product(normed_one, weight[:, :triple]).astype(BF16)
        parts = [(heads, member * pairs, pairs) for member in range(3)]
        mixed, log_sums = attend(*parts, True)
        total = total + across(mixed, weight[:, triple:])
        self_parts.append(parts + [mixed, log_sums])
        self_mixed.append(mixed)
    total = after(total, (results["crossy"], results["feedz" + str(deep - 1)]))
    residual_one = residual + collect(total)

    normed_two = spread(layer_norm(residual_one, gains[2], gains[3]))
    cross_parts, cross_mixed, total = [], [], 0.0
    for weight in weight_cross:
        query = product(normed_two, weight[:, :cols_in]).astype(BF16)
        key_value = product(memory, weight[:, cols_in:triple]).astype(BF16)
        parts = [(query, 0, pairs), (key_value, 0, pairs), (key_value, pairs, pairs)]
        mixed, log_sums = attend(*parts, False)
        total = total + across(mixed, weight[:, triple:])
        cross_parts.append(parts + [mixed, log_sums])
        cross_mixed.append(mixed)
    weight_expand, weight_shrink = feed_second(cross_mixed[0])
    total = after(total, (up_far, back_far))
    residual_two = after(
        residual_one + collect(total), (head, weight_expand[1], weight_shrink[1])
    )

    normed_three = spread(layer_norm(residual_two, gains[4], gains[5]))
    slopes, actives, total = [], [], 0.0
    for up, back in zip(weight_expand, weight_shrink):
        active, slope = gelu_and_slope(product(normed_three, up))
        active, slope = lax.optimization_barrier((active.astype(BF16), slope))
        total = total + across(active, back)
        slopes.append(slope)
        actives.append(active)
    residual_three = true(residual_two + collect(total))

    final = spread(layer_norm(residual_three, norm_params[6], norm_params[7]))
    logits, targets, stats = [], [], []
    for half, part in enumerate(head):
        wanted = next_codes[half * books // 2 : (half + 1) * books // 2]
        values = jnp.einsum("fd,kvd->kfv", final, part, preferred_element_type=F32)
        is_target = head_ids[None, None, :] == wanted[:, :, None]
        row_max = jnp.max(values, -1)
        picked = jnp.sum(jnp.where(is_target, values, 0.0), -1)
        row_sum = jnp.sum(jnp.exp(values - row_max[..., None]), -1)
        logits.append(values)
        targets.append(is_target)
        stats.append(jnp.stack([row_max, row_sum, picked], 0))
    stats = grid.ring(jnp.concatenate(stats, 1), "c")
    top = stats[0][0]
    for stat in stats[1:]:
        top = jnp.maximum(top, stat[0])
    row_sum = sum(stat[1] * jnp.exp(stat[0] - top) for stat in stats)
    picked = sum(stat[2] for stat in stats)
    log_total = top + jnp.log(row_sum)
    loss_local = jnp.where(at_c == 0, jnp.sum((log_total - picked) * live), 0.0)
    share = live / token_count
    grad_logits = []
    for half in range(2):
        part = slice(half * books // 2, (half + 1) * books // 2)
        grad_part = jnp.exp(logits[half] - log_total[part][..., None]) - targets[half].astype(F32)
        grad_logits.append((grad_part * share[part][..., None]).astype(BF16))
    grad_logits = lax.optimization_barrier(grad_logits)
    grad_final = collect(
        sum(
            jnp.einsum("kfv,kvd->fd", values, part, preferred_element_type=F32)
            for values, part in zip(grad_logits, head)
        )
    )
    tasks, sums = {}, {}

    def add(name, axis, size, needs, value, between=0, first=0):
        tasks[name] = (axis, size, needs, between, first, lambda r: value(r).astype(BF16))

    def add_ring(name, size, needs, parts, direct=False):
        if direct:
            for step in range(1, deep):
                add(
                    name + "z" + str(step), "z" + str(step), size, needs,
                    lambda r, k=step: parts(r)[k],
                )
            return once(
                sums,
                name + "far",
                lambda r: sum(
                    (r[name + "z" + str(step)].astype(F32) for step in range(1, deep)),
                    parts(r)[0].astype(F32),
                ),
            )
        get = once(sums, name + "0", lambda r: parts(r)[deep - 1])
        for step in range(1, deep):
            add(name + "z" + str(step), "z", size, needs, get)
            needs = [name + "z" + str(step)]
            get = once(
                sums,
                name + str(step),
                lambda r, n=needs[0], k=step: r[n].astype(F32) + parts(r)[deep - 1 - k].astype(F32),
            )
        return get

    def add_rows(name, size, route, first, own, other):
        half = width // 2
        if route[0] == "y":
            add(name + "y", "y", 8 * size, [], lambda r: other, 0, first)
            whole = once(sums, name + "sum", lambda r: own + r[name + "y"].astype(F32))
            add(name + "x", "x", 4 * size, [name + "y"], lambda r: whole(r)[half:])
            quarter = once(
                sums,
                name + "part", lambda r: whole(r)[:half] + r[name + "x"].astype(F32)
            )
        else:
            far = jnp.concatenate([own[half:].astype(BF16), other[half:].astype(BF16)], 0)
            add(name + "x", "x", 8 * size, [], lambda r: far, 0, first)
            add(
                name + "y",
                "y",
                4 * size,
                [name + "x"],
                lambda r: other[:half] + r[name + "x"][half:].astype(F32),
            )
            quarter = once(
                sums,
                name + "part",
                lambda r: own[:half]
                + r[name + "x"][:half].astype(F32)
                + r[name + "y"].astype(F32),
            )
        return quarter, [name + route[1]]

    def add_rest(name, size, parts, direct=False):
        whole = once(
            sums,
            name + "whole",
            lambda r: jnp.concatenate([quarter(r) for quarter, _ in parts], 1)
            if len(parts) > 1
            else parts[0][0](r),
        )
        return add_ring(
            name,
            size,
            [need for _, needs in parts for need in needs],
            lambda r: [
                whole(r)[step * rows_in : (step + 1) * rows_in] for step in range(deep)
            ],
            direct,
        )

    def add_head(name, route, value):
        value = value.reshape(value.shape[0], 2, deep, 2, table_rows, width)
        own, far = (value[:, 0], value[:, 1]) if route == "x" else (
            value[:, :, :, 0], value[:, :, :, 1]
        )
        add(name + route, route, 16, [], lambda r: far)
        nearer = once(sums, name + "half", lambda r: own + r[name + route].astype(F32))
        depth = 1 if route == "x" else 2
        last = add_ring(
            name,
            4,
            [name + route],
            lambda r: [
                lax.index_in_dim(nearer(r), step, depth, keepdims=False) for step in range(deep)
            ],
        )
        final_axis = "y" if route == "x" else "x"
        add(name + final_axis, final_axis, 2, [name + "z" + str(deep - 1)], lambda r: last(r)[:, 1])
        return lambda r: last(r)[:, 0] + r[name + final_axis].astype(F32)

    grad_head = [
        add_head(
            "head" + str(half),
            "xy"[half],
            jnp.einsum(
                "kfv,fd->kvd",
                grad_logits[half],
                final,
                preferred_element_type=F32,
            ),
        )
        for half in range(2)
    ]

    grad, gain_final, shift_final = norm_back(
        residual_three, norm_params[6], norm_params[7], grad_final
    )
    grad = near(grad)

    rows_grad = spread(grad)
    grad_uppers, total = [], 0.0
    for up, back, slope in zip(weight_expand, weight_shrink, slopes):
        grad_active = product(rows_grad, back)
        grad_upper = (slope * grad_active).astype(BF16)
        total = total + across(grad_upper, up)
        grad_uppers.append(grad_upper)
    grad_normed = collect(total)
    grad_expand = add_rest(
        "expand",
        2,
        [add_rows("expand", 2, "yxz", 1, *(down(normed_three, part) for part in grad_uppers))],
    )
    grads_shrink = [down(rows_grad, active) for active in actives]
    grad_shrink = add_rest("shrink", 2, [add_rows("shrink", 2, "xyz", 1, *grads_shrink)])
    change, gain_three, shift_three = norm_back(residual_two, gains[4], gains[5], grad_normed)
    grad = grad + change

    rows_grad = spread(grad)
    grads, total = [], 0.0
    for weight, parts, mixed in zip(weight_cross, cross_parts, cross_mixed):
        grad_mixed = product(rows_grad, weight[:, triple:]).astype(BF16)
        grad_q, grad_k, grad_v = attend_back(*parts, grad_mixed, False)
        total = total + across(grad_q, weight[:, :cols_in])
        grads.append(
            jnp.concatenate(
                [
                    down(normed_two, grad_q),
                    down(memory, grad_k),
                    down(memory, grad_v),
                    down(rows_grad, mixed),
                ],
                1,
            )
        )
    grad_normed = collect(total)
    cut = grads[0].shape[1] // 2
    grad_cross = add_rest(
        "cross",
        2,
        [
            add_rows("cross0", 1, "yxz", 2, grads[0][:, :cut], grads[1][:, :cut]),
            add_rows("cross1", 1, "xyz", 2, grads[0][:, cut:], grads[1][:, cut:]),
        ],
    )
    early = {1: [rows_grad]}
    change, gain_two, shift_two = norm_back(residual_one, gains[2], gains[3], grad_normed)
    grad = grad + change

    rows_grad = spread(grad)
    grads, total = [], 0.0
    for weight, parts, mixed in zip(weight_self, self_parts, self_mixed):
        grad_mixed = product(rows_grad, weight[:, triple:]).astype(BF16)
        grad_heads = jnp.concatenate(attend_back(*parts, grad_mixed, True), 1)
        early[2] = [grad_heads]
        total = total + across(grad_heads, weight[:, :triple])
        grads.append(
            jnp.concatenate([down(normed_one, grad_heads), down(rows_grad, mixed)], 1)
        )
    grad_normed = collect(total)
    change, gain_one, shift_one = norm_back(residual, gains[0], gains[1], grad_normed)
    cut = grads[0].shape[1] // 2
    grad_self = add_rest(
        "self",
        2,
        [
            add_rows("self0", 1, "yxz", 3, grads[0][:, :cut], grads[1][:, :cut]),
            add_rows("self1", 1, "xyz", 3, grads[0][:, cut:], grads[1][:, cut:]),
        ],
        True,
    )
    grad = true(grad + change)

    rows_grad = grad.astype(BF16)
    early[3] = [rows_grad]

    def add_table():
        def spread_out(rows):
            return placed(grid.ring(rows, "c"), "c").reshape(frames, width)

        own_rows = spread_out(rows_grad)
        beside = [("x", "y", codes_other, table_ids), ("y", "x", codes_beside, beside_ids)]
        halves = []
        for half, (across_axis, sum_axis, codes_far, ids) in enumerate(beside):
            name = "table" + str(half)
            part = slice(half * books // 2, (half + 1) * books // 2)
            add("rows" + str(half), across_axis, 8, [], lambda r: rows_grad, 0, 4)
            far_rows = once(
                sums, "rows" + str(half), lambda r, k=half: spread_out(r["rows" + str(k)])
            )

            def value(r, part=part, far_rows=far_rows, codes_far=codes_far, ids=ids):
                result = 0.0
                for codes, rows in ((codes_own, own_rows), (codes_far, far_rows(r))):
                    places = (codes[part][..., None] == ids).astype(BF16)
                    result = result + jnp.einsum(
                        "kfv,fd->kvd", places, rows, preferred_element_type=F32
                    )
                return result.reshape(-1, deep, 2, table_rows, width)

            value = once(sums, name + "value", value)
            add(
                name + sum_axis, sum_axis, 8, ["rows" + str(half)],
                lambda r, v=value: v(r)[:, :, 1],
            )
            both = once(
                sums,
                name + "both",
                lambda r, v=value, n=name + sum_axis: v(r)[:, :, 0] + r[n].astype(F32),
            )
            halves.append(
                add_ring(
                    name,
                    2,
                    [name + sum_axis],
                    lambda r, b=both: [b(r)[:, -step % deep] for step in range(deep)],
                    True,
                )
            )
        return halves

    grad_table = add_table()
    norm_grads = [gain_one, shift_one, gain_two, shift_two, gain_three, shift_three]
    norm_grads = jnp.take(
        jnp.stack(norm_grads, 0).reshape(6, groups, -1), order_true, axis=1
    ).reshape(6, width)
    norm_grads = jnp.concatenate([norm_grads, gain_final[None], shift_final[None]], 0)
    loss_row = jnp.full((8, width), loss_local)
    norm_own = grid.total(jnp.concatenate([norm_grads, loss_row], 0), ("c",))
    tasks["normy"] = ("y", 0, [], 0, 3, lambda r: norm_own)
    tasks["normx"] = ("x", 0, ["normy"], 0, 4, lambda r: norm_own + r["normy"])
    norm_plane = once(sums, "norm", lambda r: norm_own + r["normy"] + r["normx"])
    for step in range(1, deep):
        tasks["normz" + str(step)] = ("z" + str(step), 0, ["normx"], 0, 0, norm_plane)
    ranks = ["self", "rows", "table", "cross", "expand", "shrink", "head", "norm"]
    tasks = {
        name: tasks[name]
        for rank in ranks
        for name in tasks
        if name.startswith(rank)
    }
    results = grid.rounds(tasks, BACK_BUDGET, early)
    grad_head = jnp.concatenate([part(results) for part in grad_head], 0)
    grad_table = jnp.concatenate([part(results) for part in grad_table], 0)
    grad_self, grad_cross = grad_self(results), grad_cross(results)
    grad_expand, grad_shrink = grad_expand(results), grad_shrink(results)
    summed = norm_plane(results)
    for step in range(1, deep):
        summed = summed + results["normz" + str(step)]
    grad_norm, loss_sum = summed[:8], summed[8, 0]

    def columns(array, first, count):
        return [
            array[:, (first + step) * cols_in : (first + step + 1) * cols_in]
            for step in range(count)
        ]

    stack_rows = min(128, cols_in)
    momentum_in = attend_in_momentum.transpose(1, 0, 2)

    def muon(tensor_parts, data_parts):
        tensor_factor = newton(
            grid.total(jnp.concatenate([folded_gram(part) for part in tensor_parts], 0), ("c", "y"))
        )
        blocks = [part.reshape(-1, stack_rows, cols_out) for part in data_parts]
        blocks = jnp.concatenate(blocks, 0)
        grams = grid.total(folded_gram(blocks), ("x", "z"))
        ortho = orthogonal(newton(grams), blocks)
        tensor_out, data_out, start = [], [], 0
        for part in tensor_parts:
            count = part.shape[0]
            tensor_out.append(orthogonal(tensor_factor[start : start + count], part))
            start += count
        start = 0
        for part in data_parts:
            count = part.size // (stack_rows * cols_out)
            data_out.append(ortho[start : start + count].reshape(part.shape))
            start += count
        return tensor_out, data_out

    next_cross = MOMENTUM * momentum_in[3:] + jnp.stack(columns(grad_cross, 0, 3), 0)
    next_expand = MOMENTUM * expand_momentum + grad_expand
    next_shrink = MOMENTUM * shrink_momentum + grad_shrink.T
    next_out_cross = MOMENTUM * attend_out_momentum[1] + columns(grad_cross, 3, 1)[0].T
    next_self = MOMENTUM * momentum_in[:3] + jnp.stack(columns(grad_self, 0, 3), 0)
    next_out_self = MOMENTUM * attend_out_momentum[0] + columns(grad_self, 3, 1)[0].T
    next_in = jnp.concatenate([next_self, next_cross], 0)
    next_out = jnp.stack([next_out_self, next_out_cross], 0)
    (ortho_in, ortho_expand), (ortho_out, ortho_shrink) = muon(
        [next_in, next_expand[None]], [next_out, next_shrink]
    )
    ortho_expand = ortho_expand[0]
    attend_in_new = (turned_in * (1.0 - 0.5 * DECAY) - 0.5 * ortho_in).transpose(1, 0, 2)
    attend_out_new = attend_out * (1.0 - 1.0 * DECAY) - 1.0 * ortho_out
    expand_new = expand_weights * (1.0 - 0.5 * DECAY) - 0.5 * ortho_expand
    shrink_new = shrink_weights * (1.0 - 0.5 * DECAY) - 0.5 * ortho_shrink
    embed_new, embed_first_new, embed_second_new = adam(
        embed_table, embed_first, embed_second, grad_table, 0.1, DECAY
    )
    head_new, head_first_new, head_second_new = adam(
        head_table, head_first, head_second, grad_head, 0.03, DECAY
    )
    norm_new, norm_first_new, norm_second_new = adam(
        norm_params, norm_first, norm_second, grad_norm, 0.5, 0.0
    )
    return (
        loss_sum,
        token_count,
        attend_in_new,
        attend_out_new,
        expand_new,
        shrink_new,
        next_in.transpose(1, 0, 2),
        next_out,
        next_expand,
        next_shrink,
        embed_new,
        head_new,
        norm_new,
        embed_first_new,
        embed_second_new,
        head_first_new,
        head_second_new,
        norm_first_new,
        norm_second_new,
    )


def solution(mesh):
    n_dp, n_tensor = mesh.shape["dp"], mesh.shape["tensor"]
    sizes = {"z": n_dp // 2, "x": 2, "y": 2, "c": n_tensor // 2}
    cut = Mesh(mesh.devices.reshape(tuple(sizes.values())), tuple(sizes))
    dp, tensor = ("z", "x"), ("y", "c")
    table = P(None, dp + tensor, None)
    matrices = (P(dp, None, tensor), P(None, tensor, dp), P(dp, tensor), P(tensor, dp))
    return jax.shard_map(
        lambda *args: body(Grid(sizes), *args),
        mesh=cut,
        in_specs=(P(dp, tensor, None),) * 3
        + (P(), P(dp, None))
        + matrices * 2
        + (table, table, P())
        + (table,) * 4
        + (P(), P()),
        out_specs=(P(), P())
        + matrices * 2
        + (table, table, P())
        + (table,) * 4
        + (P(), P()),
        check_vma=False,
    )
```

```python
import functools
import math

import jax
import jax.numpy as jnp
from jax import lax
from jax.experimental import pallas as pl
from jax.experimental.pallas import tpu as pltpu
from jax.sharding import Mesh
from jax.sharding import PartitionSpec as P

HEAD_DIM = 64
MUON_ROWS = 32
STEP = 10

HIGHEST = lax.Precision.HIGHEST
NEWTON = (3.4445, -4.775, 2.0315)
BETA_ONE = 0.9
BETA_TWO = 0.95
ADAM_EPS = 1e-08
DECAY = 0.01
MOMENTUM = 0.95
BF16 = jnp.bfloat16
F32 = jnp.float32
LANES = 128
BUDGET = 8
BACK_BUDGET = 16
KERNEL_VMEM = 48 * 1024 * 1024
LIGHT = pl.CostEstimate(flops=1024, bytes_accessed=1024, transcendentals=0)


def layer_norm(values, gain, shift):
    centred = values - jnp.mean(values, -1, keepdims=True)
    variance = jnp.mean(centred * centred, -1, keepdims=True)
    return centred * lax.rsqrt(variance + 1e-05) * gain + shift


def norm_back(values, gain, shift, grad):
    result, backward = jax.vjp(layer_norm, values, gain, shift)
    return backward(grad)


def gelu_and_slope(values):
    falling = jnp.exp(-0.5 * values * values)
    near = 1.0 / (1.0 + (0.3275911 * math.sqrt(0.5)) * jnp.abs(values))
    series = 1.061405429
    for weight in (-1.453152027, 1.421413741, -0.284496736, 0.254829592):
        series = series * near + weight
    tail = 0.5 * series * near * falling
    below = jnp.where(values >= 0.0, 1.0 - tail, tail)
    return values * below, below + values * falling * (1.0 / math.sqrt(2.0 * math.pi))


def sinusoid(first, length, width):
    half = width // 2
    rates = jnp.exp(jnp.arange(half, dtype=jnp.float32) * (-math.log(10000.0) / half))
    places = (first + jnp.arange(length, dtype=jnp.int32)).astype(jnp.float32)
    angles = places[:, None] * rates[None, :]
    return jnp.concatenate([jnp.sin(angles), jnp.cos(angles)], -1)


def adam(weight, first, second, gradient, rate, decay):
    first = BETA_ONE * first + (1.0 - BETA_ONE) * gradient
    second = BETA_TWO * second + (1.0 - BETA_TWO) * gradient * gradient
    direction = (
        first / (1.0 - BETA_ONE**STEP) / (jnp.sqrt(second / (1.0 - BETA_TWO**STEP)) + ADAM_EPS)
    )
    return (weight - rate * (direction + decay * weight), first, second)


class Grid:
    def __init__(self, sizes):
        self.sizes = sizes

    def index(self, axis):
        return lax.axis_index(axis)

    def rotate(self, value, axis, step=1):
        size = self.sizes[axis]
        return lax.ppermute(value, axis, [(i, (i + step) % size) for i in range(size)])

    def swap(self, value, axis, step=1):
        return lax.ppermute(value, axis, [(i, i ^ step) for i in range(self.sizes[axis])])

    def total(self, value, axes):
        for axis in axes:
            step = 1
            while step < self.sizes[axis]:
                value = value + lax.ppermute(
                    value, axis, [(i, i ^ step) for i in range(self.sizes[axis])]
                )
                step *= 2
        return value

    def ring(self, shard, axis):
        held = [shard]
        for _ in range(1, self.sizes[axis]):
            held.append(self.rotate(held[-1], axis))
        return [held[-r % self.sizes[axis]] for r in range(self.sizes[axis])]

    def ring_sum(self, parts, axis):
        size = self.sizes[axis]
        running = parts[size - 1]
        for step in range(1, size):
            arrived = self.rotate(running.astype(BF16), axis)
            running = arrived.astype(F32) + parts[size - 1 - step].astype(F32)
        return running

    def rounds(self, tasks, budget, early=None, pack=True):
        done, results, last, sent, when = {}, {}, [], [], 0

        def unpack(lists, arrived):
            start = 0
            for name, value in lists:
                results[name] = arrived
                if len(lists) > 1:
                    rows = value.size // value.shape[-1]
                    results[name] = arrived[start : start + rows].reshape(value.shape)
                    start += rows

        waiting = list(tasks)
        while waiting:
            used, picked = {}, []
            for name in waiting:
                axis, size, needs, between, first, _ = tasks[name]
                ready = when >= first and all(
                    done.get(need, when) + between < when for need in needs
                )
                load = used.get(axis[0], 0)
                if ready and (load == 0 or load + size <= budget):
                    used[axis[0]] = load + size
                    picked.append(name)
            tokens = (early or {}).get(when)
            if tokens and last:
                last = lax.optimization_barrier((last, tokens))[0]
                for (_, lists), arrived in zip(sent, last):
                    unpack(lists, arrived)
            messages = {}
            for name in picked:
                value = tasks[name][-1](results)
                key = (tasks[name][0], value.shape[-1], value.dtype if pack else name)
                messages.setdefault(key, []).append((name, value))
            if messages:
                values = [
                    lists[0][1]
                    if len(lists) == 1
                    else jnp.concatenate([value.reshape(-1, key[1]) for _, value in lists], 0)
                    for key, lists in messages.items()
                ]
                tied = lax.optimization_barrier((values, last))[0]
                last, sent = [], list(messages.items())
                for ((axis, _, _), lists), value in zip(sent, tied):
                    if axis[0] == "z":
                        last.append(self.rotate(value, "z", int(axis[1:] or 1)))
                    else:
                        last.append(self.swap(value, axis))
                    unpack(lists, last[-1])
                    for name, _ in lists:
                        done[name] = when
            waiting = [name for name in waiting if name not in picked]
            when += 1
        return results


def chosen(array, index, axis):
    return lax.dynamic_index_in_dim(array, index, axis, keepdims=False)


def move_blocks(array, order):
    rows, cols = array.shape
    count = order.shape[0]
    block = cols // count
    if block % LANES or rows % 16:
        return jnp.take(array.reshape(rows, count, block), order, axis=1).reshape(rows, cols)

    def kernel(order_ref, from_ref, to_ref):
        for p in range(count):
            start = pl.multiple_of(order_ref[p] * block, LANES)
            to_ref[:, p * block : (p + 1) * block] = from_ref[:, pl.ds(start, block)]

    step = min(rows, 256)
    return pl.pallas_call(
        kernel,
        grid_spec=pltpu.PrefetchScalarGridSpec(
            num_scalar_prefetch=1,
            grid=(rows // step,),
            in_specs=[pl.BlockSpec((step, cols), lambda p, order: (p, 0))],
            out_specs=pl.BlockSpec((step, cols), lambda p, order: (p, 0)),
        ),
        out_shape=jax.ShapeDtypeStruct(array.shape, array.dtype),
        cost_estimate=LIGHT,
    )(order, array)


def arranged(blocks, order):
    count, books, rows, cols = blocks.shape
    half = books // 2
    if rows % 16:
        whole = jnp.take(blocks, order, axis=0).transpose(1, 0, 2, 3)
        return whole[:half], whole[half:]

    def kernel(order_ref, from_ref, first_ref, second_ref):
        first_ref[...] = from_ref[:, :half].reshape(first_ref.shape)
        second_ref[...] = from_ref[:, half:].reshape(second_ref.shape)

    result = jax.ShapeDtypeStruct((half, count, rows, cols), blocks.dtype)
    spec = pl.BlockSpec((half, 1, rows, cols), lambda p, order: (0, p, 0, 0))
    return pl.pallas_call(
        kernel,
        grid_spec=pltpu.PrefetchScalarGridSpec(
            num_scalar_prefetch=1,
            grid=(count,),
            in_specs=[pl.BlockSpec((1, books, rows, cols), lambda p, order: (order[p], 0, 0, 0))],
            out_specs=[spec, spec],
        ),
        out_shape=[result, result],
        cost_estimate=LIGHT,
    )(order, blocks)


def after(value, token):
    return lax.optimization_barrier((value, token))[0]


def contract(left, right, left_dim, right_dim):
    return lax.dot_general(
        left, right, (((left_dim,), (right_dim,)), ((), ())), preferred_element_type=F32
    )


def contract_rows(left, right):
    return contract(left, right, 1, 0)


def spans(frames, keys, causal):
    block = min(256 if causal else 512, frames)
    return [
        (first, block, min(keys, first + block) if causal else keys)
        for first in range(0, frames, block)
    ]


def scores_down(query, key_ref, first, last, causal):
    if not causal:
        return contract(key_ref[pl.ds(0, last), :], query, 1, 1)
    edge = contract(key_ref[pl.ds(first, last - first), :], query, 1, 1)
    key_at = lax.broadcasted_iota(jnp.int32, edge.shape, 0)
    query_at = lax.broadcasted_iota(jnp.int32, edge.shape, 1)
    edge = jnp.where(key_at <= query_at, edge, -jnp.inf)
    if first == 0:
        return edge
    return jnp.concatenate([contract(key_ref[pl.ds(0, first), :], query, 1, 1), edge], 0)


def head_lanes(shape, head):
    lane = lax.broadcasted_iota(jnp.int32, shape, 1)
    return (lane // HEAD_DIM) == head


def attend_kernel(causal, query_ref, key_ref, value_ref, mixed_ref, total_ref):
    frames, keys = query_ref.shape[0], key_ref.shape[0]
    turned = value_ref[...].astype(F32).T.astype(BF16)
    for first, block, last in spans(frames, keys, causal):
        query = query_ref[pl.ds(first, block), :] * jnp.asarray(0.125, BF16)
        parts = []
        for head in range(LANES // HEAD_DIM):
            own = jnp.where(head_lanes(query.shape, head), query, jnp.zeros_like(query))
            scores = scores_down(own, key_ref, first, last, causal)
            top = jnp.max(scores, 0, keepdims=True)
            expo = jnp.exp(scores - top)
            total = jnp.sum(expo, 0, keepdims=True)
            total_ref[0, head : head + 1, pl.ds(first, block)] = top + jnp.log(total)
            parts.append(
                contract_rows(
                    turned[head * HEAD_DIM : (head + 1) * HEAD_DIM, :last],
                    (expo * (1.0 / total)).astype(BF16),
                )
            )
        mixed_ref[pl.ds(first, block), :] = jnp.concatenate(parts, 0).T.astype(BF16)


def attend_back_kernel(
    causal,
    query_ref,
    key_ref,
    value_ref,
    mixed_ref,
    total_ref,
    grad_ref,
    grad_query_ref,
    grad_key_ref,
    grad_value_ref,
    key_sum,
    value_sum,
):
    frames, keys = query_ref.shape[0], key_ref.shape[0]
    turned = key_ref[...].astype(F32).T.astype(BF16)
    key_sum[...] = jnp.zeros_like(key_sum)
    value_sum[...] = jnp.zeros_like(value_sum)
    for first, block, last in spans(frames, keys, causal):
        query = query_ref[pl.ds(first, block), :] * jnp.asarray(0.125, BF16)
        grad = grad_ref[pl.ds(first, block), :]
        shared = (grad.astype(F32) * mixed_ref[pl.ds(first, block), :].astype(F32)).T
        parts = []
        for head in range(LANES // HEAD_DIM):
            lanes = head_lanes(query.shape, head)
            own = jnp.where(lanes, query, jnp.zeros_like(query))
            own_grad = jnp.where(lanes, grad, jnp.zeros_like(grad))
            scores = scores_down(own, key_ref, first, last, causal)
            probs = jnp.exp(scores - total_ref[0, head : head + 1, pl.ds(first, block)])
            grad_probs = contract(value_ref[pl.ds(0, last), :], own_grad, 1, 1)
            mean = jnp.sum(shared[head * HEAD_DIM : (head + 1) * HEAD_DIM], 0, keepdims=True)
            grad_scores = (probs * (grad_probs - mean)).astype(BF16)
            value_sum[pl.ds(0, last), :] += contract_rows(probs.astype(BF16), own_grad)
            key_sum[pl.ds(0, last), :] += contract_rows(grad_scores, own)
            parts.append(
                contract_rows(
                    turned[head * HEAD_DIM : (head + 1) * HEAD_DIM, :last],
                    grad_scores,
                )
            )
        grad_query_ref[pl.ds(first, block), :] = (jnp.concatenate(parts, 0).T * 0.125).astype(BF16)
    grad_key_ref[...] = key_sum[...].astype(BF16)
    grad_value_ref[...] = value_sum[...].astype(BF16)


def attend(queries, keys, values, causal):
    frames, key_rows = queries[0].shape[0], keys[0].shape[0]
    count = queries[2]

    def spec(rows, start):
        return pl.BlockSpec((rows, LANES), lambda p, start=start: (0, start + p))

    return pl.pallas_call(
        functools.partial(attend_kernel, causal),
        grid=(count,),
        in_specs=[
            spec(frames, queries[1]),
            spec(key_rows, keys[1]),
            spec(key_rows, values[1]),
        ],
        out_specs=[spec(frames, 0), pl.BlockSpec((1, 2, frames), lambda p: (p, 0, 0))],
        out_shape=[
            jax.ShapeDtypeStruct((frames, count * LANES), BF16),
            jax.ShapeDtypeStruct((count, 2, frames), F32),
        ],
        compiler_params=pltpu.CompilerParams(vmem_limit_bytes=KERNEL_VMEM),
        cost_estimate=LIGHT,
    )(queries[0], keys[0], values[0])


def attend_back(queries, keys, values, mixed, total, grad, causal):
    frames, key_rows = queries[0].shape[0], keys[0].shape[0]
    count = queries[2]

    def spec(rows, start):
        return pl.BlockSpec((rows, LANES), lambda p, start=start: (0, start + p))

    wide = count * LANES
    return pl.pallas_call(
        functools.partial(attend_back_kernel, causal),
        grid=(count,),
        in_specs=[
            spec(frames, queries[1]),
            spec(key_rows, keys[1]),
            spec(key_rows, values[1]),
            spec(frames, 0),
            pl.BlockSpec((1, 2, frames), lambda p: (p, 0, 0)),
            spec(frames, 0),
        ],
        out_specs=[spec(frames, 0), spec(key_rows, 0), spec(key_rows, 0)],
        out_shape=[
            jax.ShapeDtypeStruct((frames, wide), BF16),
            jax.ShapeDtypeStruct((key_rows, wide), BF16),
            jax.ShapeDtypeStruct((key_rows, wide), BF16),
        ],
        scratch_shapes=[pltpu.VMEM((key_rows, LANES), F32), pltpu.VMEM((key_rows, LANES), F32)],
        compiler_params=pltpu.CompilerParams(vmem_limit_bytes=KERNEL_VMEM),
        cost_estimate=LIGHT,
    )(queries[0], keys[0], values[0], mixed, total, grad)


def newton(grams):
    count, _, rows = grams.shape
    repeats = rows // MUON_ROWS
    band = jnp.arange(rows) // MUON_ROWS
    mask = band[:, None] == band[None, :]
    eye = jnp.eye(rows, dtype=F32)
    gram = jnp.where(mask, jnp.tile(grams, (1, repeats, 1)), 0.0)
    diagonal = jnp.sum(gram * eye, -1).reshape(count, repeats, MUON_ROWS)
    size = jnp.sqrt(jnp.sum(diagonal, -1, keepdims=True)) + 1e-07
    size = jnp.broadcast_to(size, diagonal.shape).reshape(count, rows, 1)
    gram = gram / (size * size)

    def times(left, right):
        return jnp.einsum("brs,bst->brt", left, right, precision=HIGHEST)

    factor = None
    for repeat in range(5):
        mixing = NEWTON[0] * eye + NEWTON[1] * gram + NEWTON[2] * times(gram, gram)
        factor = mixing if factor is None else times(mixing, factor)
        if repeat < 4:
            gram = times(mixing, times(gram, mixing))
    return factor / size


def folded_gram(part):
    count, rows, _ = part.shape
    gram = jnp.einsum("brc,bsc->brs", part, part, precision=HIGHEST)
    band = jnp.arange(rows) // MUON_ROWS
    gram = jnp.where(band[:, None] == band[None, :], gram, 0.0)
    return jnp.sum(gram.reshape(count, rows // MUON_ROWS, MUON_ROWS, rows), 1)


def orthogonal(factor, part):
    return jnp.einsum("brs,bsc->brc", factor, part, precision=HIGHEST)


def body(
    grid,
    codes_in,
    codes_out,
    pad_mask,
    text_table,
    text_index,
    attend_in,
    attend_out,
    expand_weights,
    shrink_weights,
    attend_in_momentum,
    attend_out_momentum,
    expand_momentum,
    shrink_momentum,
    embed_table,
    head_table,
    norm_params,
    embed_first,
    embed_second,
    head_first,
    head_second,
    norm_first,
    norm_second,
):
    sizes = grid.sizes
    at_z, at_x, at_y, at_c = (grid.index(axis) for axis in ("z", "x", "y", "c"))
    deep, inner = sizes["z"], sizes["c"]
    width = norm_params.shape[1]
    clips, frames_part, books = codes_in.shape
    frames = frames_part * 2 * inner
    own_frames = frames // inner
    rows_in, members, cols_in = attend_in.shape
    cols_out = attend_out.shape[2]
    table_rows = embed_table.shape[1]
    groups = deep * 2

    place = jnp.arange(groups)
    order_near = (place % deep + at_z) % deep * 2 + (place // deep + at_x) % 2
    order_true = (place % 2 + at_x) % 2 * deep + (place // 2 - at_z) % deep

    def near(array):
        return move_blocks(array, order_near)

    def true(array):
        return move_blocks(array, order_true)

    codes = jnp.stack([codes_in, codes_out, pad_mask], 0).transpose(0, 3, 1, 2)

    def placed(pieces, axis):
        full = jnp.zeros((len(pieces),) + pieces[0].shape, pieces[0].dtype)
        for step, piece in enumerate(pieces):
            full = lax.dynamic_update_index_in_dim(
                full, piece, (lax.axis_index(axis) + step) % len(pieces), 0
            )
        return full

    def all_along(piece, axis):
        size = sizes[axis]
        held = [piece]
        for _ in range(1, size):
            held.append(
                lax.ppermute(held[-1], axis, [(i, (i + 1) % size) for i in range(size)])
            )
        return placed([held[-step % size] for step in range(size)], axis)

    codes = all_along(codes, "c")

    def once(kept, name, make):
        def get(results):
            if name not in kept:
                kept[name] = make(results)
            return kept[name]

        return get

    made = {}

    def clip_codes(results):
        both = placed([codes, results["codesy"]], "y")
        both = both.transpose(2, 3, 4, 0, 1, 5).reshape(3, books, clips, frames)
        return chosen(both, at_y, 2), jnp.sum(both[2]), chosen(both[0], 1 - at_y, 1)

    clip_codes = once(made, "codes", clip_codes)

    def codes_sent(results):
        own, count, _ = clip_codes(results)
        return jnp.concatenate([own[0], jnp.full((books, frames), count)], 0)

    turned_in = attend_in.transpose(1, 0, 2)
    turned_out = attend_out.transpose(0, 2, 1)

    def side_by_side(parts):
        return jnp.concatenate([part.astype(BF16) for part in parts], 1)

    hidden = expand_weights.shape[1]
    shard_rows = [books * table_rows, rows_in, rows_in]
    shards = {
        "first": jnp.concatenate(
            [embed_table.astype(BF16).reshape(-1, width)]
            + [
                side_by_side(parts).reshape(-1, width)
                for parts in (
                    list(turned_in[:3]) + [turned_out[0]],
                    list(turned_in[3:]) + [turned_out[1]],
                )
            ],
            0,
        ),
        "feed": jnp.concatenate(
            [part.astype(BF16).reshape(-1, width) for part in (expand_weights, shrink_weights.T)], 0
        ),
    }
    attend_rows = (shards["first"].shape[0] - books * table_rows) // 2
    starts = {"embed": 0, "self": books * table_rows, "cross": books * table_rows + attend_rows}
    tasks = {}

    def arrived(results, group, step):
        return results[group + "z" + str(step)] if step else shards[group]

    def embed_piece(results, axis, step):
        if axis == "y":
            return results["embedy" + str(step)]
        rows = arrived(results, "first", step)[: starts["self"]]
        return rows.reshape(books, table_rows, width)

    def attend_piece(results, axis, step, part=None):
        if axis == "x":
            rows = results["attendx" + str(step)]
        else:
            rows = arrived(results, "first", step)[starts["self"] :]
        if part is not None:
            rows = rows[part * attend_rows : (part + 1) * attend_rows]
        return rows

    def near_part(results, part):
        order = [-spot % deep for spot in range(deep)]
        blocks = [
            attend_piece(results, axis, step, part).reshape(rows_in, -1)
            for axis in ("z", "x")
            for step in order
        ]
        return jnp.concatenate(blocks, 0)

    def add_ring_of(group, size, first):
        for step in range(1, deep):
            ahead = [group + "z" + str(step - 1)] if step > 1 else []
            tasks[group + "z" + str(step)] = (
                "z", size, ahead, 0, first, lambda r, k=step: arrived(r, group, k - 1)
            )

    add_ring_of("first", 8, 0)
    for step in range(deep):
        needs = ["firstz" + str(step)] if step else []
        tasks["embedy" + str(step)] = (
            "y", 4, needs, 0, 0, lambda r, k=step: embed_piece(r, "z", k)
        )
        tasks["attendx" + str(step)] = (
            "x", 4, needs, 0, 0, lambda r, k=step: attend_piece(r, "z", k)
        )
        tasks["selfy" + str(step)] = (
            "y", 4, ["attendx" + str(step)], 0, 0,
            lambda r, k=step: jnp.concatenate(
                [attend_piece(r, "z", k, 0), attend_piece(r, "x", k, 0)], 0
            ),
        )
    tasks["codesy"] = ("y", 0, [], 0, 1, lambda r: codes)
    tasks["codesx"] = ("x", 0, ["codesy"], 0, 2, codes_sent)

    def pair_count(results):
        count = clip_codes(results)[1] + results["codesx"][books, 0]
        return jnp.full((8, LANES), count)

    steps = [1 << power for power in range((deep - 1).bit_length())]

    def counted(results, known):
        count = pair_count(results)
        for step in steps[:known]:
            count = count + results["count" + str(step)]
        return count

    for at, step in enumerate(steps):
        ahead = "count" + str(steps[at - 1]) if at else "codesx"
        tasks["count" + str(step)] = (
            "z" + str(step), 0, [ahead], 0, 0, lambda r, k=at: counted(r, k)
        )
    add_ring_of("feed", 4, deep - 1)
    tasks["rows"] = (
        "x", 8, ["embedy" + str(step) for step in range(deep)] + ["codesx"], 0, deep + 1,
        lambda r: embedded_of(r["codesx"][:books], table_of(r)),
    )
    tasks["crossy"] = (
        "y", 16, ["attendx" + str(step) for step in range(deep)], 0, deep + 1,
        lambda r: near_part(r, 1),
    )

    z_place = (at_z - jnp.arange(deep)) % deep
    y_place = jnp.stack([at_y, 1 - at_y])
    table_ids = ((z_place * 2 + at_x) * 2)[:, None] + y_place[None, :]
    table_ids = ((table_ids * inner + at_c)[:, :, None] * table_rows + jnp.arange(table_rows)).reshape(
        -1
    )
    beside_ids = ((z_place * 2)[:, None] + jnp.stack([at_x, 1 - at_x])[None, :]) * 2 + at_y
    beside_ids = (beside_ids * inner + at_c)[:, :, None] * table_rows + jnp.arange(table_rows)
    beside_ids = beside_ids.reshape(-1)
    kept_table = []

    def table_of(results):
        if not kept_table:
            pieces = []
            for step in range(deep):
                pieces += [embed_piece(results, "z", step), embed_piece(results, "y", step)]
            kept_table.append(jnp.concatenate(pieces, 1))
        return kept_table[0]

    def hot(codes):
        return (codes[..., None] == table_ids).astype(BF16)

    def embedded_of(codes, table):
        rows = jnp.einsum("kfv,kvd->fd", hot(codes), table, preferred_element_type=F32)
        rows = rows.reshape(inner, own_frames, width)
        rows = grid.ring_sum(
            [chosen(rows, (at_c + step) % inner, 0) for step in range(inner)], "c"
        )
        return rows.astype(BF16)

    results = grid.rounds(tasks, BUDGET, pack=False)
    clip, _, codes_beside = clip_codes(results)
    codes_own, next_codes, live = clip[0], clip[1], clip[2].astype(F32)
    codes_other = results["codesx"][:books]
    token_count = counted(results, len(steps))[0, 0].astype(F32)
    own_part = embedded_of(codes_own, table_of(results)).astype(F32)
    embedded = own_part + results["rows"].astype(F32)
    residual = near(embedded + sinusoid(at_c * own_frames, own_frames, width))
    residual = after(residual, token_count)

    far_self = [results["selfy" + str(-spot % deep)] for spot in range(deep)]
    far_self = [
        part[half * attend_rows : (half + 1) * attend_rows].reshape(rows_in, -1)
        for half in range(2)
        for part in far_self
    ]
    weight_self = [near_part(results, 0), jnp.concatenate(far_self, 0)]
    weight_cross = [near_part(results, 1), results["crossy"]]

    feed_rows = shards["feed"].shape[0] // 2
    halves = [
        jnp.concatenate(
            [
                arrived(results, "feed", -spot % deep)[part * feed_rows : (part + 1) * feed_rows]
                for spot in range(deep)
            ],
            0,
        )
        for part in range(2)
    ]
    up_half, back_half = after(halves, residual)
    up_far, back_far = grid.swap(up_half, "x"), grid.swap(back_half, "y")

    def feed_second(token):
        rows = up_half.shape[0]
        near_up, far_back = after((up_far, back_far), token)
        up = jnp.concatenate([up_half, near_up], 0)
        back = jnp.concatenate([back_half, far_back], 0)
        up_other, back_other = grid.swap(up, "y"), grid.swap(back, "x")
        backs = [
            jnp.concatenate([back_half, back_other[:rows]], 0),
            jnp.concatenate([far_back, back_other[rows:]], 0),
        ]
        ups = [up, up_other]
        return [
            [matrix.reshape(width, hidden) for matrix in pair] for pair in (ups, backs)
        ]

    head_shard = after(head_table.astype(BF16), results["rows"])
    head = lax.all_gather(head_shard, ("z", "x", "y"), axis=0)
    head_order = (order_near[:, None] * 2 + y_place[None, :]).reshape(-1)
    head = [part.reshape(books // 2, -1, width) for part in arranged(head, head_order)]
    head_ids = (head_order * inner + at_c)[:, None] * table_rows + jnp.arange(table_rows)
    head_ids = head_ids.reshape(-1)

    def spread(rows):
        return placed(grid.ring(rows.astype(BF16), "c"), "c").reshape(frames, width)

    def collect(partial_rows):
        parts = partial_rows.reshape(inner, own_frames, width)
        running = chosen(parts, (at_c + inner - 1) % inner, 0)
        for step in range(1, inner):
            arrived = grid.rotate(running, "c")
            running = arrived + chosen(parts, (at_c + inner - 1 - step) % inner, 0)
        return running

    def product(left, right):
        return contract(left, right, 1, 0)

    def across(left, right):
        return contract(left, right, 1, 1)

    def down(left, right):
        return contract(left, right, 0, 0)

    gains = jnp.take(norm_params.reshape(8, groups, -1), order_near, axis=1).reshape(8, width)
    memory = jnp.take(text_table, chosen(text_index, at_y, 0), axis=0)
    memory = near(memory)
    pairs = cols_in // LANES
    triple = 3 * cols_in

    normed_one = spread(layer_norm(residual, gains[0], gains[1]))
    self_parts, self_mixed, total = [], [], 0.0
    for weight in weight_self:
        heads = product(normed_one, weight[:, :triple]).astype(BF16)
        parts = [(heads, member * pairs, pairs) for member in range(3)]
        mixed, log_sums = attend(*parts, True)
        total = total + across(mixed, weight[:, triple:])
        self_parts.append(parts + [mixed, log_sums])
        self_mixed.append(mixed)
    total = after(total, (results["crossy"], results["feedz" + str(deep - 1)]))
    residual_one = residual + collect(total)

    normed_two = spread(layer_norm(residual_one, gains[2], gains[3]))
    cross_parts, cross_mixed, total = [], [], 0.0
    for weight in weight_cross:
        query = product(normed_two, weight[:, :cols_in]).astype(BF16)
        key_value = product(memory, weight[:, cols_in:triple]).astype(BF16)
        parts = [(query, 0, pairs), (key_value, 0, pairs), (key_value, pairs, pairs)]
        mixed, log_sums = attend(*parts, False)
        total = total + across(mixed, weight[:, triple:])
        cross_parts.append(parts + [mixed, log_sums])
        cross_mixed.append(mixed)
    weight_expand, weight_shrink = feed_second(cross_mixed[0])
    total = after(total, (up_far, back_far))
    residual_two = after(
        residual_one + collect(total), (head, weight_expand[1], weight_shrink[1])
    )

    normed_three = spread(layer_norm(residual_two, gains[4], gains[5]))
    slopes, actives, total = [], [], 0.0
    for up, back in zip(weight_expand, weight_shrink):
        active, slope = gelu_and_slope(product(normed_three, up))
        active, slope = lax.optimization_barrier((active.astype(BF16), slope))
        total = total + across(active, back)
        slopes.append(slope)
        actives.append(active)
    residual_three = residual_two + collect(total)

    final = spread(true(layer_norm(residual_three, gains[6], gains[7]).astype(BF16)))
    logits, targets, stats = [], [], []
    for half, part in enumerate(head):
        wanted = next_codes[half * books // 2 : (half + 1) * books // 2]
        values = jnp.einsum("fd,kvd->kfv", final, part, preferred_element_type=F32)
        is_target = head_ids[None, None, :] == wanted[:, :, None]
        row_max = jnp.max(values, -1)
        picked = jnp.sum(jnp.where(is_target, values, 0.0), -1)
        row_sum = jnp.sum(jnp.exp(values - row_max[..., None]), -1)
        logits.append(values)
        targets.append(is_target)
        stats.append(jnp.stack([row_max, row_sum, picked], 0))
    stats = grid.ring(jnp.concatenate(stats, 1), "c")
    top = stats[0][0]
    for stat in stats[1:]:
        top = jnp.maximum(top, stat[0])
    row_sum = sum(stat[1] * jnp.exp(stat[0] - top) for stat in stats)
    picked = sum(stat[2] for stat in stats)
    log_total = top + jnp.log(row_sum)
    loss_local = jnp.where(at_c == 0, jnp.sum((log_total - picked) * live), 0.0)
    share = live / token_count
    grad_logits = []
    for half in range(2):
        part = slice(half * books // 2, (half + 1) * books // 2)
        grad_part = jnp.exp(logits[half] - log_total[part][..., None]) - targets[half].astype(F32)
        grad_logits.append((grad_part * share[part][..., None]).astype(BF16))
    grad_logits = lax.optimization_barrier(grad_logits)
    grad_final = collect(
        sum(
            jnp.einsum("kfv,kvd->fd", values, part, preferred_element_type=F32)
            for values, part in zip(grad_logits, head)
        )
    )
    tasks, sums = {}, {}

    def add(name, axis, size, needs, value, between=0, first=0):
        tasks[name] = (axis, size, needs, between, first, lambda r: value(r).astype(BF16))

    def add_ring(name, size, needs, parts, direct=False):
        if direct:
            for step in range(1, deep):
                add(
                    name + "z" + str(step), "z" + str(step), size, needs,
                    lambda r, k=step: parts(r)[k],
                )
            return once(
                sums,
                name + "far",
                lambda r: sum(
                    (r[name + "z" + str(step)].astype(F32) for step in range(1, deep)),
                    parts(r)[0].astype(F32),
                ),
            )
        get = once(sums, name + "0", lambda r: parts(r)[deep - 1])
        for step in range(1, deep):
            add(name + "z" + str(step), "z", size, needs, get)
            needs = [name + "z" + str(step)]
            get = once(
                sums,
                name + str(step),
                lambda r, n=needs[0], k=step: r[n].astype(F32) + parts(r)[deep - 1 - k].astype(F32),
            )
        return get

    def add_rows(name, size, route, first, own, other):
        half = width // 2
        if route[0] == "y":
            add(name + "y", "y", 8 * size, [], lambda r: other, 0, first)
            whole = once(sums, name + "sum", lambda r: own + r[name + "y"].astype(F32))
            add(name + "x", "x", 4 * size, [name + "y"], lambda r: whole(r)[half:])
            quarter = once(
                sums,
                name + "part", lambda r: whole(r)[:half] + r[name + "x"].astype(F32)
            )
        else:
            far = jnp.concatenate([own[half:].astype(BF16), other[half:].astype(BF16)], 0)
            add(name + "x", "x", 8 * size, [], lambda r: far, 0, first)
            add(
                name + "y",
                "y",
                4 * size,
                [name + "x"],
                lambda r: other[:half] + r[name + "x"][half:].astype(F32),
            )
            quarter = once(
                sums,
                name + "part",
                lambda r: own[:half]
                + r[name + "x"][:half].astype(F32)
                + r[name + "y"].astype(F32),
            )
        return quarter, [name + route[1]]

    def add_rest(name, size, parts, direct=False):
        whole = once(
            sums,
            name + "whole",
            lambda r: jnp.concatenate([quarter(r) for quarter, _ in parts], 1)
            if len(parts) > 1
            else parts[0][0](r),
        )
        return add_ring(
            name,
            size,
            [need for _, needs in parts for need in needs],
            lambda r: [
                whole(r)[step * rows_in : (step + 1) * rows_in] for step in range(deep)
            ],
            direct,
        )

    def add_head(name, route, value):
        value = value.reshape(value.shape[0], 2, deep, 2, table_rows, width)
        own, far = (value[:, 0], value[:, 1]) if route == "x" else (
            value[:, :, :, 0], value[:, :, :, 1]
        )
        add(name + route, route, 16, [], lambda r: far)
        nearer = once(sums, name + "half", lambda r: own + r[name + route].astype(F32))
        depth = 1 if route == "x" else 2
        last = add_ring(
            name,
            4,
            [name + route],
            lambda r: [
                lax.index_in_dim(nearer(r), step, depth, keepdims=False) for step in range(deep)
            ],
        )
        final_axis = "y" if route == "x" else "x"
        add(name + final_axis, final_axis, 2, [name + "z" + str(deep - 1)], lambda r: last(r)[:, 1])
        return lambda r: last(r)[:, 0] + r[name + final_axis].astype(F32)

    grad_head = [
        add_head(
            "head" + str(half),
            "xy"[half],
            jnp.einsum(
                "kfv,fd->kvd",
                grad_logits[half],
                final,
                preferred_element_type=F32,
            ),
        )
        for half in range(2)
    ]

    grad, gain_final, shift_final = norm_back(
        residual_three, gains[6], gains[7], near(grad_final)
    )

    rows_grad = spread(grad)
    grad_uppers, total = [], 0.0
    for up, back, slope in zip(weight_expand, weight_shrink, slopes):
        grad_active = product(rows_grad, back)
        grad_upper = (slope * grad_active).astype(BF16)
        total = total + across(grad_upper, up)
        grad_uppers.append(grad_upper)
    grad_normed = collect(total)
    grad_expand = add_rest(
        "expand",
        2,
        [add_rows("expand", 2, "yxz", 1, *(down(normed_three, part) for part in grad_uppers))],
    )
    grads_shrink = [down(rows_grad, active) for active in actives]
    grad_shrink = add_rest("shrink", 2, [add_rows("shrink", 2, "xyz", 1, *grads_shrink)])
    change, gain_three, shift_three = norm_back(residual_two, gains[4], gains[5], grad_normed)
    grad = grad + change

    rows_grad = spread(grad)
    grads, total = [], 0.0
    for weight, parts, mixed in zip(weight_cross, cross_parts, cross_mixed):
        grad_mixed = product(rows_grad, weight[:, triple:]).astype(BF16)
        grad_q, grad_k, grad_v = attend_back(*parts, grad_mixed, False)
        total = total + across(grad_q, weight[:, :cols_in])
        grads.append(
            jnp.concatenate(
                [
                    down(normed_two, grad_q),
                    down(memory, grad_k),
                    down(memory, grad_v),
                    down(rows_grad, mixed),
                ],
                1,
            )
        )
    grad_normed = collect(total)
    cut = grads[0].shape[1] // 2
    grad_cross = add_rest(
        "cross",
        2,
        [
            add_rows("cross0", 1, "yxz", 2, grads[0][:, :cut], grads[1][:, :cut]),
            add_rows("cross1", 1, "xyz", 2, grads[0][:, cut:], grads[1][:, cut:]),
        ],
    )
    early = {1: [rows_grad]}
    change, gain_two, shift_two = norm_back(residual_one, gains[2], gains[3], grad_normed)
    grad = grad + change

    rows_grad = spread(grad)
    grads, total = [], 0.0
    for weight, parts, mixed in zip(weight_self, self_parts, self_mixed):
        grad_mixed = product(rows_grad, weight[:, triple:]).astype(BF16)
        grad_heads = jnp.concatenate(attend_back(*parts, grad_mixed, True), 1)
        early[2] = [grad_heads]
        total = total + across(grad_heads, weight[:, :triple])
        grads.append(
            jnp.concatenate([down(normed_one, grad_heads), down(rows_grad, mixed)], 1)
        )
    grad_normed = collect(total)
    change, gain_one, shift_one = norm_back(residual, gains[0], gains[1], grad_normed)
    cut = grads[0].shape[1] // 2
    grad_self = add_rest(
        "self",
        2,
        [
            add_rows("self0", 1, "yxz", 3, grads[0][:, :cut], grads[1][:, :cut]),
            add_rows("self1", 1, "xyz", 3, grads[0][:, cut:], grads[1][:, cut:]),
        ],
        True,
    )
    grad = true(grad + change)

    rows_grad = grad.astype(BF16)
    early[3] = [rows_grad]

    def add_table():
        def spread_out(rows):
            return placed(grid.ring(rows, "c"), "c").reshape(frames, width)

        own_rows = spread_out(rows_grad)
        beside = [("x", "y", codes_other, table_ids), ("y", "x", codes_beside, beside_ids)]
        halves = []
        for half, (across_axis, sum_axis, codes_far, ids) in enumerate(beside):
            name = "table" + str(half)
            part = slice(half * books // 2, (half + 1) * books // 2)
            add("rows" + str(half), across_axis, 8, [], lambda r: rows_grad, 0, 4)
            far_rows = once(
                sums, "rows" + str(half), lambda r, k=half: spread_out(r["rows" + str(k)])
            )

            def value(r, part=part, far_rows=far_rows, codes_far=codes_far, ids=ids):
                result = 0.0
                for codes, rows in ((codes_own, own_rows), (codes_far, far_rows(r))):
                    places = (codes[part][..., None] == ids).astype(BF16)
                    result = result + jnp.einsum(
                        "kfv,fd->kvd", places, rows, preferred_element_type=F32
                    )
                return result.reshape(-1, deep, 2, table_rows, width)

            value = once(sums, name + "value", value)
            add(
                name + sum_axis, sum_axis, 8, ["rows" + str(half)],
                lambda r, v=value: v(r)[:, :, 1],
            )
            both = once(
                sums,
                name + "both",
                lambda r, v=value, n=name + sum_axis: v(r)[:, :, 0] + r[n].astype(F32),
            )
            halves.append(
                add_ring(
                    name,
                    2,
                    [name + sum_axis],
                    lambda r, b=both: [b(r)[:, -step % deep] for step in range(deep)],
                    True,
                )
            )
        return halves

    grad_table = add_table()
    norm_grads = [gain_one, shift_one, gain_two, shift_two, gain_three, shift_three]
    norm_grads = jnp.stack(norm_grads + [gain_final, shift_final], 0)
    norm_grads = jnp.take(norm_grads.reshape(8, groups, -1), order_true, axis=1).reshape(8, width)
    loss_row = jnp.full((8, width), loss_local)
    norm_own = grid.total(jnp.concatenate([norm_grads, loss_row], 0), ("c",))
    tasks["normy"] = ("y", 0, [], 0, 3, lambda r: norm_own)
    tasks["normx"] = ("x", 0, ["normy"], 0, 4, lambda r: norm_own + r["normy"])
    norm_plane = once(sums, "norm", lambda r: norm_own + r["normy"] + r["normx"])
    for step in range(1, deep):
        tasks["normz" + str(step)] = ("z" + str(step), 0, ["normx"], 0, 0, norm_plane)
    ranks = ["self", "rows", "table", "cross", "expand", "shrink", "head", "norm"]
    tasks = {
        name: tasks[name]
        for rank in ranks
        for name in tasks
        if name.startswith(rank)
    }
    results = grid.rounds(tasks, BACK_BUDGET, early)
    grad_head = jnp.concatenate([part(results) for part in grad_head], 0)
    grad_table = jnp.concatenate([part(results) for part in grad_table], 0)
    grad_self, grad_cross = grad_self(results), grad_cross(results)
    grad_expand, grad_shrink = grad_expand(results), grad_shrink(results)
    summed = norm_plane(results)
    for step in range(1, deep):
        summed = summed + results["normz" + str(step)]
    grad_norm, loss_sum = summed[:8], summed[8, 0]

    def columns(array, first, count):
        return [
            array[:, (first + step) * cols_in : (first + step + 1) * cols_in]
            for step in range(count)
        ]

    stack_rows = min(128, cols_in)
    momentum_in = attend_in_momentum.transpose(1, 0, 2)

    def muon(tensor_parts, data_parts):
        tensor_factor = newton(
            grid.total(jnp.concatenate([folded_gram(part) for part in tensor_parts], 0), ("c", "y"))
        )
        blocks = [part.reshape(-1, stack_rows, cols_out) for part in data_parts]
        blocks = jnp.concatenate(blocks, 0)
        grams = grid.total(folded_gram(blocks), ("x", "z"))
        ortho = orthogonal(newton(grams), blocks)
        tensor_out, data_out, start = [], [], 0
        for part in tensor_parts:
            count = part.shape[0]
            tensor_out.append(orthogonal(tensor_factor[start : start + count], part))
            start += count
        start = 0
        for part in data_parts:
            count = part.size // (stack_rows * cols_out)
            data_out.append(ortho[start : start + count].reshape(part.shape))
            start += count
        return tensor_out, data_out

    next_cross = MOMENTUM * momentum_in[3:] + jnp.stack(columns(grad_cross, 0, 3), 0)
    next_expand = MOMENTUM * expand_momentum + grad_expand
    next_shrink = MOMENTUM * shrink_momentum + grad_shrink.T
    next_out_cross = MOMENTUM * attend_out_momentum[1] + columns(grad_cross, 3, 1)[0].T
    next_self = MOMENTUM * momentum_in[:3] + jnp.stack(columns(grad_self, 0, 3), 0)
    next_out_self = MOMENTUM * attend_out_momentum[0] + columns(grad_self, 3, 1)[0].T
    next_in = jnp.concatenate([next_self, next_cross], 0)
    next_out = jnp.stack([next_out_self, next_out_cross], 0)
    (ortho_in, ortho_expand), (ortho_out, ortho_shrink) = muon(
        [next_in, next_expand[None]], [next_out, next_shrink]
    )
    ortho_expand = ortho_expand[0]
    attend_in_new = (turned_in * (1.0 - 0.5 * DECAY) - 0.5 * ortho_in).transpose(1, 0, 2)
    attend_out_new = attend_out * (1.0 - 1.0 * DECAY) - 1.0 * ortho_out
    expand_new = expand_weights * (1.0 - 0.5 * DECAY) - 0.5 * ortho_expand
    shrink_new = shrink_weights * (1.0 - 0.5 * DECAY) - 0.5 * ortho_shrink
    embed_new, embed_first_new, embed_second_new = adam(
        embed_table, embed_first, embed_second, grad_table, 0.1, DECAY
    )
    head_new, head_first_new, head_second_new = adam(
        head_table, head_first, head_second, grad_head, 0.03, DECAY
    )
    norm_new, norm_first_new, norm_second_new = adam(
        norm_params, norm_first, norm_second, grad_norm, 0.5, 0.0
    )
    return (
        loss_sum,
        token_count,
        attend_in_new,
        attend_out_new,
        expand_new,
        shrink_new,
        next_in.transpose(1, 0, 2),
        next_out,
        next_expand,
        next_shrink,
        embed_new,
        head_new,
        norm_new,
        embed_first_new,
        embed_second_new,
        head_first_new,
        head_second_new,
        norm_first_new,
        norm_second_new,
    )


def solution(mesh):
    n_dp, n_tensor = mesh.shape["dp"], mesh.shape["tensor"]
    sizes = {"z": n_dp // 2, "x": 2, "y": 2, "c": n_tensor // 2}
    cut = Mesh(mesh.devices.reshape(tuple(sizes.values())), tuple(sizes))
    dp, tensor = ("z", "x"), ("y", "c")
    table = P(None, dp + tensor, None)
    matrices = (P(dp, None, tensor), P(None, tensor, dp), P(dp, tensor), P(tensor, dp))
    return jax.shard_map(
        lambda *args: body(Grid(sizes), *args),
        mesh=cut,
        in_specs=(P(dp, tensor, None),) * 3
        + (P(), P(dp, None))
        + matrices * 2
        + (table, table, P())
        + (table,) * 4
        + (P(), P()),
        out_specs=(P(), P())
        + matrices * 2
        + (table, table, P())
        + (table,) * 4
        + (P(), P()),
        check_vma=False,
    )
```
